32 devices in a mesh: img: 4 (over y, core), tile: 8 (over z, x).
Axes of the slice: x: 2, y: 2, z: 4, core: 2. Of those that a mesh axis runs over, the one named last changes fastest.
Arguments:
- features: bfloat16 [8, 64, 160, 256], P('img', 'tile'), may hold values from -6 to 6
- conv_weight: float32 [2560, 256], replicated, may hold values from -0.21875 to 0.21875
- conv_first: float32 [2560, 256], replicated, may hold values from -0.0029296875 to 0.0029296875
- conv_second: float32 [2560, 256], replicated, may hold values from 3.6621093e-09 to 1.4648437e-08
- head_weight: float32 [3, 1024, 85], replicated, may hold values from -0.375 to 0.375
- head_first: float32 [3, 1024, 85], replicated, may hold values from -0.0048828125 to 0.0048828125
- head_second: float32 [3, 1024, 85], replicated, may hold values from 1.0986328e-08 to 4.3945313e-08
- bias_vector: float32 [6911], replicated, may hold values from -0.3 to 0.3
- bias_first: float32 [6911], replicated, may hold values from -0.0048828125 to 0.0048828125
- bias_second: float32 [6911], replicated, may hold values from 1.0986328e-08 to 4.3945313e-08
- block_master: float32 [1280, 32, 1024], P(('img', 'tile')), may hold values from -0.109375 to 0.109375
- block_first: float32 [1280, 32, 1024], P(('img', 'tile')), may hold values from -0.0017089844 to 0.0017089844
- block_second: float32 [1280, 32, 1024], P(('img', 'tile')), may hold values from 1.2207031e-09 to 4.8828124e-09
- slot_block: int32 [1280], replicated, may hold values from -1 to 1271, as said below
- roi_image: int32 [8192], P(('img', 'tile')), may hold values from 0 to 1
- corner_index: int32 [3, 49, 8192], P(None, None, ('img', 'tile')), may hold values from 0 to 1758, as said below
- corner_frac: float32 [3, 2, 49, 8192], P(None, None, None, ('img', 'tile')), may hold values from 0 to 1
- labels: int32 [3, 8192], P(None, ('img', 'tile')), may hold values from 0 to 80
- valid: int32 [8192], P(('img', 'tile')), may hold values from 0 to 1, as said below
- box_deltas: float32 [3, 4, 8192], P(None, None, ('img', 'tile')), may hold values from -0.6 to 0.6
Outputs:
- loss: float32 [1], replicated
- conv_new: float32 [2560, 256], replicated
- conv_first_new: float32 [2560, 256], replicated
- conv_second_new: float32 [2560, 256], replicated
- head_new: float32 [3, 1024, 85], replicated
- head_first_new: float32 [3, 1024, 85], replicated
- head_second_new: float32 [3, 1024, 85], replicated
- bias_new: float32 [6911], replicated
- bias_first_new: float32 [6911], replicated
- bias_second_new: float32 [6911], replicated
- block_new: float32 [1280, 32, 1024], P(('img', 'tile'))
- block_first_new: float32 [1280, 32, 1024], P(('img', 'tile'))
- block_second_new: float32 [1280, 32, 1024], P(('img', 'tile'))
The draws below stay inside these ranges and needn't reach their ends.
Inputs may be any that keep to these rules, and one draw needn't show every extreme that they name: `slot_block`: each of the 1272 blocks is held by exactly one slot; every other slot holds -1. `corner_index`: flat index y * 160 + x into the device's 8 + 2 * 2 padded rows of the image; x <= 158 and y <= 10; no sample point reads a row outside the image. On each device the valid slots come first; a device has 256, 128 or 64 of them, and some device has 256.
All inputs are finite; a program needn't handle non-finite values.
Results may differ from the reference program's by a relative error of at most 0.011.
Values may be sent and summed in bfloat16 or wider, within the bound.
A program may use at most 832 MiB of HBM per device.

```python
import math
import jax
import jax.numpy as jnp
from jax import lax

C = 256
CIN = 256
FC = 1024
CLS = 81
POOL = 7
SECTIONS = 3
BLK = 32
HR = 2
STEP = 5
IMG_DEV = 2
H_DEV = 8
W = 160
R_DEV = 256
BINS = 49
IMAGES = 8
HEIGHT = 64
ROIS = 8192
HEADW = 85
BIASES = 6911
STACK = 13568
BLOCKS = 1272
SLOTS_ALL = 1280
N_TILE = 8


def draw_slot_block(key, part):
    order = jax.random.permutation(key, SLOTS_ALL).astype(jnp.int32)
    return jnp.where(order < BLOCKS, order, -1).astype(jnp.int32)


def section_corners(key):
    roi_pos = jnp.arange(ROIS, dtype=jnp.int32)
    tile_pos = roi_pos // R_DEV % N_TILE
    lowest = jnp.where(tile_pos == 0, HR, 0).astype(jnp.int32)
    highest = jnp.where(tile_pos == N_TILE - 1, HR + H_DEV - 2, H_DEV + 2 * HR - 2).astype(jnp.int32)
    keys = jax.random.split(key, 4)
    row_start = jax.random.randint(keys[0], (ROIS,), lowest, highest + 1)
    row_span = jax.random.randint(keys[1], (ROIS,), 0, highest - row_start + 1)
    col_start = jax.random.randint(keys[2], (ROIS,), 0, W - 1)
    col_span = jax.random.randint(keys[3], (ROIS,), 0, W - 1 - col_start)
    first_roi = roi_pos % R_DEV == 0
    row_start = jnp.where(first_roi, lowest, row_start)
    row_span = jnp.where(first_roi, highest - lowest, row_span)
    col_start = jnp.where(first_roi, 0, col_start)
    col_span = jnp.where(first_roi, W - 2, col_span)
    bin_pos = jnp.arange(BINS, dtype=jnp.int32)
    bin_row = bin_pos // POOL
    bin_col = bin_pos % POOL
    rows_at = row_start[None, :] + bin_row[:, None] * row_span[None, :] // (POOL - 1)
    cols_at = col_start[None, :] + bin_col[:, None] * col_span[None, :] // (POOL - 1)
    return (rows_at * W + cols_at).astype(jnp.int32)


def draw_corner_index(key, part):
    return jnp.stack([section_corners(jax.random.fold_in(key, 11 + section)) for section in range(SECTIONS)]).astype(jnp.int32)


def draw_valid(key, part):
    keys = jax.random.split(key, 2)
    groups = ROIS // R_DEV
    halving = jax.random.randint(keys[0], (groups,), 0, 3)
    chosen = jax.random.randint(keys[1], (), 0, groups)
    halving = jnp.where(jnp.arange(groups, dtype=jnp.int32) == chosen, 0, halving)
    kept = jnp.right_shift(jnp.full((groups,), R_DEV, jnp.int32), halving)
    roi_pos = jnp.arange(ROIS, dtype=jnp.int32)
    return (roi_pos % R_DEV < kept[roi_pos // R_DEV]).astype(jnp.int32)


def with_ends(values, rng, low, largest):
    dims = values.shape
    index_at = [jax.random.randint(jax.random.fold_in(rng, axis), (), 0, dims[axis]) for axis in range(len(dims))]
    values = values.at[tuple(index_at)].set(low)
    longest = dims.index(max(dims))
    index_at[longest] = (index_at[longest] + 1) % dims[longest]
    return values.at[tuple(index_at)].set(largest)


def level_of(key, shape, cuts, low, largest):
    loudness, own = 1.0, jax.random.fold_in(key, 6)
    for dim, parts in cuts:
        steps = jnp.exp(jax.random.uniform(jax.random.fold_in(own, dim), (parts,), jnp.float32, low / len(cuts), largest / len(cuts)))
        loudness = loudness * jnp.repeat(steps, shape[dim] // parts).reshape([-1 if axis == dim else 1 for axis in range(len(shape))])
    return loudness


def bell_draw(own_key, dims, scale, reach, cuts=(), kind=jnp.bfloat16):
    gain = level_of(own_key, dims, cuts, -0.22, 0.18) if cuts else 1.0
    drawn = jax.random.normal(own_key, dims, jnp.float32) * scale * gain
    return jnp.minimum(jnp.maximum(drawn, -reach), reach).astype(kind)


def setup_inputs(seed: int = 0) -> dict:
    arg_keys = jax.random.split(jax.random.key(seed), 21)
    return {
        "features": bell_draw(arg_keys[0], (IMAGES, HEIGHT, W, CIN), 1.0, 6.0, ((0, 4), (1, 8))),
        "conv_weight": bell_draw(arg_keys[1], (CIN + 9 * C, C), (3 * C) ** -0.5, 0.21875, (), jnp.float32),
        "conv_first": bell_draw(arg_keys[2], (CIN + 9 * C, C), (0.019 / ROIS ** 0.5), 0.0029296875, (), jnp.float32),
        "conv_second": jnp.clip(jnp.exp(jax.random.uniform(arg_keys[3], (CIN + 9 * C, C), jnp.float32, math.log(3.662109282487336e-09), math.log(1.4648437129949343e-08))), 3.662109282487336e-09, 1.4648437129949343e-08),
        "head_weight": bell_draw(arg_keys[4], (SECTIONS, FC, HEADW), (FC // 4) ** -0.5, 0.375, (), jnp.float32),
        "head_first": bell_draw(arg_keys[5], (SECTIONS, FC, HEADW), (0.033 / ROIS ** 0.5), 0.0048828125, (), jnp.float32),
        "head_second": jnp.clip(jnp.exp(jax.random.uniform(arg_keys[6], (SECTIONS, FC, HEADW), jnp.float32, math.log(1.0986328291551217e-08), math.log(4.394531316620487e-08))), 1.0986328291551217e-08, 4.394531316620487e-08),
        "bias_vector": bell_draw(arg_keys[7], (BIASES,), 0.05, 0.3, (), jnp.float32),
        "bias_first": bell_draw(arg_keys[8], (BIASES,), (0.033 / ROIS ** 0.5), 0.0048828125, (), jnp.float32),
        "bias_second": jnp.clip(jnp.exp(jax.random.uniform(arg_keys[9], (BIASES,), jnp.float32, math.log(1.0986328291551217e-08), math.log(4.394531316620487e-08))), 1.0986328291551217e-08, 4.394531316620487e-08),
        "block_master": bell_draw(arg_keys[10], (SLOTS_ALL, BLK, FC), (STACK // 4) ** -0.5, 0.109375, ((0, 32),), jnp.float32),
        "block_first": bell_draw(arg_keys[11], (SLOTS_ALL, BLK, FC), (0.011 / ROIS ** 0.5), 0.0017089844, ((0, 32),), jnp.float32),
        "block_second": jnp.clip(jnp.exp(math.log(4.882812376649781e-09) - 1.3862944 * jax.random.uniform(arg_keys[12], (SLOTS_ALL, BLK, FC), jnp.float32) ** level_of(arg_keys[12], (SLOTS_ALL, BLK, FC), ((0, 32),), -0.2, 0.2)), 1.2207030941624453e-09, 4.882812376649781e-09),
        "slot_block": draw_slot_block(jax.random.fold_in(arg_keys[20], 71), 0),
        "roi_image": with_ends(jax.random.randint(arg_keys[14], (ROIS,), 0, IMG_DEV), jax.random.fold_in(arg_keys[14], 1), 0, IMG_DEV - 1).astype(jnp.int32),
        "corner_index": draw_corner_index(jax.random.fold_in(arg_keys[20], 71), 0),
        "corner_frac": jnp.clip(1.0 * jax.random.uniform(arg_keys[16], (SECTIONS, 2, BINS, ROIS), jnp.float32) ** level_of(arg_keys[16], (SECTIONS, 2, BINS, ROIS), ((3, 32),), -0.2, 0.2), 0.0, 1.0),
        "labels": with_ends(jax.random.randint(arg_keys[17], (SECTIONS, ROIS), 0, CLS), jax.random.fold_in(arg_keys[17], 1), 0, CLS - 1).astype(jnp.int32),
        "valid": draw_valid(jax.random.fold_in(arg_keys[20], 71), 0),
        "box_deltas": bell_draw(arg_keys[19], (SECTIONS, 4, ROIS), 0.1, 0.6, ((2, 32),), jnp.float32),
    }


HIGHEST = lax.Precision.HIGHEST
BETA_ONE = 0.9
BETA_TWO = 0.999
RATE = 0.025
DECAY = 0.01
EPSILON = 1e-08

@jax.custom_vjp
def low(v):
    return lax.optimization_barrier(v.astype(jnp.bfloat16)).astype(jnp.float32)

@jax.custom_vjp
def low_back(v):
    return v

def low_keep(v):
    return (low(v), None)

def low_pass(kept, grad):
    return (grad,)

def back_keep(v):
    return (v, None)

def back_low(kept, grad):
    return (low(grad),)
low.defvjp(low_keep, low_pass)
low_back.defvjp(back_keep, back_low)

def adamw(master, first, second, grad, step):
    first_new = BETA_ONE * first + (1.0 - BETA_ONE) * grad
    second_new = BETA_TWO * second + (1.0 - BETA_TWO) * grad * grad
    first_hat = first_new / (1.0 - BETA_ONE ** step)
    second_hat = second_new / (1.0 - BETA_TWO ** step)
    master_new = master - RATE * (first_hat / (jnp.sqrt(second_hat) + EPSILON) + DECAY * master)
    return (master_new, first_new, second_new)

def convolve(padded, kernel_taps, height, breadth):
    summed = None
    for kernel_pos in range(9):
        row_shift = kernel_pos // 3
        col_shift = kernel_pos % 3
        window = padded[:, row_shift:row_shift + height, col_shift:col_shift + breadth]
        contrib = jnp.einsum('ihwc,cd->ihwd', window, kernel_taps[kernel_pos], precision=HIGHEST)
        summed = contrib if summed is None else summed + contrib
    return summed

def reference(features, conv_weight, conv_first, conv_second, head_weight, head_first, head_second, bias_vector, bias_first, bias_second, block_master, block_first, block_second, slot_block, roi_image, corner_index, corner_frac, labels, valid, box_deltas):
    position = jnp.arange(SLOTS_ALL, dtype=jnp.int32)
    owner_slot = jnp.zeros((BLOCKS,), jnp.int32).at[jnp.where(slot_block >= 0, slot_block, BLOCKS)].set(position, mode='drop')
    roi_pos = jnp.arange(ROIS, dtype=jnp.int32)
    device = roi_pos // R_DEV
    group_pos = device // N_TILE
    tile_pos = device % N_TILE
    padded_height = HEIGHT + 2 * HR
    image_id = group_pos * IMG_DEV + roi_image
    valid_float = valid.astype(jnp.float32)
    count = jnp.sum(valid_float)
    block = math.gcd(ROIS, 2048)
    turns = ROIS // block
    section_pieces = []
    for section in range(SECTIONS):
        corner_turn = corner_index[section].T
        corner_base = ((image_id * padded_height + tile_pos * H_DEV)[:, None] + corner_turn // W) * W + corner_turn % W
        one_hot = (labels[section][:, None] == jnp.arange(CLS, dtype=jnp.int32)[None, :]).astype(jnp.float32)
        foreground = (labels[section] > 0).astype(jnp.float32)
        box_scale = jnp.array([10.0, 10.0, 5.0, 5.0], jnp.float32) * (section + 1)
        target = box_deltas[section].T * box_scale
        section_pieces.append((corner_base.reshape(turns, block, BINS), corner_frac[section, 0].T.reshape(turns, block, BINS), corner_frac[section, 1].T.reshape(turns, block, BINS), one_hot.reshape(turns, block, CLS), foreground.reshape(turns, block), target.reshape(turns, block, 4), valid_float.reshape(turns, block)))
    image = features.astype(jnp.float32)

    def forward(conv_weight, head_weight, bias_vector, block_master):
        conv_low = low(conv_weight)
        lateral_w = conv_low[:CIN]
        kernel_taps = conv_low[CIN:].reshape(9, C, C)
        lateral_bias = bias_vector[:C]
        conv_bias = bias_vector[C:2 * C]
        lateral = low(low_back(jnp.einsum('ihwc,cd->ihwd', image, lateral_w, precision=HIGHEST) + lateral_bias))
        lateral_padded = jnp.pad(lateral, ((0, 0), (1, 1), (1, 1), (0, 0)))
        feature_map = low(low_back(convolve(lateral_padded, kernel_taps, HEIGHT, W) + conv_bias))
        flat_map = jnp.pad(feature_map, ((0, 0), (HR, HR), (0, 0), (0, 0))).reshape(-1, C)
        stacked = low(block_master)[owner_slot].reshape(SECTIONS, STACK, FC)
        head_all = low(head_weight)
        total = jnp.zeros((), jnp.float32)
        for section in range(SECTIONS):
            first_matrix = stacked[section, :BINS * C]
            second_matrix = stacked[section, BINS * C:]
            head_low = head_all[section]
            offset = 2 * C + section * (2 * FC + HEADW)
            first_bias = bias_vector[offset:offset + FC]
            second_bias = bias_vector[offset + FC:offset + 2 * FC]
            head_bias = bias_vector[offset + 2 * FC:offset + 2 * FC + HEADW]

            def block_loss(piece):
                base, frow, fcol, hot, fore, goal, live = piece
                pooled = ((1.0 - frow) * (1.0 - fcol))[:, :, None] * flat_map[base]
                pooled = pooled + ((1.0 - frow) * fcol)[:, :, None] * flat_map[base + 1]
                pooled = pooled + (frow * (1.0 - fcol))[:, :, None] * flat_map[base + W]
                pooled = pooled + (frow * fcol)[:, :, None] * flat_map[base + W + 1]
                roi_feats = low(pooled.reshape(block, BINS * C))
                first_pre = low_back(jnp.dot(roi_feats, first_matrix, precision=HIGHEST) + first_bias)
                first_act = low(jax.nn.silu(first_pre))
                second_pre = low_back(jnp.dot(first_act, second_matrix, precision=HIGHEST) + second_bias)
                second_act = low(jax.nn.silu(second_pre))
                outputs = low_back(jnp.dot(second_act, head_low, precision=HIGHEST) + head_bias)
                cross = -lax.optimization_barrier(jnp.sum(jax.nn.log_softmax(outputs[:, :CLS], axis=1) * hot, axis=1))
                differ = outputs[:, CLS:] - goal
                magnitude = jnp.abs(differ)
                smooth = jnp.where(magnitude < 1.0, 0.5 * differ * differ, magnitude - 0.5)
                return jnp.sum(live * (cross + fore * lax.optimization_barrier(jnp.sum(smooth, axis=1))))
            checked = jax.checkpoint(block_loss)

            def scan_step(carry, piece):
                return (carry + checked(piece), None)
            summed, _ = lax.scan(scan_step, jnp.zeros((), jnp.float32), section_pieces[section])
            total = total + summed
        return total / count
    loss, pull = jax.vjp(forward, conv_weight, head_weight, bias_vector, block_master)
    grad_conv, grad_head, grad_bias, grad_block = pull(jnp.ones((), jnp.float32))
    step = float(STEP)
    conv_new, conv_first_new, conv_second_new = adamw(conv_weight, conv_first, conv_second, grad_conv, step)
    head_new, head_first_new, head_second_new = adamw(head_weight, head_first, head_second, grad_head, step)
    bias_new, bias_first_new, bias_second_new = adamw(bias_vector, bias_first, bias_second, grad_bias, step)
    block_new, block_first_new, block_second_new = adamw(block_master, block_first, block_second, grad_block, step)
    return (loss.reshape(1), conv_new, conv_first_new, conv_second_new, head_new, head_first_new, head_second_new, bias_new, bias_first_new, bias_second_new, block_new, block_first_new, block_second_new)
```

```python
import jax
import jax.numpy as jnp
from jax import lax
from jax.experimental import pallas as pl
from jax.experimental.pallas import tpu as pltpu
from jax.sharding import PartitionSpec as P

HR = 2
STEP = 5
BINS = 49
POOL = 7

BETA_ONE = 0.9
BETA_TWO = 0.999
RATE = 0.025
DECAY = 0.01
EPSILON = 1e-08

VMEM_LIMIT = 56 * 1024 * 1024
AXES = ("img", "tile")


def padded_2(cells, sides, width):
    for axis, dim in sides:
        count = lax.axis_size(axis)
        ends = count - 1
        head = lax.slice_in_dim(cells, 0, width, axis=dim)
        tail = lax.slice_in_dim(cells, cells.shape[dim] - width, cells.shape[dim], axis=dim)
        cells = jnp.concatenate(
            [
                lax.ppermute(tail, axis, [(i, (i + 1) % count) for i in range(ends)]),
                cells,
                lax.ppermute(head, axis, [((i + 1) % count, i) for i in range(ends)]),
            ],
            axis=dim,
        )
    return cells


def adamw(master, first, second, grad, step):
    first_new = BETA_ONE * first + (1.0 - BETA_ONE) * grad
    second_new = BETA_TWO * second + (1.0 - BETA_TWO) * grad * grad
    first_hat = first_new / (1.0 - BETA_ONE**step)
    second_hat = second_new / (1.0 - BETA_TWO**step)
    master_new = master - RATE * (first_hat / (jnp.sqrt(second_hat) + EPSILON) + DECAY * master)
    return (master_new, first_new, second_new)


def silu_slope(value):
    sigmoid = jax.nn.sigmoid(value)
    return sigmoid * (1.0 + value * (1.0 - sigmoid))


def convolve(padded, kernel_taps, height, breadth):
    summed = None
    for kernel_pos in range(9):
        row_shift = kernel_pos // 3
        col_shift = kernel_pos % 3
        window = padded[:, row_shift : row_shift + height, col_shift : col_shift + breadth]
        contrib = jnp.einsum(
            "ihwc,cd->ihwd", window, kernel_taps[kernel_pos], preferred_element_type=jnp.float32
        )
        summed = contrib if summed is None else summed + contrib
    return summed


def convolve_back(grad_padded, lateral_padded, grad_low, kernel_taps, height, breadth):
    grad_input = None
    tap_grads = []
    for kernel_pos in range(9):
        row_shift = kernel_pos // 3
        col_shift = kernel_pos % 3
        window = lateral_padded[:, row_shift : row_shift + height, col_shift : col_shift + breadth]
        tap_grads.append(
            jnp.einsum("ihwc,ihwd->cd", window, grad_low, preferred_element_type=jnp.float32)
        )
        source = grad_padded[
            :, 2 - row_shift : 2 - row_shift + height, 2 - col_shift : 2 - col_shift + breadth
        ]
        contrib = jnp.einsum(
            "ihwd,cd->ihwc", source, kernel_taps[kernel_pos], preferred_element_type=jnp.float32
        )
        grad_input = contrib if grad_input is None else grad_input + contrib
    return (jnp.concatenate(tap_grads, axis=0), grad_input)


def column_weights(column, frac, breadth):
    regions = column.shape[1]
    away = lax.broadcasted_iota(jnp.int32, (breadth, regions), 0) - column
    return jnp.where(away == 0, 1.0 - frac, jnp.where(away == 1, frac, 0.0))


def row_weight(row, frac, at):
    away = at - row
    return jnp.where(away == 0, 1.0 - frac, jnp.where(away == 1, frac, 0.0))


def pool_regions(map_t, rows, cols, fracs_row, fracs_col, breadth):
    section_count, bins, regions = rows.shape
    channels, cells = map_t.shape
    lines = cells // breadth
    group = POOL
    chunk = 8

    def body(map_ref, row_ref, col_ref, fr_ref, fc_ref, out_ref):
        turn = pl.program_id(1)

        def one_bin(b, carry):
            p = turn * group + b
            row = row_ref[0, pl.ds(p, 1), :]
            col = col_ref[0, pl.ds(p, 1), :]
            frow = fr_ref[0, pl.ds(p, 1), :]
            fcol = fc_ref[0, pl.ds(p, 1), :]
            across = column_weights(col, fcol, breadth)
            total = None
            for first in range(0, lines, chunk):
                weights = jnp.concatenate(
                    [
                        (across * row_weight(row, frow, line)).astype(jnp.bfloat16)
                        for line in range(first, first + chunk)
                    ],
                    axis=0,
                )
                part = jnp.dot(
                    map_ref[:, first * breadth : (first + chunk) * breadth],
                    weights,
                    preferred_element_type=jnp.float32,
                )
                total = part if total is None else total + part
            out_ref[0, b] = total.astype(jnp.bfloat16)
            return carry

        lax.fori_loop(0, group, one_bin, 0)

    samples = pl.BlockSpec((1, bins, regions), lambda u, t: (u, 0, 0))
    return pl.pallas_call(
        body,
        grid=(section_count, bins // group),
        in_specs=[pl.BlockSpec((channels, cells), lambda u, t: (0, 0))] + [samples] * 4,
        out_specs=pl.BlockSpec((1, group, channels, regions), lambda u, t: (u, t, 0, 0)),
        out_shape=jax.ShapeDtypeStruct((section_count, bins, channels, regions), jnp.bfloat16),
        compiler_params=pltpu.CompilerParams(vmem_limit_bytes=VMEM_LIMIT),
        cost_estimate=pl.CostEstimate(
            flops=2 * section_count * bins * regions * cells * channels,
            bytes_accessed=section_count * bins * regions * channels * 2,
            transcendentals=0,
        ),
        name="pool_regions",
    )(map_t, rows, cols, fracs_row, fracs_col)


def fetch_blocks(table, blocks_ref, buffer, sem, base, slot, count, block_rows):
    def one(b, carry):
        pltpu.make_async_copy(
            blocks_ref.at[table[base + b]],
            buffer.at[slot, pl.ds(pl.multiple_of(b * block_rows, block_rows), block_rows)],
            sem.at[slot],
        ).start()
        return carry

    lax.fori_loop(0, count, one, 0, unroll=8)


def first_layer(table, blocks, feats_t, section_blocks):
    section_count, bins, channels, regions = feats_t.shape
    _, block_rows, hidden = blocks.shape
    group = POOL
    turns = bins // group
    per_bin = channels // block_rows
    count = group * per_bin

    def body(table_ref, blocks_ref, x_ref, out_ref, buffer, sem):
        u, t = pl.program_id(0), pl.program_id(1)
        step = u * turns + t
        slot = lax.rem(step, 2)

        def fetch(at, into):
            base = (at // turns) * section_blocks + lax.rem(at, turns) * count
            fetch_blocks(table_ref, blocks_ref, buffer, sem, base, into, count, block_rows)

        @pl.when(step == 0)
        def _():
            fetch(step, slot)

        @pl.when(step + 1 < section_count * turns)
        def _():
            fetch(step + 1, 1 - slot)

        pltpu.make_async_copy(buffer.at[slot], buffer.at[slot], sem.at[slot]).wait()

        @pl.when(t == 0)
        def _():
            out_ref[...] = jnp.zeros_like(out_ref)

        def one_bin(b, carry):
            at = pl.ds(pl.multiple_of(b * channels, channels), channels)
            out_ref[0] += lax.dot_general(
                x_ref[0, b],
                buffer[slot, at],
                (((0,), (0,)), ((), ())),
                preferred_element_type=jnp.float32,
            )
            return carry

        lax.fori_loop(0, group, one_bin, 0)

    return pl.pallas_call(
        body,
        grid_spec=pltpu.PrefetchScalarGridSpec(
            num_scalar_prefetch=1,
            grid=(section_count, turns),
            in_specs=[
                pl.BlockSpec(memory_space=pl.ANY),
                pl.BlockSpec((1, group, channels, regions), lambda u, t, _: (u, t, 0, 0)),
            ],
            out_specs=pl.BlockSpec((1, regions, hidden), lambda u, t, _: (u, 0, 0)),
            scratch_shapes=[
                pltpu.VMEM((2, count * block_rows, hidden), jnp.bfloat16),
                pltpu.SemaphoreType.DMA((2,)),
            ],
        ),
        out_shape=jax.ShapeDtypeStruct((section_count, regions, hidden), jnp.float32),
        compiler_params=pltpu.CompilerParams(vmem_limit_bytes=VMEM_LIMIT),
        cost_estimate=pl.CostEstimate(
            flops=2 * section_count * bins * regions * channels * hidden,
            bytes_accessed=section_count * bins * channels * (regions + hidden) * 2,
            transcendentals=0,
        ),
        name="first_layer",
    )(table, blocks, feats_t)


def weight_grads(order, place, offsets, feats_t, acts_t, grads_first, grads_second, sizes):
    section_count, bins, channels, regions = feats_t.shape
    hidden = grads_first.shape[2]
    block_rows = sizes[0][1]
    group = POOL
    turns = bins // group + 1
    rows = group * channels
    wide = acts_t.shape[1]
    steps = section_count * turns
    kinds = len(sizes)

    def body(order_ref, place_ref, offset_ref, x_ref, a_ref, gf_ref, gs_ref, *rest):
        outs, (buffer, sem) = rest[:kinds], rest[kinds:]
        u, t = pl.program_id(0), pl.program_id(1)
        step = u * turns + t
        slot = lax.rem(step, 2)

        def drain(at, into):
            last = lax.rem(at, turns) == turns - 1

            @pl.when(last)
            def _():
                half = buffer.at[into, pl.ds(0, wide)]
                pltpu.make_async_copy(half, half, sem.at[into]).wait()

            @pl.when(jnp.logical_not(last))
            def _():
                pltpu.make_async_copy(buffer.at[into], buffer.at[into], sem.at[into]).wait()

        @pl.when(step >= 2)
        def _():
            drain(step - 2, slot)

        @pl.when(t < turns - 1)
        def _():
            def one_bin(b, carry):
                at = pl.ds(pl.multiple_of(b * channels, channels), channels)
                buffer[slot, at] = jnp.dot(
                    x_ref[0, b], gf_ref[0], preferred_element_type=jnp.float32
                ).astype(jnp.bfloat16)
                return carry

            lax.fori_loop(0, group, one_bin, 0)

        @pl.when(t == turns - 1)
        def _():
            def one_part(b, carry):
                at = pl.ds(pl.multiple_of(b * channels, channels), channels)
                buffer[slot, at] = jnp.dot(
                    a_ref[0, at], gs_ref[0], preferred_element_type=jnp.float32
                ).astype(jnp.bfloat16)
                return carry

            lax.fori_loop(0, wide // channels, one_part, 0)

        for kind in range(kinds):

            def one(i, carry, kind=kind):
                at = pl.ds(pl.multiple_of(order_ref[i] * block_rows, block_rows), block_rows)
                pltpu.make_async_copy(
                    buffer.at[slot, at], outs[kind].at[place_ref[i]], sem.at[slot]
                ).start()
                return carry

            lax.fori_loop(
                offset_ref[step * kinds + kind], offset_ref[step * kinds + kind + 1], one, 0
            )

        @pl.when(step == steps - 1)
        def _():
            drain(step - 1, 1 - slot)
            drain(step, slot)

    return pl.pallas_call(
        body,
        grid_spec=pltpu.PrefetchScalarGridSpec(
            num_scalar_prefetch=3,
            grid=(section_count, turns),
            in_specs=[
                pl.BlockSpec(
                    (1, group, channels, regions),
                    lambda u, t, *_: (u, jnp.minimum(t, turns - 2), 0, 0),
                ),
                pl.BlockSpec((1, wide, regions), lambda u, t, *_: (u, 0, 0)),
                pl.BlockSpec((1, regions, hidden), lambda u, t, *_: (u, 0, 0)),
                pl.BlockSpec((1, regions, hidden), lambda u, t, *_: (u, 0, 0)),
            ],
            out_specs=[pl.BlockSpec(memory_space=pl.ANY)] * kinds,
            scratch_shapes=[
                pltpu.VMEM((2, rows, hidden), jnp.bfloat16),
                pltpu.SemaphoreType.DMA((2,)),
            ],
        ),
        out_shape=[jax.ShapeDtypeStruct(size, jnp.bfloat16) for size in sizes],
        compiler_params=pltpu.CompilerParams(vmem_limit_bytes=VMEM_LIMIT),
        cost_estimate=pl.CostEstimate(
            flops=2 * section_count * regions * (bins * channels + wide) * hidden,
            bytes_accessed=section_count * (bins * channels + wide) * (regions + hidden) * 2,
            transcendentals=0,
        ),
        name="weight_grads",
    )(order, place, offsets, feats_t, acts_t, grads_first, grads_second)


def map_grads(table, blocks, grads_first, rows, cols, fracs_row, fracs_col, section_blocks, lines, breadth, channels):
    section_count, bins, regions = rows.shape
    _, block_rows, hidden = blocks.shape
    group = POOL
    turns = bins // group
    count = group * channels // block_rows
    cells = lines * breadth

    def body(table_ref, blocks_ref, g_ref, row_ref, col_ref, fr_ref, fc_ref, out_ref, buffer, sem):
        u, t = pl.program_id(0), pl.program_id(1)
        step = u * turns + t
        slot = lax.rem(step, 2)

        def fetch(at, into):
            base = (at // turns) * section_blocks + lax.rem(at, turns) * count
            fetch_blocks(table_ref, blocks_ref, buffer, sem, base, into, count, block_rows)

        @pl.when(step == 0)
        def _():
            out_ref[...] = jnp.zeros_like(out_ref)
            fetch(step, slot)

        @pl.when(step + 1 < section_count * turns)
        def _():
            fetch(step + 1, 1 - slot)

        pltpu.make_async_copy(buffer.at[slot], buffer.at[slot], sem.at[slot]).wait()

        def one_bin(b, carry):
            p = t * group + b
            at = pl.ds(pl.multiple_of(b * channels, channels), channels)
            pooled = lax.dot_general(
                g_ref[0],
                buffer[slot, at],
                (((1,), (1,)), ((), ())),
                preferred_element_type=jnp.float32,
            ).astype(jnp.bfloat16)
            row = row_ref[0, pl.ds(p, 1), :]
            frow = fr_ref[0, pl.ds(p, 1), :]
            across = column_weights(
                col_ref[0, pl.ds(p, 1), :], fc_ref[0, pl.ds(p, 1), :], breadth
            )
            for line in range(lines):
                weights = (across * row_weight(row, frow, line)).astype(jnp.bfloat16)
                out_ref[line * breadth : (line + 1) * breadth] += jnp.dot(
                    weights, pooled, preferred_element_type=jnp.float32
                )
            return carry

        lax.fori_loop(0, group, one_bin, 0)

    samples = pl.BlockSpec((1, bins, regions), lambda u, t, _: (u, 0, 0))
    return pl.pallas_call(
        body,
        grid_spec=pltpu.PrefetchScalarGridSpec(
            num_scalar_prefetch=1,
            grid=(section_count, turns),
            in_specs=[
                pl.BlockSpec(memory_space=pl.ANY),
                pl.BlockSpec((1, regions, hidden), lambda u, t, _: (u, 0, 0)),
            ]
            + [samples] * 4,
            out_specs=pl.BlockSpec((cells, channels), lambda u, t, _: (0, 0)),
            scratch_shapes=[
                pltpu.VMEM((2, count * block_rows, hidden), jnp.bfloat16),
                pltpu.SemaphoreType.DMA((2,)),
            ],
        ),
        out_shape=jax.ShapeDtypeStruct((cells, channels), jnp.float32),
        compiler_params=pltpu.CompilerParams(vmem_limit_bytes=VMEM_LIMIT),
        cost_estimate=pl.CostEstimate(
            flops=2 * section_count * bins * regions * channels * (hidden + cells),
            bytes_accessed=section_count * bins * channels * hidden * 2,
            transcendentals=0,
        ),
        name="map_grads",
    )(table, blocks, grads_first, rows, cols, fracs_row, fracs_col)


def bits_of(count):
    return list(range(count.bit_length() - 1))


def part_orders(n_img, n_tile):
    low = [("tile", b) for b in bits_of(n_tile)[:1]]
    high = [("tile", b) for b in bits_of(n_tile)[1:]]
    side = [("img", b) for b in bits_of(n_img)[1:]]
    return [low + side + high, side + high + low, high + low + side]


def part_sizes(slots):
    first = (3 * slots + 7) // 8
    second = (slots - first + 1) * 5 // 9
    return [first, second, slots - first - second]


def swap(values, axis, bit):
    count = lax.axis_size(axis)
    return lax.ppermute(values, axis, [(i, i ^ (1 << bit)) for i in range(count)])


def add_low(a, b):
    return (a.astype(jnp.float32) + b.astype(jnp.float32)).astype(jnp.bfloat16)


def sum_parts(kept, sent, orders):
    received = [swap(s, "img", 0) for s in sent]
    results = [None] * len(kept)
    pairs = [(k, r) for k, r in zip(kept, received)]
    for stage in range(len(orders[0])):
        for i, order in enumerate(orders):
            mine, theirs = pairs[i]
            half = mine.shape[0] // 2
            away = add_low(mine[half:], theirs[half:])
            stay = add_low(mine[:half], theirs[:half])
            pairs[i] = (stay, swap(away, *order[stage]))
    for i, (mine, theirs) in enumerate(pairs):
        results[i] = mine.astype(jnp.float32) + theirs.astype(jnp.float32)
    return results


def on_device(
    features,
    conv_weight,
    conv_first,
    conv_second,
    head_weight,
    head_first,
    head_second,
    bias_vector,
    bias_first,
    bias_second,
    block_master,
    block_first,
    block_second,
    slot_block,
    roi_image,
    corner_index,
    corner_frac,
    labels,
    valid,
    box_deltas,
):
    images, height, breadth, in_channels = features.shape
    channels = conv_weight.shape[1]
    section_count, hidden, out_width = head_weight.shape
    classes = out_width - 4
    slots, block_rows, _ = block_master.shape
    all_slots = slot_block.shape[0]
    rim = HR
    first_rows = BINS * channels
    section_rows = first_rows + hidden
    section_blocks = section_rows // block_rows
    first_blocks = first_rows // block_rows
    block_total = section_count * section_blocks
    n_img, n_tile = lax.axis_size("img"), lax.axis_size("tile")
    at_img, at_tile = lax.axis_index("img"), lax.axis_index("tile")

    gathered = lax.all_gather(block_master.astype(jnp.bfloat16), AXES, axis=0, tiled=True)
    position = jnp.arange(all_slots, dtype=jnp.int32)
    owner_slot = (
        jnp.zeros((block_total,), jnp.int32)
        .at[jnp.where(slot_block >= 0, slot_block, block_total)]
        .set(position, mode="drop")
    )

    orders = part_orders(n_img, n_tile)
    shares = part_sizes(slots)
    groups = n_img * n_tile // 2
    owner = owner_slot // slots
    within = owner_slot % slots
    relative = {"img": (owner // n_tile) ^ at_img, "tile": (owner % n_tile) ^ at_tile}
    kind = jnp.zeros((block_total,), jnp.int32)
    place = jnp.zeros((block_total,), jnp.int32)
    start = 0
    for i, (order, share) in enumerate(zip(orders, shares)):
        rank = jnp.zeros((block_total,), jnp.int32)
        for axis, bit in order:
            rank = rank * 2 + ((relative[axis] >> bit) & 1)
        inside = (within >= start) & (within < start + share)
        kind = jnp.where(inside, 2 * i + (relative["img"] & 1), kind)
        place = jnp.where(inside, rank * share + within - start, place)
        start += share
    kinds = 2 * len(orders)
    block_id = jnp.arange(block_total, dtype=jnp.int32)
    per_turn = POOL * channels // block_rows
    turn = (block_id // section_blocks) * (POOL + 1) + (block_id % section_blocks) // per_turn
    bucket = turn * kinds + kind
    buckets = section_count * (POOL + 1) * kinds
    within_turn = (block_id % section_blocks) % per_turn
    _, order_list, place_list = lax.sort((bucket, within_turn, place), num_keys=1)
    offsets = jnp.sum(
        (bucket[None, :] < jnp.arange(buckets + 1, dtype=jnp.int32)[:, None]).astype(jnp.int32), axis=1
    )

    valid_float = valid.astype(jnp.float32)
    conv_low = conv_weight.astype(jnp.bfloat16)
    lateral_w = conv_low[:in_channels]
    kernel_taps = conv_low[in_channels:].reshape(9, channels, channels)
    head_all = head_weight.astype(jnp.bfloat16)
    lateral_bias = bias_vector[:channels]
    conv_bias = bias_vector[channels : 2 * channels]
    lateral = (
        jnp.einsum("ihwc,cd->ihwd", features, lateral_w, preferred_element_type=jnp.float32)
        + lateral_bias
    ).astype(jnp.bfloat16)
    column_pad = ((0, 0), (0, 0), (1, 1), (0, 0))
    lateral_padded = jnp.pad(padded_2(lateral, (("tile", 1),), 1), column_pad)
    feature_map = (convolve(lateral_padded, kernel_taps, height, breadth) + conv_bias).astype(
        jnp.bfloat16
    )
    map_padded = padded_2(feature_map, (("tile", 1),), rim)
    padded_rows = height + 2 * rim
    lines = images * padded_rows
    map_t = map_padded.reshape(lines * breadth, channels).T
    sample_rows = roi_image * padded_rows + corner_index // breadth
    sample_cols = corner_index % breadth
    fracs_row = corner_frac[:, 0]
    fracs_col = corner_frac[:, 1]
    feats_t = pool_regions(map_t, sample_rows, sample_cols, fracs_row, fracs_col, breadth)
    first_pres = first_layer(owner_slot, gathered, feats_t, section_blocks)

    loss_part = jnp.zeros((), jnp.float32)
    head_grads = []
    section_bias_grads = []
    acts_t, grads_first, grads_second = [], [], []
    for section in range(section_count):
        second_slots = lax.slice_in_dim(
            owner_slot, section * section_blocks + first_blocks, (section + 1) * section_blocks
        )
        second_matrix = gathered[second_slots].reshape(hidden, hidden)
        head_low = head_all[section]
        offset = 2 * channels + section * (2 * hidden + out_width)
        first_bias = bias_vector[offset : offset + hidden]
        second_bias = bias_vector[offset + hidden : offset + 2 * hidden]
        head_bias = bias_vector[offset + 2 * hidden : offset + 2 * hidden + out_width]
        first_pre = first_pres[section] + first_bias
        first_act = jax.nn.silu(first_pre).astype(jnp.bfloat16)
        acts_t.append(first_act.T)
        second_pre = (
            jnp.dot(first_act, second_matrix, preferred_element_type=jnp.float32) + second_bias
        )
        second_act = jax.nn.silu(second_pre).astype(jnp.bfloat16)
        outputs = jnp.dot(second_act, head_low, preferred_element_type=jnp.float32) + head_bias
        logits = outputs[:, :classes]
        shifted = logits - jnp.max(logits, axis=1, keepdims=True)
        log_total = jnp.log(jnp.sum(jnp.exp(shifted), axis=1, keepdims=True))
        one_hot = (
            labels[section][:, None] == jnp.arange(classes, dtype=jnp.int32)[None, :]
        ).astype(jnp.float32)
        cross = log_total[:, 0] - jnp.sum(shifted * one_hot, axis=1)
        foreground = (labels[section] > 0).astype(jnp.float32)
        target = box_deltas[section].T * (
            jnp.array([10.0, 10.0, 5.0, 5.0], jnp.float32) * (section + 1)
        )
        differ = outputs[:, classes:] - target
        magnitude = jnp.abs(differ)
        smooth = jnp.where(magnitude < 1.0, 0.5 * differ * differ, magnitude - 0.5)
        loss_part = loss_part + jnp.sum(
            valid_float * (cross + foreground * jnp.sum(smooth, axis=1))
        )
        probs = jnp.exp(shifted - log_total)
        grad_logits = valid_float[:, None] * (probs - one_hot)
        grad_box = (valid_float * foreground)[:, None] * jnp.clip(differ, -1.0, 1.0)
        grad_out = jnp.concatenate([grad_logits, grad_box], axis=1).astype(jnp.bfloat16)
        head_grads.append(
            jnp.einsum("rk,rf->kf", second_act, grad_out, preferred_element_type=jnp.float32)
        )
        grad_head_bias = jnp.sum(grad_out.astype(jnp.float32), axis=0)
        grad_second = (
            jnp.einsum("rf,kf->rk", grad_out, head_low, preferred_element_type=jnp.float32)
            * silu_slope(second_pre)
        ).astype(jnp.bfloat16)
        grad_second_bias = jnp.sum(grad_second.astype(jnp.float32), axis=0)
        grad_first = (
            jnp.einsum("rf,kf->rk", grad_second, second_matrix, preferred_element_type=jnp.float32)
            * silu_slope(first_pre)
        ).astype(jnp.bfloat16)
        grad_first_bias = jnp.sum(grad_first.astype(jnp.float32), axis=0)
        section_bias_grads.extend([grad_first_bias, grad_second_bias, grad_head_bias])
        grads_first.append(grad_first)
        grads_second.append(grad_second)
    acts_t = jnp.stack(acts_t)
    grads_first = jnp.stack(grads_first)
    grads_second = jnp.stack(grads_second)

    sizes = []
    for share in shares:
        sizes += [(groups * share, block_rows, hidden)] * 2
    parts = weight_grads(
        order_list, place_list, offsets, feats_t, acts_t, grads_first, grads_second, sizes
    )
    block_parts = sum_parts(parts[0::2], parts[1::2], orders)

    grad_flat = map_grads(
        owner_slot, gathered, grads_first, sample_rows, sample_cols, fracs_row, fracs_col,
        section_blocks, lines, breadth, channels,
    )
    grad_padded_map = grad_flat.reshape(images, padded_rows, breadth, channels)
    outer_rims = jnp.concatenate(
        [grad_padded_map[:, :rim], grad_padded_map[:, rim + height :]], axis=1
    )
    returned = padded_2(outer_rims, (("tile", 1),), rim)
    grad_own = grad_padded_map[:, rim : rim + height]
    grad_own = (
        grad_own.at[:, :rim]
        .add(returned[:, :rim])
        .at[:, height - rim :]
        .add(returned[:, 3 * rim :])
    )
    grad_map = grad_own.astype(jnp.bfloat16)
    grad_conv_bias = jnp.sum(grad_map.astype(jnp.float32), axis=(0, 1, 2))
    grad_map_padded = jnp.pad(padded_2(grad_map, (("tile", 1),), 1), column_pad)
    grad_taps, grad_lateral_full = convolve_back(
        grad_map_padded, lateral_padded, grad_map, kernel_taps, height, breadth
    )
    grad_lateral = grad_lateral_full.astype(jnp.bfloat16)
    grad_lateral_w = jnp.einsum(
        "ihwc,ihwd->cd", features, grad_lateral, preferred_element_type=jnp.float32
    )
    grad_lateral_bias = jnp.sum(grad_lateral.astype(jnp.float32), axis=(0, 1, 2))
    grad_conv = jnp.concatenate([grad_lateral_w, grad_taps], axis=0)
    grad_head = jnp.stack(head_grads)
    grad_bias = jnp.concatenate([grad_lateral_bias, grad_conv_bias] + section_bias_grads)
    conv_sum, head_sum, bias_sum, loss_total, valid_sum = lax.psum(
        (grad_conv, grad_head, grad_bias, loss_part, jnp.sum(valid_float)), AXES
    )
    scale = 1.0 / valid_sum
    mine = lax.dynamic_slice_in_dim(slot_block, (at_img * n_tile + at_tile) * slots, slots)
    block_grad = jnp.where(
        (mine >= 0)[:, None, None], jnp.concatenate(block_parts, axis=0) * scale, 0.0
    )
    step = float(STEP)
    conv_new, conv_first_new, conv_second_new = adamw(
        conv_weight, conv_first, conv_second, conv_sum * scale, step
    )
    head_new, head_first_new, head_second_new = adamw(
        head_weight, head_first, head_second, head_sum * scale, step
    )
    bias_new, bias_first_new, bias_second_new = adamw(
        bias_vector, bias_first, bias_second, bias_sum * scale, step
    )
    block_new, block_first_new, block_second_new = adamw(
        block_master, block_first, block_second, block_grad, step
    )
    loss = (loss_total * scale).reshape(1)
    return (
        loss,
        conv_new,
        conv_first_new,
        conv_second_new,
        head_new,
        head_first_new,
        head_second_new,
        bias_new,
        bias_first_new,
        bias_second_new,
        block_new,
        block_first_new,
        block_second_new,
    )


def solution(mesh):
    split = P(AXES, None, None)
    return jax.shard_map(
        on_device,
        mesh=mesh,
        in_specs=(
            P("img", "tile", None, None),
            P(), P(), P(), P(), P(), P(), P(), P(), P(),
            split, split, split,
            P(),
            P(AXES),
            P(None, None, AXES),
            P(None, None, None, AXES),
            P(None, AXES),
            P(AXES),
            P(None, None, AXES),
        ),
        out_specs=(P(),) * 10 + (split,) * 3,
        check_vma=False,
    )
```

```python
import jax
import jax.numpy as jnp
from jax import lax
from jax.experimental import pallas as pl
from jax.experimental.pallas import tpu as pltpu
from jax.sharding import PartitionSpec as P

HR = 2
STEP = 5
BINS = 49
POOL = 7

BETA_ONE = 0.9
BETA_TWO = 0.999
RATE = 0.025
DECAY = 0.01
EPSILON = 1e-08

VMEM_LIMIT = 56 * 1024 * 1024
AXES = ("img", "tile")


def padded_2(cells, sides, width):
    for axis, dim in sides:
        count = lax.axis_size(axis)
        ends = count - 1
        head = lax.slice_in_dim(cells, 0, width, axis=dim)
        tail = lax.slice_in_dim(cells, cells.shape[dim] - width, cells.shape[dim], axis=dim)
        cells = jnp.concatenate(
            [
                lax.ppermute(tail, axis, [(i, (i + 1) % count) for i in range(ends)]),
                cells,
                lax.ppermute(head, axis, [((i + 1) % count, i) for i in range(ends)]),
            ],
            axis=dim,
        )
    return cells


def adamw(master, first, second, grad, step):
    first_new = BETA_ONE * first + (1.0 - BETA_ONE) * grad
    second_new = BETA_TWO * second + (1.0 - BETA_TWO) * grad * grad
    first_hat = first_new / (1.0 - BETA_ONE**step)
    second_hat = second_new / (1.0 - BETA_TWO**step)
    master_new = master - RATE * (first_hat / (jnp.sqrt(second_hat) + EPSILON) + DECAY * master)
    return (master_new, first_new, second_new)


def silu_slope(value):
    sigmoid = jax.nn.sigmoid(value)
    return sigmoid * (1.0 + value * (1.0 - sigmoid))


def convolve(padded, kernel_taps, height, breadth):
    summed = None
    for kernel_pos in range(9):
        row_shift = kernel_pos // 3
        col_shift = kernel_pos % 3
        window = padded[:, row_shift : row_shift + height, col_shift : col_shift + breadth]
        contrib = jnp.einsum(
            "ihwc,cd->ihwd", window, kernel_taps[kernel_pos], preferred_element_type=jnp.float32
        )
        summed = contrib if summed is None else summed + contrib
    return summed


def convolve_back(grad_padded, lateral_padded, grad_low, kernel_taps, height, breadth):
    grad_input = None
    tap_grads = []
    for kernel_pos in range(9):
        row_shift = kernel_pos // 3
        col_shift = kernel_pos % 3
        window = lateral_padded[:, row_shift : row_shift + height, col_shift : col_shift + breadth]
        tap_grads.append(
            jnp.einsum("ihwc,ihwd->cd", window, grad_low, preferred_element_type=jnp.float32)
        )
        source = grad_padded[
            :, 2 - row_shift : 2 - row_shift + height, 2 - col_shift : 2 - col_shift + breadth
        ]
        contrib = jnp.einsum(
            "ihwd,cd->ihwc", source, kernel_taps[kernel_pos], preferred_element_type=jnp.float32
        )
        grad_input = contrib if grad_input is None else grad_input + contrib
    return (jnp.concatenate(tap_grads, axis=0), grad_input)


def column_weights(column, frac, breadth):
    regions = column.shape[1]
    away = lax.broadcasted_iota(jnp.int32, (breadth, regions), 0) - column
    return jnp.where(away == 0, 1.0 - frac, jnp.where(away == 1, frac, 0.0))


def row_weight(row, frac, at):
    away = at - row
    return jnp.where(away == 0, 1.0 - frac, jnp.where(away == 1, frac, 0.0))


def pool_regions(map_t, rows, cols, fracs_row, fracs_col, breadth):
    section_count, bins, regions = rows.shape
    channels, cells = map_t.shape
    lines = cells // breadth
    group = POOL
    chunk = 8

    def body(map_ref, row_ref, col_ref, fr_ref, fc_ref, out_ref):
        turn = pl.program_id(1)

        def one_bin(b, carry):
            p = turn * group + b
            row = row_ref[0, pl.ds(p, 1), :]
            col = col_ref[0, pl.ds(p, 1), :]
            frow = fr_ref[0, pl.ds(p, 1), :]
            fcol = fc_ref[0, pl.ds(p, 1), :]
            across = column_weights(col, fcol, breadth)
            total = None
            for first in range(0, lines, chunk):
                weights = jnp.concatenate(
                    [
                        (across * row_weight(row, frow, line)).astype(jnp.bfloat16)
                        for line in range(first, first + chunk)
                    ],
                    axis=0,
                )
                part = jnp.dot(
                    map_ref[:, first * breadth : (first + chunk) * breadth],
                    weights,
                    preferred_element_type=jnp.float32,
                )
                total = part if total is None else total + part
            out_ref[0, b] = total.astype(jnp.bfloat16)
            return carry

        lax.fori_loop(0, group, one_bin, 0)

    samples = pl.BlockSpec((1, bins, regions), lambda u, t: (u, 0, 0))
    return pl.pallas_call(
        body,
        grid=(section_count, bins // group),
        in_specs=[pl.BlockSpec((channels, cells), lambda u, t: (0, 0))] + [samples] * 4,
        out_specs=pl.BlockSpec((1, group, channels, regions), lambda u, t: (u, t, 0, 0)),
        out_shape=jax.ShapeDtypeStruct((section_count, bins, channels, regions), jnp.bfloat16),
        compiler_params=pltpu.CompilerParams(vmem_limit_bytes=VMEM_LIMIT),
        cost_estimate=pl.CostEstimate(
            flops=2 * section_count * bins * regions * cells * channels,
            bytes_accessed=section_count * bins * regions * channels * 2,
            transcendentals=0,
        ),
        name="pool_regions",
    )(map_t, rows, cols, fracs_row, fracs_col)


def fetch_blocks(table, blocks_ref, buffer, sem, base, slot, count, block_rows):
    def one(b, carry):
        pltpu.make_async_copy(
            blocks_ref.at[table[base + b]],
            buffer.at[slot, pl.ds(pl.multiple_of(b * block_rows, block_rows), block_rows)],
            sem.at[slot],
        ).start()
        return carry

    lax.fori_loop(0, count, one, 0, unroll=8)


def first_layer(table, blocks, feats_t, section_blocks):
    section_count, bins, channels, regions = feats_t.shape
    _, block_rows, hidden = blocks.shape
    group = POOL
    turns = bins // group
    per_bin = channels // block_rows
    count = group * per_bin

    def body(table_ref, blocks_ref, x_ref, out_ref, buffer, sem):
        u, t = pl.program_id(0), pl.program_id(1)
        step = u * turns + t
        slot = lax.rem(step, 2)

        def fetch(at, into):
            base = (at // turns) * section_blocks + lax.rem(at, turns) * count
            fetch_blocks(table_ref, blocks_ref, buffer, sem, base, into, count, block_rows)

        @pl.when(step == 0)
        def _():
            fetch(step, slot)

        @pl.when(step + 1 < section_count * turns)
        def _():
            fetch(step + 1, 1 - slot)

        pltpu.make_async_copy(buffer.at[slot], buffer.at[slot], sem.at[slot]).wait()

        @pl.when(t == 0)
        def _():
            out_ref[...] = jnp.zeros_like(out_ref)

        def one_bin(b, carry):
            at = pl.ds(pl.multiple_of(b * channels, channels), channels)
            out_ref[0] += lax.dot_general(
                x_ref[0, b],
                buffer[slot, at],
                (((0,), (0,)), ((), ())),
                preferred_element_type=jnp.float32,
            )
            return carry

        lax.fori_loop(0, group, one_bin, 0)

    return pl.pallas_call(
        body,
        grid_spec=pltpu.PrefetchScalarGridSpec(
            num_scalar_prefetch=1,
            grid=(section_count, turns),
            in_specs=[
                pl.BlockSpec(memory_space=pl.ANY),
                pl.BlockSpec((1, group, channels, regions), lambda u, t, _: (u, t, 0, 0)),
            ],
            out_specs=pl.BlockSpec((1, regions, hidden), lambda u, t, _: (u, 0, 0)),
            scratch_shapes=[
                pltpu.VMEM((2, count * block_rows, hidden), jnp.bfloat16),
                pltpu.SemaphoreType.DMA((2,)),
            ],
        ),
        out_shape=jax.ShapeDtypeStruct((section_count, regions, hidden), jnp.float32),
        compiler_params=pltpu.CompilerParams(vmem_limit_bytes=VMEM_LIMIT),
        cost_estimate=pl.CostEstimate(
            flops=2 * section_count * bins * regions * channels * hidden,
            bytes_accessed=section_count * bins * channels * (regions + hidden) * 2,
            transcendentals=0,
        ),
        name="first_layer",
    )(table, blocks, feats_t)


def weight_grads(order, place, offsets, feats_t, acts_t, grads_first, grads_second, sizes):
    section_count, bins, channels, regions = feats_t.shape
    hidden = grads_first.shape[2]
    block_rows = sizes[0][1]
    group = POOL
    turns = bins // group + 1
    rows = group * channels
    wide = acts_t.shape[1]
    steps = section_count * turns
    kinds = len(sizes)

    def body(order_ref, place_ref, offset_ref, x_ref, a_ref, gf_ref, gs_ref, *rest):
        outs, (buffer, sem) = rest[:kinds], rest[kinds:]
        u, t = pl.program_id(0), pl.program_id(1)
        step = u * turns + t
        slot = lax.rem(step, 2)

        def drain(at, into):
            last = lax.rem(at, turns) == turns - 1

            @pl.when(last)
            def _():
                half = buffer.at[into, pl.ds(0, wide)]
                pltpu.make_async_copy(half, half, sem.at[into]).wait()

            @pl.when(jnp.logical_not(last))
            def _():
                pltpu.make_async_copy(buffer.at[into], buffer.at[into], sem.at[into]).wait()

        @pl.when(step >= 2)
        def _():
            drain(step - 2, slot)

        @pl.when(t < turns - 1)
        def _():
            def one_bin(b, carry):
                at = pl.ds(pl.multiple_of(b * channels, channels), channels)
                buffer[slot, at] = jnp.dot(
                    x_ref[0, b], gf_ref[0], preferred_element_type=jnp.float32
                ).astype(jnp.bfloat16)
                return carry

            lax.fori_loop(0, group, one_bin, 0)

        @pl.when(t == turns - 1)
        def _():
            def one_part(b, carry):
                at = pl.ds(pl.multiple_of(b * channels, channels), channels)
                buffer[slot, at] = jnp.dot(
                    a_ref[0, at], gs_ref[0], preferred_element_type=jnp.float32
                ).astype(jnp.bfloat16)
                return carry

            lax.fori_loop(0, wide // channels, one_part, 0)

        for kind in range(kinds):

            def one(i, carry, kind=kind):
                at = pl.ds(pl.multiple_of(order_ref[i] * block_rows, block_rows), block_rows)
                pltpu.make_async_copy(
                    buffer.at[slot, at], outs[kind].at[place_ref[i]], sem.at[slot]
                ).start()
                return carry

            lax.fori_loop(
                offset_ref[step * kinds + kind], offset_ref[step * kinds + kind + 1], one, 0
            )

        @pl.when(step == steps - 1)
        def _():
            drain(step - 1, 1 - slot)
            drain(step, slot)

    return pl.pallas_call(
        body,
        grid_spec=pltpu.PrefetchScalarGridSpec(
            num_scalar_prefetch=3,
            grid=(section_count, turns),
            in_specs=[
                pl.BlockSpec(
                    (1, group, channels, regions),
                    lambda u, t, *_: (u, jnp.minimum(t, turns - 2), 0, 0),
                ),
                pl.BlockSpec((1, wide, regions), lambda u, t, *_: (u, 0, 0)),
                pl.BlockSpec((1, regions, hidden), lambda u, t, *_: (u, 0, 0)),
                pl.BlockSpec((1, regions, hidden), lambda u, t, *_: (u, 0, 0)),
            ],
            out_specs=[pl.BlockSpec(memory_space=pl.ANY)] * kinds,
            scratch_shapes=[
                pltpu.VMEM((2, rows, hidden), jnp.bfloat16),
                pltpu.SemaphoreType.DMA((2,)),
            ],
        ),
        out_shape=[jax.ShapeDtypeStruct(size, jnp.bfloat16) for size in sizes],
        compiler_params=pltpu.CompilerParams(vmem_limit_bytes=VMEM_LIMIT),
        cost_estimate=pl.CostEstimate(
            flops=2 * section_count * regions * (bins * channels + wide) * hidden,
            bytes_accessed=section_count * (bins * channels + wide) * (regions + hidden) * 2,
            transcendentals=0,
        ),
        name="weight_grads",
    )(order, place, offsets, feats_t, acts_t, grads_first, grads_second)


def map_grads(before, span, table, blocks, grads_first, rows, cols, fracs_row, fracs_col, section_blocks, lines, breadth, after):
    section_count, bins, regions = rows.shape
    _, block_rows, hidden = blocks.shape
    cells, channels = before.shape
    group = POOL
    chunk = 8
    turns = bins // group
    count = group * channels // block_rows
    start, stop = span

    def body(table_ref, blocks_ref, g_ref, row_ref, col_ref, fr_ref, fc_ref, old_ref, after_ref, out_ref, buffer, sem, pooled, across, down, weights_a, weights_b):
        del after_ref
        step = start + pl.program_id(0)
        slot = lax.rem(step, 2)
        t = lax.rem(step, turns)

        def fetch(at, into):
            base = (at // turns) * section_blocks + lax.rem(at, turns) * count
            fetch_blocks(table_ref, blocks_ref, buffer, sem, base, into, count, block_rows)

        @pl.when(step == start)
        def _():
            fetch(step, slot)
            out_ref[...] = old_ref[...]

        @pl.when(step + 1 < stop)
        def _():
            fetch(step + 1, 1 - slot)

        pltpu.make_async_copy(buffer.at[slot], buffer.at[slot], sem.at[slot]).wait()

        def one_bin(b, carry):
            p = t * group + b
            at = pl.ds(pl.multiple_of(b * channels, channels), channels)
            pooled[at] = lax.dot_general(
                g_ref[0],
                buffer[slot, at],
                (((1,), (1,)), ((), ())),
                preferred_element_type=jnp.float32,
            ).astype(jnp.bfloat16)
            here = pl.ds(pl.multiple_of(b * regions, regions), regions)
            across[:, here] = column_weights(
                col_ref[0, pl.ds(p, 1), :], fc_ref[0, pl.ds(p, 1), :], breadth
            ).astype(jnp.bfloat16)
            row = row_ref[0, pl.ds(p, 1), :]
            frow = fr_ref[0, pl.ds(p, 1), :]
            at_line = lax.broadcasted_iota(jnp.int32, (lines, regions), 0)
            down[:, here] = row_weight(row, frow, at_line)
            return carry

        lax.fori_loop(0, group, one_bin, 0)

        def build(first, into):
            for i in range(chunk):
                into[i * breadth : (i + 1) * breadth] = across[...] * down[
                    first + i : first + i + 1, :
                ].astype(jnp.bfloat16)

        stores = (weights_a, weights_b)
        build(0, stores[0])
        for turn in range(lines // chunk):
            if turn + 1 < lines // chunk:
                build((turn + 1) * chunk, stores[(turn + 1) % 2])
            at = slice(turn * chunk * breadth, (turn + 1) * chunk * breadth)
            out_ref[at] += jnp.dot(
                stores[turn % 2][...], pooled[...], preferred_element_type=jnp.float32
            )

    samples = pl.BlockSpec((1, bins, regions), lambda i, _: ((start + i) // turns, 0, 0))
    whole = pl.BlockSpec((cells, channels), lambda i, _: (0, 0))
    return pl.pallas_call(
        body,
        grid_spec=pltpu.PrefetchScalarGridSpec(
            num_scalar_prefetch=1,
            grid=(stop - start,),
            in_specs=[
                pl.BlockSpec(memory_space=pl.ANY),
                pl.BlockSpec((1, regions, hidden), lambda i, _: ((start + i) // turns, 0, 0)),
            ]
            + [samples] * 4
            + [whole, pl.BlockSpec(memory_space=pl.ANY)],
            out_specs=whole,
            scratch_shapes=[
                pltpu.VMEM((2, count * block_rows, hidden), jnp.bfloat16),
                pltpu.SemaphoreType.DMA((2,)),
                pltpu.VMEM((group * channels, channels), jnp.bfloat16),
                pltpu.VMEM((breadth, group * regions), jnp.bfloat16),
                pltpu.VMEM((lines, group * regions), jnp.float32),
                pltpu.VMEM((chunk * breadth, group * regions), jnp.bfloat16),
                pltpu.VMEM((chunk * breadth, group * regions), jnp.bfloat16),
            ],
        ),
        out_shape=jax.ShapeDtypeStruct((cells, channels), jnp.float32),
        compiler_params=pltpu.CompilerParams(vmem_limit_bytes=VMEM_LIMIT),
        cost_estimate=pl.CostEstimate(
            flops=2 * (stop - start) * group * regions * channels * (hidden + cells),
            bytes_accessed=(stop - start) * count * block_rows * hidden * 2,
            transcendentals=0,
        ),
        name="map_grads",
    )(table, blocks, grads_first, rows, cols, fracs_row, fracs_col, before, after)


def sum_blocks(terms, half, after):
    _, block_rows, hidden = terms[0].shape
    batch = max(b for b in range(1, 17) if half % b == 0)
    count = len(terms)

    def body(*refs):
        total = None
        for ref in refs[:count]:
            value = ref[...].astype(jnp.float32)
            total = value if total is None else total + value
        refs[-1][...] = total.astype(jnp.bfloat16)

    return pl.pallas_call(
        body,
        grid=(half // batch,),
        in_specs=[
            pl.BlockSpec((batch, block_rows, hidden), lambda i: (i + half // batch, 0, 0))
        ] * count
        + [pl.BlockSpec(memory_space=pl.ANY)],
        out_specs=pl.BlockSpec((batch, block_rows, hidden), lambda i: (i, 0, 0)),
        out_shape=jax.ShapeDtypeStruct((half, block_rows, hidden), jnp.bfloat16),
        compiler_params=pltpu.CompilerParams(vmem_limit_bytes=VMEM_LIMIT),
        cost_estimate=pl.CostEstimate(
            flops=half * block_rows * hidden * count,
            bytes_accessed=half * block_rows * hidden * 2 * (count + 1),
            transcendentals=0,
        ),
        name="sum_blocks",
    )(*terms, after)


def bits_of(count):
    return list(range(count.bit_length() - 1))


PARTS = ((7, "zwxy"), (7, "yxzw"), (10, "xzyw"), (10, "yxzw"), (6, "zwxy"))
TURNS_AT = {0: 5, 5: 6, 7: 3, 8: 2, 10: 5}
REST_AT = 15


def part_orders(n_img, n_tile):
    bits = {
        "x": [("tile", b) for b in bits_of(n_tile)[:1]],
        "y": [("img", b) for b in bits_of(n_img)[1:]],
        "z": [("tile", b) for b in bits_of(n_tile)[1:2]],
        "w": [("tile", b) for b in bits_of(n_tile)[2:]],
    }
    return [[place for letter in order for place in bits[letter]] for _, order in PARTS]


def part_sizes(slots):
    total = sum(share for share, _ in PARTS)
    ends, done = [0], 0
    for share, _ in PARTS:
        done += share
        ends.append((done * slots + total // 2) // total)
    return [b - a for a, b in zip(ends, ends[1:])]


def swap(values, axis, bit):
    count = lax.axis_size(axis)
    return lax.ppermute(values, axis, [(i, i ^ (1 << bit)) for i in range(count)])


def sum_parts(kept, sent, orders, events):
    terms = [[k, swap(s, "img", 0)] for k, s in zip(kept, sent)]
    sums = [(stage, i) for stage in range(len(orders[0])) for i in range(len(orders))]
    last = kept[0]
    for at, (stage, i) in enumerate(sums):
        if at in events:
            last = events[at](last)
        half = terms[i][-1].shape[0] // 2
        last = sum_blocks(terms[i], half, last)
        terms[i].append(swap(last, *orders[i][stage]))
    results = []
    for part in terms:
        size = part[-1].shape[0]
        results.append(sum(term[:size].astype(jnp.float32) for term in part))
    return results


def sum_everywhere(wide, narrow, after, n_img, n_tile):
    x = [("tile", 1)]
    y = [("img", 1 << b) for b in bits_of(n_img)[1:]]
    z = [("tile", 1 << b) for b in bits_of(n_tile)[1:]]
    pair = [("img", 1)]
    orders = [pair + x + y + z, pair + y + z + x, pair + z + x + y]
    stages = len(orders[0])
    streams = len(orders)
    lanes = 128
    placed, rows = [], 0
    for i, array in enumerate(wide):
        for half in range(2):
            placed.append((i, half, rows, array.shape[0], lanes))
            rows += array.shape[0]
    for i, array in enumerate(narrow):
        placed.append((len(wide) + i, 0, rows, array.shape[0], array.shape[1]))
        rows += array.shape[0]
    unit = 8 * n_img * n_tile
    size = -(-rows // (streams * unit)) * unit
    operands = list(wide) + list(narrow)
    number = len(operands)

    def body(*refs):
        inputs = refs[:number]
        out_ref, total, landing, send, recv, send_back, recv_back = refs[number + 1 :]
        place = {"img": lax.axis_index("img"), "tile": lax.axis_index("tile")}

        def partner(axis, step):
            here = place[axis]
            bit = (here // step) % 2
            there = dict(place)
            there[axis] = here + step - 2 * step * bit
            return bit, (there["img"], there["tile"])

        barrier = pltpu.get_barrier_semaphore()
        for axis, step in orders[0]:
            _, there = partner(axis, step)
            pl.semaphore_signal(
                barrier, inc=1, device_id=there, device_id_type=pl.DeviceIdType.MESH
            )
        pl.semaphore_wait(barrier, stages)

        for i, half, first, count, columns in placed:
            if columns < lanes:
                total[first : first + count] = jnp.zeros((count, lanes), jnp.float32)
            total[first : first + count, :columns] = inputs[i][
                :, half * lanes : half * lanes + columns
            ]
        if rows < streams * size:
            total[rows:] = jnp.zeros((streams * size - rows, lanes), jnp.float32)

        start = [s * size for s in range(streams)]
        copies = {}

        def rows_at(first, count):
            return pl.ds(pl.multiple_of(first, 8), count)

        def send_half(s, k):
            half = size >> (k + 1)
            bit, there = partner(*orders[s][k])
            copy = pltpu.make_async_remote_copy(
                src_ref=total.at[rows_at(start[s] + (1 - bit) * half, half)],
                dst_ref=landing.at[pl.ds(s * size + size - 2 * half, half)],
                send_sem=send.at[s, k],
                recv_sem=recv.at[s, k],
                device_id=there,
                device_id_type=pl.DeviceIdType.MESH,
            )
            copy.start()
            copies[s, k] = copy

        for s in range(streams):
            send_half(s, 0)
        for k in range(stages):
            for s in range(streams):
                half = size >> (k + 1)
                bit, _ = partner(*orders[s][k])
                copies[s, k].wait()
                keep = rows_at(start[s] + bit * half, half)
                target = out_ref if k == stages - 1 else total
                target[keep] = total[keep] + landing[pl.ds(s * size + size - 2 * half, half)]
                start[s] = start[s] + bit * half
                if k + 1 < stages:
                    send_half(s, k + 1)

        def send_back_half(s, k):
            half = size >> (k + 1)
            _, there = partner(*orders[s][k])
            at = rows_at(start[s], half)
            copy = pltpu.make_async_remote_copy(
                src_ref=out_ref.at[at],
                dst_ref=out_ref.at[at],
                send_sem=send_back.at[s, k],
                recv_sem=recv_back.at[s, k],
                device_id=there,
                device_id_type=pl.DeviceIdType.MESH,
            )
            copy.start()
            copies[s, k] = copy

        for s in range(streams):
            send_back_half(s, stages - 1)
        for k in reversed(range(stages)):
            for s in range(streams):
                half = size >> (k + 1)
                bit, _ = partner(*orders[s][k])
                copies[s, k].wait()
                start[s] = start[s] - bit * half
                if k > 0:
                    send_back_half(s, k - 1)

    whole = pl.BlockSpec(memory_space=pltpu.VMEM)
    result = pl.pallas_call(
        body,
        in_specs=[whole] * number + [pl.BlockSpec(memory_space=pl.ANY)],
        out_specs=whole,
        out_shape=jax.ShapeDtypeStruct((streams * size, lanes), jnp.float32),
        scratch_shapes=[
            pltpu.VMEM((streams * size, lanes), jnp.float32),
            pltpu.VMEM((streams * size, lanes), jnp.float32),
        ]
        + [pltpu.SemaphoreType.DMA((streams, stages))] * 4,
        compiler_params=pltpu.CompilerParams(
            collective_id=0, has_side_effects=True, vmem_limit_bytes=VMEM_LIMIT
        ),
        name="sum_everywhere",
    )(*operands, after)
    results, at = [], 0
    for array in wide:
        count = array.shape[0]
        results.append(
            jnp.concatenate([result[at : at + count], result[at + count : at + 2 * count]], axis=1)
        )
        at += 2 * count
    for array in narrow:
        results.append(result[at : at + array.shape[0], : array.shape[1]])
        at += array.shape[0]
    return results


def on_device(
    features,
    conv_weight,
    conv_first,
    conv_second,
    head_weight,
    head_first,
    head_second,
    bias_vector,
    bias_first,
    bias_second,
    block_master,
    block_first,
    block_second,
    slot_block,
    roi_image,
    corner_index,
    corner_frac,
    labels,
    valid,
    box_deltas,
):
    images, height, breadth, in_channels = features.shape
    channels = conv_weight.shape[1]
    section_count, hidden, out_width = head_weight.shape
    classes = out_width - 4
    slots, block_rows, _ = block_master.shape
    all_slots = slot_block.shape[0]
    rim = HR
    first_rows = BINS * channels
    section_rows = first_rows + hidden
    section_blocks = section_rows // block_rows
    first_blocks = first_rows // block_rows
    block_total = section_count * section_blocks
    n_img, n_tile = lax.axis_size("img"), lax.axis_size("tile")
    at_img, at_tile = lax.axis_index("img"), lax.axis_index("tile")

    gathered = lax.all_gather(block_master.astype(jnp.bfloat16), AXES, axis=0, tiled=True)
    position = jnp.arange(all_slots, dtype=jnp.int32)
    owner_slot = (
        jnp.zeros((block_total,), jnp.int32)
        .at[jnp.where(slot_block >= 0, slot_block, block_total)]
        .set(position, mode="drop")
    )

    orders = part_orders(n_img, n_tile)
    shares = part_sizes(slots)
    groups = n_img * n_tile // 2
    owner = owner_slot // slots
    within = owner_slot % slots
    relative = {"img": (owner // n_tile) ^ at_img, "tile": (owner % n_tile) ^ at_tile}
    kind = jnp.zeros((block_total,), jnp.int32)
    place = jnp.zeros((block_total,), jnp.int32)
    start = 0
    for i, (order, share) in enumerate(zip(orders, shares)):
        rank = jnp.zeros((block_total,), jnp.int32)
        for axis, bit in order:
            rank = rank * 2 + ((relative[axis] >> bit) & 1)
        inside = (within >= start) & (within < start + share)
        kind = jnp.where(inside, 2 * i + (relative["img"] & 1), kind)
        place = jnp.where(inside, rank * share + within - start, place)
        start += share
    kinds = 2 * len(orders)
    block_id = jnp.arange(block_total, dtype=jnp.int32)
    per_turn = POOL * channels // block_rows
    turn = (block_id // section_blocks) * (POOL + 1) + (block_id % section_blocks) // per_turn
    bucket = turn * kinds + kind
    buckets = section_count * (POOL + 1) * kinds
    within_turn = (block_id % section_blocks) % per_turn
    _, order_list, place_list = lax.sort((bucket, within_turn, place), num_keys=1)
    offsets = jnp.sum(
        (bucket[None, :] < jnp.arange(buckets + 1, dtype=jnp.int32)[:, None]).astype(jnp.int32), axis=1
    )

    valid_float = valid.astype(jnp.float32)
    conv_low = conv_weight.astype(jnp.bfloat16)
    lateral_w = conv_low[:in_channels]
    kernel_taps = conv_low[in_channels:].reshape(9, channels, channels)
    head_all = head_weight.astype(jnp.bfloat16)
    lateral_bias = bias_vector[:channels]
    conv_bias = bias_vector[channels : 2 * channels]
    lateral = (
        jnp.einsum("ihwc,cd->ihwd", features, lateral_w, preferred_element_type=jnp.float32)
        + lateral_bias
    ).astype(jnp.bfloat16)
    column_pad = ((0, 0), (0, 0), (1, 1), (0, 0))
    lateral_padded = jnp.pad(padded_2(lateral, (("tile", 1),), 1), column_pad)
    feature_map = (convolve(lateral_padded, kernel_taps, height, breadth) + conv_bias).astype(
        jnp.bfloat16
    )
    map_padded = padded_2(feature_map, (("tile", 1),), rim)
    padded_rows = height + 2 * rim
    lines = images * padded_rows
    map_t = map_padded.reshape(lines * breadth, channels).T
    sample_rows = roi_image * padded_rows + corner_index // breadth
    sample_cols = corner_index % breadth
    fracs_row = corner_frac[:, 0]
    fracs_col = corner_frac[:, 1]
    feats_t = pool_regions(map_t, sample_rows, sample_cols, fracs_row, fracs_col, breadth)
    first_pres = first_layer(owner_slot, gathered, feats_t, section_blocks)

    loss_part = jnp.zeros((), jnp.float32)
    head_grads = []
    section_bias_grads = []
    acts_t, grads_first, grads_second = [], [], []
    for section in range(section_count):
        second_slots = lax.slice_in_dim(
            owner_slot, section * section_blocks + first_blocks, (section + 1) * section_blocks
        )
        second_matrix = gathered[second_slots].reshape(hidden, hidden)
        head_low = head_all[section]
        offset = 2 * channels + section * (2 * hidden + out_width)
        first_bias = bias_vector[offset : offset + hidden]
        second_bias = bias_vector[offset + hidden : offset + 2 * hidden]
        head_bias = bias_vector[offset + 2 * hidden : offset + 2 * hidden + out_width]
        first_pre = first_pres[section] + first_bias
        first_act = jax.nn.silu(first_pre).astype(jnp.bfloat16)
        acts_t.append(first_act.T)
        second_pre = (
            jnp.dot(first_act, second_matrix, preferred_element_type=jnp.float32) + second_bias
        )
        second_act = jax.nn.silu(second_pre).astype(jnp.bfloat16)
        outputs = jnp.dot(second_act, head_low, preferred_element_type=jnp.float32) + head_bias
        logits = outputs[:, :classes]
        shifted = logits - jnp.max(logits, axis=1, keepdims=True)
        log_total = jnp.log(jnp.sum(jnp.exp(shifted), axis=1, keepdims=True))
        one_hot = (
            labels[section][:, None] == jnp.arange(classes, dtype=jnp.int32)[None, :]
        ).astype(jnp.float32)
        cross = log_total[:, 0] - jnp.sum(shifted * one_hot, axis=1)
        foreground = (labels[section] > 0).astype(jnp.float32)
        target = box_deltas[section].T * (
            jnp.array([10.0, 10.0, 5.0, 5.0], jnp.float32) * (section + 1)
        )
        differ = outputs[:, classes:] - target
        magnitude = jnp.abs(differ)
        smooth = jnp.where(magnitude < 1.0, 0.5 * differ * differ, magnitude - 0.5)
        loss_part = loss_part + jnp.sum(
            valid_float * (cross + foreground * jnp.sum(smooth, axis=1))
        )
        probs = jnp.exp(shifted - log_total)
        grad_logits = valid_float[:, None] * (probs - one_hot)
        grad_box = (valid_float * foreground)[:, None] * jnp.clip(differ, -1.0, 1.0)
        grad_out = jnp.concatenate([grad_logits, grad_box], axis=1).astype(jnp.bfloat16)
        head_grads.append(
            jnp.einsum("rk,rf->kf", second_act, grad_out, preferred_element_type=jnp.float32)
        )
        grad_head_bias = jnp.sum(grad_out.astype(jnp.float32), axis=0)
        grad_second = (
            jnp.einsum("rf,kf->rk", grad_out, head_low, preferred_element_type=jnp.float32)
            * silu_slope(second_pre)
        ).astype(jnp.bfloat16)
        grad_second_bias = jnp.sum(grad_second.astype(jnp.float32), axis=0)
        grad_first = (
            jnp.einsum("rf,kf->rk", grad_second, second_matrix, preferred_element_type=jnp.float32)
            * silu_slope(first_pre)
        ).astype(jnp.bfloat16)
        grad_first_bias = jnp.sum(grad_first.astype(jnp.float32), axis=0)
        section_bias_grads.extend([grad_first_bias, grad_second_bias, grad_head_bias])
        grads_first.append(grad_first)
        grads_second.append(grad_second)
    acts_t = jnp.stack(acts_t)
    grads_first = jnp.stack(grads_first)
    grads_second = jnp.stack(grads_second)

    sizes = []
    for share in shares:
        sizes += [(groups * share, block_rows, hidden)] * 2
    parts = weight_grads(
        order_list, place_list, offsets, feats_t, acts_t, grads_first, grads_second, sizes
    )

    found = {"map": jnp.zeros((lines * breadth, channels), jnp.float32)}

    def turns_of(start, stop):
        def work(after):
            found["map"] = map_grads(
                found["map"], (start, stop), owner_slot, gathered, grads_first, sample_rows,
                sample_cols, fracs_row, fracs_col, section_blocks, lines, breadth, after,
            )
            return found["map"]

        return work

    def rest(after):
        grad_flat = found["map"]
        grad_padded_map = grad_flat.reshape(images, padded_rows, breadth, channels)
        outer_rims = jnp.concatenate(
            [grad_padded_map[:, :rim], grad_padded_map[:, rim + height :]], axis=1
        )
        returned = padded_2(outer_rims, (("tile", 1),), rim)
        grad_own = grad_padded_map[:, rim : rim + height]
        grad_own = (
            grad_own.at[:, :rim]
            .add(returned[:, :rim])
            .at[:, height - rim :]
            .add(returned[:, 3 * rim :])
        )
        grad_map = grad_own.astype(jnp.bfloat16)
        grad_conv_bias = jnp.sum(grad_map.astype(jnp.float32), axis=(0, 1, 2))
        grad_map_padded = jnp.pad(padded_2(grad_map, (("tile", 1),), 1), column_pad)
        grad_taps, grad_lateral_full = convolve_back(
            grad_map_padded, lateral_padded, grad_map, kernel_taps, height, breadth
        )
        grad_lateral = grad_lateral_full.astype(jnp.bfloat16)
        grad_lateral_w = jnp.einsum(
            "ihwc,ihwd->cd", features, grad_lateral, preferred_element_type=jnp.float32
        )
        grad_lateral_bias = jnp.sum(grad_lateral.astype(jnp.float32), axis=(0, 1, 2))
        misc = jnp.concatenate(
            [grad_lateral_bias, grad_conv_bias]
            + section_bias_grads
            + [loss_part[None], jnp.sum(valid_float)[None]]
        )
        filled = -(-misc.size // 1024) * 1024
        misc = jnp.pad(misc, (0, filled - misc.size)).reshape(-1, 128)
        heads = jnp.stack(head_grads).reshape(-1, out_width)
        found["sums"] = sum_everywhere(
            [grad_lateral_w, grad_taps], [heads, misc], after, n_img, n_tile
        )
        return found["sums"][-1]

    events, start = {}, 0
    for at, count in TURNS_AT.items():
        events[at] = turns_of(start, start + count)
        start += count
    events[REST_AT] = rest
    block_parts = sum_parts(parts[0::2], parts[1::2], orders, events)

    conv_sum = jnp.concatenate(found["sums"][:2], axis=0)
    head_sum = found["sums"][2].reshape(section_count, hidden, out_width)
    misc_sum = found["sums"][3].reshape(-1)
    biases = bias_vector.shape[0]
    bias_sum, loss_total, valid_sum = misc_sum[:biases], misc_sum[biases], misc_sum[biases + 1]
    scale = 1.0 / valid_sum
    mine = lax.dynamic_slice_in_dim(slot_block, (at_img * n_tile + at_tile) * slots, slots)
    block_grad = jnp.where(
        (mine >= 0)[:, None, None], jnp.concatenate(block_parts, axis=0) * scale, 0.0
    )
    step = float(STEP)
    conv_new, conv_first_new, conv_second_new = adamw(
        conv_weight, conv_first, conv_second, conv_sum * scale, step
    )
    head_new, head_first_new, head_second_new = adamw(
        head_weight, head_first, head_second, head_sum * scale, step
    )
    bias_new, bias_first_new, bias_second_new = adamw(
        bias_vector, bias_first, bias_second, bias_sum * scale, step
    )
    block_new, block_first_new, block_second_new = adamw(
        block_master, block_first, block_second, block_grad, step
    )
    loss = (loss_total * scale).reshape(1)
    return (
        loss,
        conv_new,
        conv_first_new,
        conv_second_new,
        head_new,
        head_first_new,
        head_second_new,
        bias_new,
        bias_first_new,
        bias_second_new,
        block_new,
        block_first_new,
        block_second_new,
    )


def solution(mesh):
    split = P(AXES, None, None)
    return jax.shard_map(
        on_device,
        mesh=mesh,
        in_specs=(
            P("img", "tile", None, None),
            P(), P(), P(), P(), P(), P(), P(), P(), P(),
            split, split, split,
            P(),
            P(AXES),
            P(None, None, AXES),
            P(None, None, None, AXES),
            P(None, AXES),
            P(AXES),
            P(None, None, AXES),
        ),
        out_specs=(P(),) * 10 + (split,) * 3,
        check_vma=False,
    )
```

```python
import jax
import jax.numpy as jnp
from jax import lax
from jax.experimental import pallas as pl
from jax.experimental.pallas import tpu as pltpu
from jax.sharding import PartitionSpec as P

HR = 2
STEP = 5
BINS = 49
POOL = 7

BETA_ONE = 0.9
BETA_TWO = 0.999
RATE = 0.025
DECAY = 0.01
EPSILON = 1e-08

VMEM_LIMIT = 56 * 1024 * 1024
AXES = ("img", "tile")


def padded_2(cells, sides, width):
    for axis, dim in sides:
        count = lax.axis_size(axis)
        ends = count - 1
        head = lax.slice_in_dim(cells, 0, width, axis=dim)
        tail = lax.slice_in_dim(cells, cells.shape[dim] - width, cells.shape[dim], axis=dim)
        cells = jnp.concatenate(
            [
                lax.ppermute(tail, axis, [(i, (i + 1) % count) for i in range(ends)]),
                cells,
                lax.ppermute(head, axis, [((i + 1) % count, i) for i in range(ends)]),
            ],
            axis=dim,
        )
    return cells


def adamw(master, first, second, grad, step):
    first_new = BETA_ONE * first + (1.0 - BETA_ONE) * grad
    second_new = BETA_TWO * second + (1.0 - BETA_TWO) * grad * grad
    first_hat = first_new / (1.0 - BETA_ONE**step)
    second_hat = second_new / (1.0 - BETA_TWO**step)
    master_new = master - RATE * (first_hat / (jnp.sqrt(second_hat) + EPSILON) + DECAY * master)
    return (master_new, first_new, second_new)


def silu_slope(value):
    sigmoid = jax.nn.sigmoid(value)
    return sigmoid * (1.0 + value * (1.0 - sigmoid))


def convolve(padded, kernel_taps, height, breadth):
    summed = None
    for kernel_pos in range(9):
        row_shift = kernel_pos // 3
        col_shift = kernel_pos % 3
        window = padded[:, row_shift : row_shift + height, col_shift : col_shift + breadth]
        contrib = jnp.einsum(
            "ihwc,cd->ihwd", window, kernel_taps[kernel_pos], preferred_element_type=jnp.float32
        )
        summed = contrib if summed is None else summed + contrib
    return summed


def convolve_back(grad_padded, lateral_padded, grad_low, kernel_taps, height, breadth):
    grad_input = None
    tap_grads = []
    for kernel_pos in range(9):
        row_shift = kernel_pos // 3
        col_shift = kernel_pos % 3
        window = lateral_padded[:, row_shift : row_shift + height, col_shift : col_shift + breadth]
        tap_grads.append(
            jnp.einsum("ihwc,ihwd->cd", window, grad_low, preferred_element_type=jnp.float32)
        )
        source = grad_padded[
            :, 2 - row_shift : 2 - row_shift + height, 2 - col_shift : 2 - col_shift + breadth
        ]
        contrib = jnp.einsum(
            "ihwd,cd->ihwc", source, kernel_taps[kernel_pos], preferred_element_type=jnp.float32
        )
        grad_input = contrib if grad_input is None else grad_input + contrib
    return (jnp.concatenate(tap_grads, axis=0), grad_input)


def column_weights(column, frac, breadth):
    regions = column.shape[1]
    away = lax.broadcasted_iota(jnp.int32, (breadth, regions), 0) - column
    return jnp.where(away == 0, 1.0 - frac, jnp.where(away == 1, frac, 0.0))


def row_weight(row, frac, at):
    away = at - row
    return jnp.where(away == 0, 1.0 - frac, jnp.where(away == 1, frac, 0.0))


def pool_regions(map_t, rows, cols, fracs_row, fracs_col, breadth):
    section_count, bins, regions = rows.shape
    channels, cells = map_t.shape
    lines = cells // breadth
    group = POOL
    chunk = 8

    def body(map_ref, row_ref, col_ref, fr_ref, fc_ref, out_ref):
        turn = pl.program_id(1)

        def one_bin(b, carry):
            p = turn * group + b
            row = row_ref[0, pl.ds(p, 1), :]
            col = col_ref[0, pl.ds(p, 1), :]
            frow = fr_ref[0, pl.ds(p, 1), :]
            fcol = fc_ref[0, pl.ds(p, 1), :]
            across = column_weights(col, fcol, breadth)
            total = None
            for first in range(0, lines, chunk):
                weights = jnp.concatenate(
                    [
                        (across * row_weight(row, frow, line)).astype(jnp.bfloat16)
                        for line in range(first, first + chunk)
                    ],
                    axis=0,
                )
                part = jnp.dot(
                    map_ref[:, first * breadth : (first + chunk) * breadth],
                    weights,
                    preferred_element_type=jnp.float32,
                )
                total = part if total is None else total + part
            out_ref[0, b] = total.astype(jnp.bfloat16)
            return carry

        lax.fori_loop(0, group, one_bin, 0)

    samples = pl.BlockSpec((1, bins, regions), lambda u, t: (u, 0, 0))
    return pl.pallas_call(
        body,
        grid=(section_count, bins // group),
        in_specs=[pl.BlockSpec((channels, cells), lambda u, t: (0, 0))] + [samples] * 4,
        out_specs=pl.BlockSpec((1, group, channels, regions), lambda u, t: (u, t, 0, 0)),
        out_shape=jax.ShapeDtypeStruct((section_count, bins, channels, regions), jnp.bfloat16),
        compiler_params=pltpu.CompilerParams(vmem_limit_bytes=VMEM_LIMIT),
        cost_estimate=pl.CostEstimate(
            flops=2 * section_count * bins * regions * cells * channels,
            bytes_accessed=section_count * bins * regions * channels * 2,
            transcendentals=0,
        ),
        name="pool_regions",
    )(map_t, rows, cols, fracs_row, fracs_col)


def fetch_blocks(table, blocks_ref, buffer, sem, base, slot, count, block_rows):
    def one(b, carry):
        pltpu.make_async_copy(
            blocks_ref.at[table[base + b]],
            buffer.at[slot, pl.ds(pl.multiple_of(b * block_rows, block_rows), block_rows)],
            sem.at[slot],
        ).start()
        return carry

    lax.fori_loop(0, count, one, 0, unroll=8)


def first_layer(table, blocks, feats_t, section_blocks):
    section_count, bins, channels, regions = feats_t.shape
    _, block_rows, hidden = blocks.shape
    group = POOL
    turns = bins // group
    per_bin = channels // block_rows
    count = group * per_bin

    def body(table_ref, blocks_ref, x_ref, out_ref, buffer, sem):
        u, t = pl.program_id(0), pl.program_id(1)
        step = u * turns + t
        slot = lax.rem(step, 2)

        def fetch(at, into):
            base = (at // turns) * section_blocks + lax.rem(at, turns) * count
            fetch_blocks(table_ref, blocks_ref, buffer, sem, base, into, count, block_rows)

        @pl.when(step == 0)
        def _():
            fetch(step, slot)

        @pl.when(step + 1 < section_count * turns)
        def _():
            fetch(step + 1, 1 - slot)

        pltpu.make_async_copy(buffer.at[slot], buffer.at[slot], sem.at[slot]).wait()

        @pl.when(t == 0)
        def _():
            out_ref[...] = jnp.zeros_like(out_ref)

        out_ref[0] += lax.dot_general(
            x_ref[0].reshape(group * channels, regions),
            buffer[slot],
            (((0,), (0,)), ((), ())),
            preferred_element_type=jnp.float32,
        )

    return pl.pallas_call(
        body,
        grid_spec=pltpu.PrefetchScalarGridSpec(
            num_scalar_prefetch=1,
            grid=(section_count, turns),
            in_specs=[
                pl.BlockSpec(memory_space=pl.ANY),
                pl.BlockSpec((1, group, channels, regions), lambda u, t, _: (u, t, 0, 0)),
            ],
            out_specs=pl.BlockSpec((1, regions, hidden), lambda u, t, _: (u, 0, 0)),
            scratch_shapes=[
                pltpu.VMEM((2, count * block_rows, hidden), jnp.bfloat16),
                pltpu.SemaphoreType.DMA((2,)),
            ],
        ),
        out_shape=jax.ShapeDtypeStruct((section_count, regions, hidden), jnp.float32),
        compiler_params=pltpu.CompilerParams(vmem_limit_bytes=VMEM_LIMIT),
        cost_estimate=pl.CostEstimate(
            flops=2 * section_count * bins * regions * channels * hidden,
            bytes_accessed=section_count * bins * channels * (regions + hidden) * 2,
            transcendentals=0,
        ),
        name="first_layer",
    )(table, blocks, feats_t)


def weight_grads(order, place, offsets, feats_t, acts_t, grads_first, grads_second, sizes):
    section_count, bins, channels, regions = feats_t.shape
    hidden = grads_first.shape[2]
    block_rows = sizes[0][1]
    group = POOL
    turns = bins // group + 1
    rows = group * channels
    wide = acts_t.shape[1]
    steps = section_count * turns
    kinds = len(sizes)

    def body(order_ref, place_ref, offset_ref, x_ref, a_ref, gf_ref, gs_ref, *rest):
        outs, (buffer, sem) = rest[:kinds], rest[kinds:]
        u, t = pl.program_id(0), pl.program_id(1)
        step = u * turns + t
        slot = lax.rem(step, 2)

        def drain(at, into):
            last = lax.rem(at, turns) == turns - 1

            @pl.when(last)
            def _():
                half = buffer.at[into, pl.ds(0, wide)]
                pltpu.make_async_copy(half, half, sem.at[into]).wait()

            @pl.when(jnp.logical_not(last))
            def _():
                pltpu.make_async_copy(buffer.at[into], buffer.at[into], sem.at[into]).wait()

        @pl.when(step >= 2)
        def _():
            drain(step - 2, slot)

        @pl.when(t < turns - 1)
        def _():
            buffer[slot] = jnp.dot(
                x_ref[0].reshape(rows, regions), gf_ref[0], preferred_element_type=jnp.float32
            ).astype(jnp.bfloat16)

        @pl.when(t == turns - 1)
        def _():
            buffer[slot, 0:wide] = jnp.dot(
                a_ref[0], gs_ref[0], preferred_element_type=jnp.float32
            ).astype(jnp.bfloat16)

        for kind in range(kinds):

            def one(i, carry, kind=kind):
                at = pl.ds(pl.multiple_of(order_ref[i] * block_rows, block_rows), block_rows)
                pltpu.make_async_copy(
                    buffer.at[slot, at], outs[kind].at[place_ref[i]], sem.at[slot]
                ).start()
                return carry

            lax.fori_loop(
                offset_ref[step * kinds + kind], offset_ref[step * kinds + kind + 1], one, 0
            )

        @pl.when(step == steps - 1)
        def _():
            drain(step - 1, 1 - slot)
            drain(step, slot)

    return pl.pallas_call(
        body,
        grid_spec=pltpu.PrefetchScalarGridSpec(
            num_scalar_prefetch=3,
            grid=(section_count, turns),
            in_specs=[
                pl.BlockSpec(
                    (1, group, channels, regions),
                    lambda u, t, *_: (u, jnp.minimum(t, turns - 2), 0, 0),
                ),
                pl.BlockSpec((1, wide, regions), lambda u, t, *_: (u, 0, 0)),
                pl.BlockSpec((1, regions, hidden), lambda u, t, *_: (u, 0, 0)),
                pl.BlockSpec((1, regions, hidden), lambda u, t, *_: (u, 0, 0)),
            ],
            out_specs=[pl.BlockSpec(memory_space=pl.ANY)] * kinds,
            scratch_shapes=[
                pltpu.VMEM((2, rows, hidden), jnp.bfloat16),
                pltpu.SemaphoreType.DMA((2,)),
            ],
        ),
        out_shape=[jax.ShapeDtypeStruct(size, jnp.bfloat16) for size in sizes],
        compiler_params=pltpu.CompilerParams(vmem_limit_bytes=VMEM_LIMIT),
        cost_estimate=pl.CostEstimate(
            flops=2 * section_count * regions * (bins * channels + wide) * hidden,
            bytes_accessed=section_count * (bins * channels + wide) * (regions + hidden) * 2,
            transcendentals=0,
        ),
        name="weight_grads",
    )(order, place, offsets, feats_t, acts_t, grads_first, grads_second)


def map_grads(before, span, table, blocks, grads_first, rows, cols, fracs_row, fracs_col, section_blocks, lines, breadth, after):
    section_count, bins, regions = rows.shape
    _, block_rows, hidden = blocks.shape
    cells, channels = before.shape
    group = POOL
    chunk = 8
    turns = bins // group
    count = group * channels // block_rows
    start, stop = span

    def body(table_ref, blocks_ref, g_ref, row_ref, col_ref, fr_ref, fc_ref, old_ref, after_ref, out_ref, buffer, sem, pooled, across, down, weights_a, weights_b):
        del after_ref
        step = start + pl.program_id(0)
        slot = lax.rem(step, 2)
        t = lax.rem(step, turns)

        def fetch(at, into):
            base = (at // turns) * section_blocks + lax.rem(at, turns) * count
            fetch_blocks(table_ref, blocks_ref, buffer, sem, base, into, count, block_rows)

        @pl.when(step == start)
        def _():
            fetch(step, slot)
            out_ref[...] = old_ref[...]

        @pl.when(step + 1 < stop)
        def _():
            fetch(step + 1, 1 - slot)

        pltpu.make_async_copy(buffer.at[slot], buffer.at[slot], sem.at[slot]).wait()

        grads = lax.dot_general(
            g_ref[0], buffer[slot], (((1,), (1,)), ((), ())), preferred_element_type=jnp.float32
        )
        for b in range(group):
            pooled[b * regions : (b + 1) * regions] = grads[
                :, b * channels : (b + 1) * channels
            ].astype(jnp.bfloat16)

        def one_bin(b, carry):
            p = t * group + b
            here = pl.ds(pl.multiple_of(b * regions, regions), regions)
            across[:, here] = column_weights(
                col_ref[0, pl.ds(p, 1), :], fc_ref[0, pl.ds(p, 1), :], breadth
            ).astype(jnp.bfloat16)
            row = row_ref[0, pl.ds(p, 1), :]
            frow = fr_ref[0, pl.ds(p, 1), :]
            at_line = lax.broadcasted_iota(jnp.int32, (lines, regions), 0)
            down[:, here] = row_weight(row, frow, at_line)
            return carry

        lax.fori_loop(0, group, one_bin, 0)

        def build(first, into):
            for i in range(chunk):
                into[i * breadth : (i + 1) * breadth] = across[...] * down[
                    first + i : first + i + 1, :
                ].astype(jnp.bfloat16)

        stores = (weights_a, weights_b)
        build(0, stores[0])
        for turn in range(lines // chunk):
            if turn + 1 < lines // chunk:
                build((turn + 1) * chunk, stores[(turn + 1) % 2])
            at = slice(turn * chunk * breadth, (turn + 1) * chunk * breadth)
            out_ref[at] += jnp.dot(
                stores[turn % 2][...], pooled[...], preferred_element_type=jnp.float32
            )

    samples = pl.BlockSpec((1, bins, regions), lambda i, _: ((start + i) // turns, 0, 0))
    whole = pl.BlockSpec((cells, channels), lambda i, _: (0, 0))
    return pl.pallas_call(
        body,
        grid_spec=pltpu.PrefetchScalarGridSpec(
            num_scalar_prefetch=1,
            grid=(stop - start,),
            in_specs=[
                pl.BlockSpec(memory_space=pl.ANY),
                pl.BlockSpec((1, regions, hidden), lambda i, _: ((start + i) // turns, 0, 0)),
            ]
            + [samples] * 4
            + [whole, pl.BlockSpec(memory_space=pl.ANY)],
            out_specs=whole,
            scratch_shapes=[
                pltpu.VMEM((2, count * block_rows, hidden), jnp.bfloat16),
                pltpu.SemaphoreType.DMA((2,)),
                pltpu.VMEM((group * regions, channels), jnp.bfloat16),
                pltpu.VMEM((breadth, group * regions), jnp.bfloat16),
                pltpu.VMEM((lines, group * regions), jnp.float32),
                pltpu.VMEM((chunk * breadth, group * regions), jnp.bfloat16),
                pltpu.VMEM((chunk * breadth, group * regions), jnp.bfloat16),
            ],
        ),
        out_shape=jax.ShapeDtypeStruct((cells, channels), jnp.float32),
        compiler_params=pltpu.CompilerParams(vmem_limit_bytes=VMEM_LIMIT),
        cost_estimate=pl.CostEstimate(
            flops=2 * (stop - start) * group * regions * channels * (hidden + cells),
            bytes_accessed=(stop - start) * count * block_rows * hidden * 2,
            transcendentals=0,
        ),
        name="map_grads",
    )(table, blocks, grads_first, rows, cols, fracs_row, fracs_col, before, after)


def sum_blocks(terms, half, after):
    _, block_rows, hidden = terms[0].shape
    batch = max(b for b in range(1, 17) if half % b == 0)
    count = len(terms)

    def body(*refs):
        total = None
        for ref in refs[:count]:
            value = ref[...].astype(jnp.float32)
            total = value if total is None else total + value
        refs[-1][...] = total.astype(jnp.bfloat16)

    return pl.pallas_call(
        body,
        grid=(half // batch,),
        in_specs=[
            pl.BlockSpec((batch, block_rows, hidden), lambda i: (i + half // batch, 0, 0))
        ] * count
        + [pl.BlockSpec(memory_space=pl.ANY)],
        out_specs=pl.BlockSpec((batch, block_rows, hidden), lambda i: (i, 0, 0)),
        out_shape=jax.ShapeDtypeStruct((half, block_rows, hidden), jnp.bfloat16),
        compiler_params=pltpu.CompilerParams(vmem_limit_bytes=VMEM_LIMIT),
        cost_estimate=pl.CostEstimate(
            flops=half * block_rows * hidden * count,
            bytes_accessed=half * block_rows * hidden * 2 * (count + 1),
            transcendentals=0,
        ),
        name="sum_blocks",
    )(*terms, after)


def bits_of(count):
    return list(range(count.bit_length() - 1))


PARTS = ((7, "zwxy"), (7, "yxzw"), (10, "xzyw"), (10, "yxzw"), (6, "zwxy"))
TURNS_AT = {0: 5, 5: 7, 7: 3, 8: 6}
EDGES_AT = 11
REST_AT = 12


def part_orders(n_img, n_tile):
    bits = {
        "x": [("tile", b) for b in bits_of(n_tile)[:1]],
        "y": [("img", b) for b in bits_of(n_img)[1:]],
        "z": [("tile", b) for b in bits_of(n_tile)[1:2]],
        "w": [("tile", b) for b in bits_of(n_tile)[2:]],
    }
    return [[place for letter in order for place in bits[letter]] for _, order in PARTS]


def part_sizes(slots):
    total = sum(share for share, _ in PARTS)
    ends, done = [0], 0
    for share, _ in PARTS:
        done += share
        ends.append((done * slots + total // 2) // total)
    return [b - a for a, b in zip(ends, ends[1:])]


def swap(values, axis, bit):
    count = lax.axis_size(axis)
    return lax.ppermute(values, axis, [(i, i ^ (1 << bit)) for i in range(count)])


def sum_parts(kept, sent, orders, events):
    terms = [[k, swap(s, "img", 0)] for k, s in zip(kept, sent)]
    sums = [(stage, i) for stage in range(len(orders[0])) for i in range(len(orders))]
    last = kept[0]
    for at, (stage, i) in enumerate(sums):
        if at in events:
            last = events[at](last)
        half = terms[i][-1].shape[0] // 2
        last = sum_blocks(terms[i], half, last)
        terms[i].append(swap(last, *orders[i][stage]))
    return terms


def sum_everywhere(wide, narrow, exact, after, n_img, n_tile):
    x = [("tile", 1)]
    y = [("img", 1 << b) for b in bits_of(n_img)[1:]]
    z = [("tile", 1 << b) for b in bits_of(n_tile)[1:]]
    pair = [("img", 1)]
    orders = [pair + x + y + z, pair + y + z + x, pair + z + x + y]
    stages = len(orders[0])
    lanes = 128
    placed, rows = [], 0
    for i, array in enumerate(wide):
        for half in range(2):
            placed.append((i, half, rows, array.shape[0], lanes))
            rows += array.shape[0]
    for i, array in enumerate(narrow):
        placed.append((len(wide) + i, 0, rows, array.shape[0], array.shape[1]))
        rows += array.shape[0]
    unit = 16 * n_img * n_tile
    units = -(-rows // unit)
    streams, first = [], 0
    for i, order in enumerate(orders):
        size = (units + len(orders) - 1 - i) // len(orders) * unit
        if size:
            streams.append((order, first, size, True))
            first += size
    filled = first
    count = exact.shape[0]
    small = -(-count // (8 * n_img * n_tile)) * 8 * n_img * n_tile
    streams.append((orders[0], 0, small, False))
    operands = list(wide) + list(narrow) + [exact]
    number = len(operands)

    def body(*refs):
        inputs = refs[:number]
        (out_low, out_exact, total, going, landing, total_exact, landing_exact) = refs[
            number + 1 : number + 8
        ]
        send, recv, send_back, recv_back = refs[number + 8 :]
        place = {"img": lax.axis_index("img"), "tile": lax.axis_index("tile")}

        def partner(axis, step):
            here = place[axis]
            bit = (here // step) % 2
            there = dict(place)
            there[axis] = here + step - 2 * step * bit
            return bit, (there["img"], there["tile"])

        barrier = pltpu.get_barrier_semaphore()
        for axis, step in orders[0]:
            _, there = partner(axis, step)
            pl.semaphore_signal(
                barrier, inc=1, device_id=there, device_id_type=pl.DeviceIdType.MESH
            )
        for i, half, first, size, columns in placed:
            if columns < lanes:
                total[first : first + size] = jnp.zeros((size, lanes), jnp.float32)
            total[first : first + size, :columns] = inputs[i][
                :, half * lanes : half * lanes + columns
            ]
        if rows < filled:
            total[rows:] = jnp.zeros((filled - rows, lanes), jnp.float32)
        total_exact[...] = jnp.zeros_like(total_exact)
        total_exact[0:count] = inputs[-1][...]
        pl.semaphore_wait(barrier, stages)

        start = [first for _, first, _, _ in streams]
        copies = {}

        def rows_at(first, size):
            return pl.ds(pl.multiple_of(first, min(size, 16)), size)

        def remote(source, target, there, sent, received):
            copy = pltpu.make_async_remote_copy(
                src_ref=source,
                dst_ref=target,
                send_sem=sent,
                recv_sem=received,
                device_id=there,
                device_id_type=pl.DeviceIdType.MESH,
            )
            copy.start()
            return copy

        def send_half(s, k):
            order, first, size, low = streams[s]
            half = size >> (k + 1)
            bit, there = partner(*order[k])
            away = rows_at(start[s] + (1 - bit) * half, half)
            landed = pl.ds(first + size - 2 * half, half)
            if low:
                going[away] = total[away].astype(jnp.bfloat16)
                source, target = going.at[away], landing.at[landed]
            else:
                source, target = total_exact.at[away], landing_exact.at[landed]
            copies[s, k] = remote(source, target, there, send.at[s, k], recv.at[s, k])

        for s in range(len(streams)):
            send_half(s, 0)
        for k in range(stages):
            for s, (order, first, size, low) in enumerate(streams):
                half = size >> (k + 1)
                bit, _ = partner(*order[k])
                copies[s, k].wait()
                keep = rows_at(start[s] + bit * half, half)
                landed = pl.ds(first + size - 2 * half, half)
                if low:
                    value = total[keep] + landing[landed].astype(jnp.float32)
                    if k == stages - 1:
                        out_low[keep] = value.astype(jnp.bfloat16)
                    else:
                        total[keep] = value
                else:
                    target = out_exact if k == stages - 1 else total_exact
                    target[keep] = total_exact[keep] + landing_exact[landed]
                start[s] = start[s] + bit * half
                if k + 1 < stages:
                    send_half(s, k + 1)

        def send_back_half(s, k):
            order, _, size, low = streams[s]
            half = size >> (k + 1)
            _, there = partner(*order[k])
            at = rows_at(start[s], half)
            out = out_low if low else out_exact
            copies[s, k] = remote(
                out.at[at], out.at[at], there, send_back.at[s, k], recv_back.at[s, k]
            )

        for s in range(len(streams)):
            send_back_half(s, stages - 1)
        for k in reversed(range(stages)):
            for s, (order, _, size, _) in enumerate(streams):
                half = size >> (k + 1)
                bit, _ = partner(*order[k])
                copies[s, k].wait()
                start[s] = start[s] - bit * half
                if k > 0:
                    send_back_half(s, k - 1)

    whole = pl.BlockSpec(memory_space=pltpu.VMEM)
    low, high = pl.pallas_call(
        body,
        in_specs=[whole] * number + [pl.BlockSpec(memory_space=pl.ANY)],
        out_specs=[whole, whole],
        out_shape=[
            jax.ShapeDtypeStruct((filled, lanes), jnp.bfloat16),
            jax.ShapeDtypeStruct((small, lanes), jnp.float32),
        ],
        scratch_shapes=[
            pltpu.VMEM((filled, lanes), jnp.float32),
            pltpu.VMEM((filled, lanes), jnp.bfloat16),
            pltpu.VMEM((filled, lanes), jnp.bfloat16),
            pltpu.VMEM((small, lanes), jnp.float32),
            pltpu.VMEM((small, lanes), jnp.float32),
        ]
        + [pltpu.SemaphoreType.DMA((len(streams), stages))] * 4,
        compiler_params=pltpu.CompilerParams(
            collective_id=0, has_side_effects=True, vmem_limit_bytes=VMEM_LIMIT
        ),
        name="sum_everywhere",
    )(*operands, after)
    results, at = [], 0
    for array in wide:
        size = array.shape[0]
        results.append(
            jnp.concatenate([low[at : at + size], low[at + size : at + 2 * size]], axis=1).astype(
                jnp.float32
            )
        )
        at += 2 * size
    for array in narrow:
        results.append(low[at : at + array.shape[0], : array.shape[1]].astype(jnp.float32))
        at += array.shape[0]
    return results + [high[:count]]


def edge_rows(grad_flat, from_last, from_next, images, height, breadth, rim, after):
    channels = grad_flat.shape[1]
    padded = height + 2 * rim
    low, high = from_last.astype(jnp.bfloat16), from_next.astype(jnp.bfloat16)

    def body(own_ref, last_ref, next_ref, after_ref, out_ref):
        del after_ref
        for i in range(images):
            for r in range(height + 2):
                line = r + rim - 1
                at = (i * padded + line) * breadth
                value = own_ref[at : at + breadth]
                if r < rim + 1:
                    value = value + last_ref[i, r].astype(jnp.float32)
                if r >= height + 1 - rim:
                    value = value + next_ref[i, r - (height + 1 - rim)].astype(jnp.float32)
                out_ref[i, r] = value.astype(jnp.bfloat16)

    whole = pl.BlockSpec(memory_space=pltpu.VMEM)
    return pl.pallas_call(
        body,
        in_specs=[whole] * 3 + [pl.BlockSpec(memory_space=pl.ANY)],
        out_specs=whole,
        out_shape=jax.ShapeDtypeStruct((images, height + 2, breadth, channels), jnp.bfloat16),
        compiler_params=pltpu.CompilerParams(vmem_limit_bytes=VMEM_LIMIT),
        name="edge_rows",
    )(grad_flat, low, high, after)


def finish_blocks(terms, start, share, masters, firsts, seconds, held, scale, old):
    slots, block_rows, hidden = masters.shape
    count = len(terms)
    correct_one = 1.0 - BETA_ONE ** float(STEP)
    correct_two = 1.0 - BETA_TWO ** float(STEP)

    def body(held_ref, scale_ref, *refs):
        total = None
        for ref in refs[:count]:
            value = ref[...].astype(jnp.float32)
            total = value if total is None else total + value
        w_ref, m_ref, v_ref = refs[count : count + 3]
        outs = refs[-3:]
        mine = held_ref[start + pl.program_id(0)] >= 0
        grad = jnp.where(mine, total * scale_ref[0], 0.0)
        first_new = BETA_ONE * m_ref[...] + (1.0 - BETA_ONE) * grad
        second_new = BETA_TWO * v_ref[...] + (1.0 - BETA_TWO) * grad * grad
        rooted = jnp.sqrt(second_new * (1.0 / correct_two)) + EPSILON
        outs[0][...] = w_ref[...] - RATE * (
            first_new * (1.0 / correct_one) / rooted + DECAY * w_ref[...]
        )
        outs[1][...] = first_new
        outs[2][...] = second_new

    term = pl.BlockSpec((1, block_rows, hidden), lambda i: (i, 0, 0))
    slot = pl.BlockSpec((1, block_rows, hidden), lambda i: (start + i, 0, 0))
    smem = pl.BlockSpec(memory_space=pltpu.SMEM)
    kept = [] if old is None else list(old)
    inputs = [held, scale] + list(terms) + [masters, firsts, seconds] + kept
    return pl.pallas_call(
        body,
        grid=(share,),
        in_specs=[smem, smem]
        + [term] * count
        + [slot] * 3
        + [pl.BlockSpec(memory_space=pl.ANY)] * len(kept),
        out_specs=[slot] * 3,
        out_shape=[jax.ShapeDtypeStruct(masters.shape, jnp.float32)] * 3,
        input_output_aliases={len(inputs) - 3 + j: j for j in range(len(kept))},
        compiler_params=pltpu.CompilerParams(vmem_limit_bytes=VMEM_LIMIT),
        name="finish_blocks",
    )(*inputs)


def on_device(
    features,
    conv_weight,
    conv_first,
    conv_second,
    head_weight,
    head_first,
    head_second,
    bias_vector,
    bias_first,
    bias_second,
    block_master,
    block_first,
    block_second,
    slot_block,
    roi_image,
    corner_index,
    corner_frac,
    labels,
    valid,
    box_deltas,
):
    images, height, breadth, in_channels = features.shape
    channels = conv_weight.shape[1]
    section_count, hidden, out_width = head_weight.shape
    classes = out_width - 4
    slots, block_rows, _ = block_master.shape
    all_slots = slot_block.shape[0]
    rim = HR
    first_rows = BINS * channels
    section_rows = first_rows + hidden
    section_blocks = section_rows // block_rows
    first_blocks = first_rows // block_rows
    block_total = section_count * section_blocks
    n_img, n_tile = lax.axis_size("img"), lax.axis_size("tile")
    at_img, at_tile = lax.axis_index("img"), lax.axis_index("tile")

    gathered = lax.all_gather(block_master.astype(jnp.bfloat16), AXES, axis=0, tiled=True)
    position = jnp.arange(all_slots, dtype=jnp.int32)
    owner_slot = (
        jnp.zeros((block_total,), jnp.int32)
        .at[jnp.where(slot_block >= 0, slot_block, block_total)]
        .set(position, mode="drop")
    )

    orders = part_orders(n_img, n_tile)
    shares = part_sizes(slots)
    groups = n_img * n_tile // 2
    owner = owner_slot // slots
    within = owner_slot % slots
    relative = {"img": (owner // n_tile) ^ at_img, "tile": (owner % n_tile) ^ at_tile}
    kind = jnp.zeros((block_total,), jnp.int32)
    place = jnp.zeros((block_total,), jnp.int32)
    start = 0
    for i, (order, share) in enumerate(zip(orders, shares)):
        rank = jnp.zeros((block_total,), jnp.int32)
        for axis, bit in order:
            rank = rank * 2 + ((relative[axis] >> bit) & 1)
        inside = (within >= start) & (within < start + share)
        kind = jnp.where(inside, 2 * i + (relative["img"] & 1), kind)
        place = jnp.where(inside, rank * share + within - start, place)
        start += share
    kinds = 2 * len(orders)
    block_id = jnp.arange(block_total, dtype=jnp.int32)
    per_turn = POOL * channels // block_rows
    turn = (block_id // section_blocks) * (POOL + 1) + (block_id % section_blocks) // per_turn
    bucket = turn * kinds + kind
    buckets = section_count * (POOL + 1) * kinds
    within_turn = (block_id % section_blocks) % per_turn
    _, order_list, place_list = lax.sort((bucket, within_turn, place), num_keys=1)
    offsets = jnp.sum(
        (bucket[None, :] < jnp.arange(buckets + 1, dtype=jnp.int32)[:, None]).astype(jnp.int32), axis=1
    )

    valid_float = valid.astype(jnp.float32)
    conv_low = conv_weight.astype(jnp.bfloat16)
    lateral_w = conv_low[:in_channels]
    kernel_taps = conv_low[in_channels:].reshape(9, channels, channels)
    head_all = head_weight.astype(jnp.bfloat16)
    lateral_bias = bias_vector[:channels]
    conv_bias = bias_vector[channels : 2 * channels]
    lateral = (
        jnp.einsum("ihwc,cd->ihwd", features, lateral_w, preferred_element_type=jnp.float32)
        + lateral_bias
    ).astype(jnp.bfloat16)
    column_pad = ((0, 0), (0, 0), (1, 1), (0, 0))
    lateral_padded = jnp.pad(padded_2(lateral, (("tile", 1),), 1), column_pad)
    feature_map = (convolve(lateral_padded, kernel_taps, height, breadth) + conv_bias).astype(
        jnp.bfloat16
    )
    map_padded = padded_2(feature_map, (("tile", 1),), rim)
    padded_rows = height + 2 * rim
    lines = images * padded_rows
    map_t = map_padded.reshape(lines * breadth, channels).T
    sample_rows = roi_image * padded_rows + corner_index // breadth
    sample_cols = corner_index % breadth
    fracs_row = corner_frac[:, 0]
    fracs_col = corner_frac[:, 1]
    feats_t = pool_regions(map_t, sample_rows, sample_cols, fracs_row, fracs_col, breadth)
    first_pres = first_layer(owner_slot, gathered, feats_t, section_blocks)

    loss_part = jnp.zeros((), jnp.float32)
    head_grads = []
    section_bias_grads = []
    acts_t, grads_first, grads_second = [], [], []
    for section in range(section_count):
        second_slots = lax.slice_in_dim(
            owner_slot, section * section_blocks + first_blocks, (section + 1) * section_blocks
        )
        second_matrix = gathered[second_slots].reshape(hidden, hidden)
        head_low = head_all[section]
        offset = 2 * channels + section * (2 * hidden + out_width)
        first_bias = bias_vector[offset : offset + hidden]
        second_bias = bias_vector[offset + hidden : offset + 2 * hidden]
        head_bias = bias_vector[offset + 2 * hidden : offset + 2 * hidden + out_width]
        first_pre = first_pres[section] + first_bias
        first_act = jax.nn.silu(first_pre).astype(jnp.bfloat16)
        acts_t.append(first_act.T)
        second_pre = (
            jnp.dot(first_act, second_matrix, preferred_element_type=jnp.float32) + second_bias
        )
        second_act = jax.nn.silu(second_pre).astype(jnp.bfloat16)
        outputs = jnp.dot(second_act, head_low, preferred_element_type=jnp.float32) + head_bias
        logits = outputs[:, :classes]
        shifted = logits - jnp.max(logits, axis=1, keepdims=True)
        log_total = jnp.log(jnp.sum(jnp.exp(shifted), axis=1, keepdims=True))
        one_hot = (
            labels[section][:, None] == jnp.arange(classes, dtype=jnp.int32)[None, :]
        ).astype(jnp.float32)
        cross = log_total[:, 0] - jnp.sum(shifted * one_hot, axis=1)
        foreground = (labels[section] > 0).astype(jnp.float32)
        target = box_deltas[section].T * (
            jnp.array([10.0, 10.0, 5.0, 5.0], jnp.float32) * (section + 1)
        )
        differ = outputs[:, classes:] - target
        magnitude = jnp.abs(differ)
        smooth = jnp.where(magnitude < 1.0, 0.5 * differ * differ, magnitude - 0.5)
        loss_part = loss_part + jnp.sum(
            valid_float * (cross + foreground * jnp.sum(smooth, axis=1))
        )
        probs = jnp.exp(shifted - log_total)
        grad_logits = valid_float[:, None] * (probs - one_hot)
        grad_box = (valid_float * foreground)[:, None] * jnp.clip(differ, -1.0, 1.0)
        grad_out = jnp.concatenate([grad_logits, grad_box], axis=1).astype(jnp.bfloat16)
        head_grads.append(
            jnp.einsum("rk,rf->kf", second_act, grad_out, preferred_element_type=jnp.float32)
        )
        grad_head_bias = jnp.sum(grad_out.astype(jnp.float32), axis=0)
        grad_second = (
            jnp.einsum("rf,kf->rk", grad_out, head_low, preferred_element_type=jnp.float32)
            * silu_slope(second_pre)
        ).astype(jnp.bfloat16)
        grad_second_bias = jnp.sum(grad_second.astype(jnp.float32), axis=0)
        grad_first = (
            jnp.einsum("rf,kf->rk", grad_second, second_matrix, preferred_element_type=jnp.float32)
            * silu_slope(first_pre)
        ).astype(jnp.bfloat16)
        grad_first_bias = jnp.sum(grad_first.astype(jnp.float32), axis=0)
        section_bias_grads.extend([grad_first_bias, grad_second_bias, grad_head_bias])
        grads_first.append(grad_first)
        grads_second.append(grad_second)
    acts_t = jnp.stack(acts_t)
    grads_first = jnp.stack(grads_first)
    grads_second = jnp.stack(grads_second)

    sizes = []
    for share in shares:
        sizes += [(groups * share, block_rows, hidden)] * 2
    parts = weight_grads(
        order_list, place_list, offsets, feats_t, acts_t, grads_first, grads_second, sizes
    )

    found = {"map": jnp.zeros((lines * breadth, channels), jnp.float32)}

    def turns_of(start, stop):
        def work(after):
            found["map"] = map_grads(
                found["map"], (start, stop), owner_slot, gathered, grads_first, sample_rows,
                sample_cols, fracs_row, fracs_col, section_blocks, lines, breadth, after,
            )
            return found["map"]

        return work

    def edges(after):
        grad_padded_map = found["map"].reshape(images, padded_rows, breadth, channels)
        to_next = grad_padded_map[:, height + rim - 1 :].astype(jnp.bfloat16)
        to_last = grad_padded_map[:, : rim + 1].astype(jnp.bfloat16)
        ends = n_tile - 1
        from_last = lax.ppermute(to_next, "tile", [(i, i + 1) for i in range(ends)])
        from_next = lax.ppermute(to_last, "tile", [(i + 1, i) for i in range(ends)])
        found["rows"] = edge_rows(
            found["map"], from_last, from_next, images, height, breadth, rim, after
        )
        return found["rows"]

    def rest(after):
        grad_rows = found["rows"]
        grad_map = grad_rows[:, 1 : height + 1]
        grad_conv_bias = jnp.sum(grad_map.astype(jnp.float32), axis=(0, 1, 2))
        grad_map_padded = jnp.pad(grad_rows, column_pad)
        grad_taps, grad_lateral_full = convolve_back(
            grad_map_padded, lateral_padded, grad_map, kernel_taps, height, breadth
        )
        grad_lateral = grad_lateral_full.astype(jnp.bfloat16)
        grad_lateral_w = jnp.einsum(
            "ihwc,ihwd->cd", features, grad_lateral, preferred_element_type=jnp.float32
        )
        grad_lateral_bias = jnp.sum(grad_lateral.astype(jnp.float32), axis=(0, 1, 2))
        misc = jnp.concatenate(
            [grad_lateral_bias, grad_conv_bias]
            + section_bias_grads
            + [loss_part[None], jnp.sum(valid_float)[None]]
        )
        filled = -(-misc.size // 1024) * 1024
        misc = jnp.pad(misc, (0, filled - misc.size)).reshape(-1, 128)
        heads = jnp.stack(head_grads).reshape(-1, out_width)
        found["sums"] = sum_everywhere(
            [grad_lateral_w, grad_taps], [heads], misc, after, n_img, n_tile
        )
        return found["sums"][-1]

    events, start = {}, 0
    for at, count in TURNS_AT.items():
        events[at] = turns_of(start, start + count)
        start += count
    events[EDGES_AT] = edges
    events[REST_AT] = rest
    block_terms = sum_parts(parts[0::2], parts[1::2], orders, events)

    conv_sum = jnp.concatenate(found["sums"][:2], axis=0)
    head_sum = found["sums"][2].reshape(section_count, hidden, out_width)
    misc_sum = found["sums"][3].reshape(-1)
    biases = bias_vector.shape[0]
    bias_sum, loss_total, valid_sum = misc_sum[:biases], misc_sum[biases], misc_sum[biases + 1]
    scale = 1.0 / valid_sum
    mine = lax.dynamic_slice_in_dim(slot_block, (at_img * n_tile + at_tile) * slots, slots)
    held, old, start = mine, None, 0
    for part, share in zip(block_terms, shares):
        old = finish_blocks(
            part, start, share, block_master, block_first, block_second, held, scale[None], old
        )
        start += share
    block_new, block_first_new, block_second_new = old
    step = float(STEP)
    conv_new, conv_first_new, conv_second_new = adamw(
        conv_weight, conv_first, conv_second, conv_sum * scale, step
    )
    head_new, head_first_new, head_second_new = adamw(
        head_weight, head_first, head_second, head_sum * scale, step
    )
    bias_new, bias_first_new, bias_second_new = adamw(
        bias_vector, bias_first, bias_second, bias_sum * scale, step
    )
    loss = (loss_total * scale).reshape(1)
    return (
        loss,
        conv_new,
        conv_first_new,
        conv_second_new,
        head_new,
        head_first_new,
        head_second_new,
        bias_new,
        bias_first_new,
        bias_second_new,
        block_new,
        block_first_new,
        block_second_new,
    )


def solution(mesh):
    split = P(AXES, None, None)
    return jax.shard_map(
        on_device,
        mesh=mesh,
        in_specs=(
            P("img", "tile", None, None),
            P(), P(), P(), P(), P(), P(), P(), P(), P(),
            split, split, split,
            P(),
            P(AXES),
            P(None, None, AXES),
            P(None, None, None, AXES),
            P(None, AXES),
            P(AXES),
            P(None, None, AXES),
        ),
        out_specs=(P(),) * 10 + (split,) * 3,
        check_vma=False,
    )
```

```python
import math

import jax
import jax.numpy as jnp
from jax import lax
from jax.experimental import pallas as pl
from jax.experimental.pallas import tpu as pltpu
from jax.sharding import PartitionSpec as P

HR = 2
STEP = 5
BINS = 49
POOL = 7

BETA_ONE = 0.9
BETA_TWO = 0.999
RATE = 0.025
DECAY = 0.01
EPSILON = 1e-08

VMEM_LIMIT = 56 * 1024 * 1024
AXES = ("img", "tile")


def padded_2(cells, sides, width):
    for axis, dim in sides:
        count = lax.axis_size(axis)
        ends = count - 1
        head = lax.slice_in_dim(cells, 0, width, axis=dim)
        tail = lax.slice_in_dim(cells, cells.shape[dim] - width, cells.shape[dim], axis=dim)
        cells = jnp.concatenate(
            [
                lax.ppermute(tail, axis, [(i, (i + 1) % count) for i in range(ends)]),
                cells,
                lax.ppermute(head, axis, [((i + 1) % count, i) for i in range(ends)]),
            ],
            axis=dim,
        )
    return cells


def adamw(master, first, second, grad, step):
    first_new = BETA_ONE * first + (1.0 - BETA_ONE) * grad
    second_new = BETA_TWO * second + (1.0 - BETA_TWO) * grad * grad
    first_hat = first_new / (1.0 - BETA_ONE**step)
    second_hat = second_new / (1.0 - BETA_TWO**step)
    master_new = master - RATE * (first_hat / (jnp.sqrt(second_hat) + EPSILON) + DECAY * master)
    return (master_new, first_new, second_new)


def silu_slope(value):
    sigmoid = jax.nn.sigmoid(value)
    return sigmoid * (1.0 + value * (1.0 - sigmoid))


def convolve(padded, kernel_taps, height, breadth):
    summed = None
    for kernel_pos in range(9):
        row_shift = kernel_pos // 3
        col_shift = kernel_pos % 3
        window = padded[:, row_shift : row_shift + height, col_shift : col_shift + breadth]
        contrib = jnp.einsum(
            "ihwc,cd->ihwd", window, kernel_taps[kernel_pos], preferred_element_type=jnp.float32
        )
        summed = contrib if summed is None else summed + contrib
    return summed


def convolve_back(grad_padded, lateral_padded, grad_low, kernel_taps, height, breadth):
    grad_input = None
    tap_grads = []
    for kernel_pos in range(9):
        row_shift = kernel_pos // 3
        col_shift = kernel_pos % 3
        window = lateral_padded[:, row_shift : row_shift + height, col_shift : col_shift + breadth]
        tap_grads.append(
            jnp.einsum("ihwc,ihwd->cd", window, grad_low, preferred_element_type=jnp.float32)
        )
        source = grad_padded[
            :, 2 - row_shift : 2 - row_shift + height, 2 - col_shift : 2 - col_shift + breadth
        ]
        contrib = jnp.einsum(
            "ihwd,cd->ihwc", source, kernel_taps[kernel_pos], preferred_element_type=jnp.float32
        )
        grad_input = contrib if grad_input is None else grad_input + contrib
    return (jnp.concatenate(tap_grads, axis=0), grad_input)


def column_weights(column, frac, breadth):
    regions = column.shape[1]
    away = lax.broadcasted_iota(jnp.int32, (breadth, regions), 0) - column
    return jnp.where(away == 0, 1.0 - frac, jnp.where(away == 1, frac, 0.0))


def row_weight(row, frac, at):
    away = at - row
    return jnp.where(away == 0, 1.0 - frac, jnp.where(away == 1, frac, 0.0))


def pool_regions(map_t, rows, cols, fracs_row, fracs_col, breadth):
    section_count, bins, regions = rows.shape
    channels, cells = map_t.shape
    lines = cells // breadth
    group = POOL
    chunk = 8

    def body(map_ref, row_ref, col_ref, fr_ref, fc_ref, out_ref):
        turn = pl.program_id(1)

        def one_bin(b, carry):
            p = turn * group + b
            row = row_ref[0, pl.ds(p, 1), :]
            col = col_ref[0, pl.ds(p, 1), :]
            frow = fr_ref[0, pl.ds(p, 1), :]
            fcol = fc_ref[0, pl.ds(p, 1), :]
            across = column_weights(col, fcol, breadth)
            total = None
            for first in range(0, lines, chunk):
                weights = jnp.concatenate(
                    [
                        (across * row_weight(row, frow, line)).astype(jnp.bfloat16)
                        for line in range(first, first + chunk)
                    ],
                    axis=0,
                )
                part = jnp.dot(
                    map_ref[:, first * breadth : (first + chunk) * breadth],
                    weights,
                    preferred_element_type=jnp.float32,
                )
                total = part if total is None else total + part
            out_ref[0, b] = total.astype(jnp.bfloat16)
            return carry

        lax.fori_loop(0, group, one_bin, 0)

    samples = pl.BlockSpec((1, bins, regions), lambda u, t: (u, 0, 0))
    return pl.pallas_call(
        body,
        grid=(section_count, bins // group),
        in_specs=[pl.BlockSpec((channels, cells), lambda u, t: (0, 0))] + [samples] * 4,
        out_specs=pl.BlockSpec((1, group, channels, regions), lambda u, t: (u, t, 0, 0)),
        out_shape=jax.ShapeDtypeStruct((section_count, bins, channels, regions), jnp.bfloat16),
        compiler_params=pltpu.CompilerParams(vmem_limit_bytes=VMEM_LIMIT),
        cost_estimate=pl.CostEstimate(
            flops=2 * section_count * bins * regions * cells * channels,
            bytes_accessed=section_count * bins * regions * channels * 2,
            transcendentals=0,
        ),
        name="pool_regions",
    )(map_t, rows, cols, fracs_row, fracs_col)


def fetch_blocks(table, blocks_ref, buffer, sem, base, slot, count, block_rows):
    def one(b, carry):
        pltpu.make_async_copy(
            blocks_ref.at[table[base + b]],
            buffer.at[slot, pl.ds(pl.multiple_of(b * block_rows, block_rows), block_rows)],
            sem.at[slot],
        ).start()
        return carry

    lax.fori_loop(0, count, one, 0, unroll=8)


def first_layer(table, blocks, feats_t, section_blocks):
    section_count, bins, channels, regions = feats_t.shape
    _, block_rows, hidden = blocks.shape
    group = POOL
    turns = bins // group
    per_bin = channels // block_rows
    count = group * per_bin

    def body(table_ref, blocks_ref, x_ref, out_ref, buffer, sem):
        u, t = pl.program_id(0), pl.program_id(1)
        step = u * turns + t
        slot = lax.rem(step, 2)

        def fetch(at, into):
            base = (at // turns) * section_blocks + lax.rem(at, turns) * count
            fetch_blocks(table_ref, blocks_ref, buffer, sem, base, into, count, block_rows)

        @pl.when(step == 0)
        def _():
            fetch(step, slot)

        @pl.when(step + 1 < section_count * turns)
        def _():
            fetch(step + 1, 1 - slot)

        pltpu.make_async_copy(buffer.at[slot], buffer.at[slot], sem.at[slot]).wait()

        @pl.when(t == 0)
        def _():
            out_ref[...] = jnp.zeros_like(out_ref)

        out_ref[0] += lax.dot_general(
            x_ref[0].reshape(group * channels, regions),
            buffer[slot],
            (((0,), (0,)), ((), ())),
            preferred_element_type=jnp.float32,
        )

    return pl.pallas_call(
        body,
        grid_spec=pltpu.PrefetchScalarGridSpec(
            num_scalar_prefetch=1,
            grid=(section_count, turns),
            in_specs=[
                pl.BlockSpec(memory_space=pl.ANY),
                pl.BlockSpec((1, group, channels, regions), lambda u, t, _: (u, t, 0, 0)),
            ],
            out_specs=pl.BlockSpec((1, regions, hidden), lambda u, t, _: (u, 0, 0)),
            scratch_shapes=[
                pltpu.VMEM((2, count * block_rows, hidden), jnp.bfloat16),
                pltpu.SemaphoreType.DMA((2,)),
            ],
        ),
        out_shape=jax.ShapeDtypeStruct((section_count, regions, hidden), jnp.float32),
        compiler_params=pltpu.CompilerParams(vmem_limit_bytes=VMEM_LIMIT),
        cost_estimate=pl.CostEstimate(
            flops=2 * section_count * bins * regions * channels * hidden,
            bytes_accessed=section_count * bins * channels * (regions + hidden) * 2,
            transcendentals=0,
        ),
        name="first_layer",
    )(table, blocks, feats_t)


def weight_grads(order, place, offsets, feats_t, acts_t, grads_first, grads_second, sizes):
    section_count, bins, channels, regions = feats_t.shape
    hidden = grads_first.shape[2]
    block_rows = sizes[0][1]
    group = POOL
    turns = bins // group + 1
    rows = group * channels
    wide = acts_t.shape[1]
    steps = section_count * turns
    kinds = len(sizes)

    def body(order_ref, place_ref, offset_ref, x_ref, a_ref, gf_ref, gs_ref, *rest):
        outs, (buffer, sem) = rest[:kinds], rest[kinds:]
        u, t = pl.program_id(0), pl.program_id(1)
        step = u * turns + t
        slot = lax.rem(step, 2)

        def drain(at, into):
            last = lax.rem(at, turns) == turns - 1

            @pl.when(last)
            def _():
                half = buffer.at[into, pl.ds(0, wide)]
                pltpu.make_async_copy(half, half, sem.at[into]).wait()

            @pl.when(jnp.logical_not(last))
            def _():
                pltpu.make_async_copy(buffer.at[into], buffer.at[into], sem.at[into]).wait()

        @pl.when(step >= 2)
        def _():
            drain(step - 2, slot)

        @pl.when(t < turns - 1)
        def _():
            buffer[slot] = jnp.dot(
                x_ref[0].reshape(rows, regions), gf_ref[0], preferred_element_type=jnp.float32
            ).astype(jnp.bfloat16)

        @pl.when(t == turns - 1)
        def _():
            buffer[slot, 0:wide] = jnp.dot(
                a_ref[0], gs_ref[0], preferred_element_type=jnp.float32
            ).astype(jnp.bfloat16)

        for kind in range(kinds):

            def one(i, carry, kind=kind):
                at = pl.ds(pl.multiple_of(order_ref[i] * block_rows, block_rows), block_rows)
                pltpu.make_async_copy(
                    buffer.at[slot, at], outs[kind].at[place_ref[i]], sem.at[slot]
                ).start()
                return carry

            lax.fori_loop(
                offset_ref[step * kinds + kind], offset_ref[step * kinds + kind + 1], one, 0
            )

        @pl.when(step == steps - 1)
        def _():
            drain(step - 1, 1 - slot)
            drain(step, slot)

    return pl.pallas_call(
        body,
        grid_spec=pltpu.PrefetchScalarGridSpec(
            num_scalar_prefetch=3,
            grid=(section_count, turns),
            in_specs=[
                pl.BlockSpec(
                    (1, group, channels, regions),
                    lambda u, t, *_: (u, jnp.minimum(t, turns - 2), 0, 0),
                ),
                pl.BlockSpec((1, wide, regions), lambda u, t, *_: (u, 0, 0)),
                pl.BlockSpec((1, regions, hidden), lambda u, t, *_: (u, 0, 0)),
                pl.BlockSpec((1, regions, hidden), lambda u, t, *_: (u, 0, 0)),
            ],
            out_specs=[pl.BlockSpec(memory_space=pl.ANY)] * kinds,
            scratch_shapes=[
                pltpu.VMEM((2, rows, hidden), jnp.bfloat16),
                pltpu.SemaphoreType.DMA((2,)),
            ],
        ),
        out_shape=[jax.ShapeDtypeStruct(size, jnp.bfloat16) for size in sizes],
        compiler_params=pltpu.CompilerParams(vmem_limit_bytes=VMEM_LIMIT),
        cost_estimate=pl.CostEstimate(
            flops=2 * section_count * regions * (bins * channels + wide) * hidden,
            bytes_accessed=section_count * (bins * channels + wide) * (regions + hidden) * 2,
            transcendentals=0,
        ),
        name="weight_grads",
    )(order, place, offsets, feats_t, acts_t, grads_first, grads_second)


def map_grads(before, span, table, blocks, grads_first, rows, cols, fracs_row, fracs_col, section_blocks, lines, breadth, after):
    section_count, bins, regions = rows.shape
    _, block_rows, hidden = blocks.shape
    cells, channels = before.shape
    group = POOL
    chunk = 8
    turns = bins // group
    count = group * channels // block_rows
    start, stop = span

    def body(table_ref, blocks_ref, g_ref, row_ref, col_ref, fr_ref, fc_ref, old_ref, after_ref, out_ref, buffer, sem, pooled, across, down, weights_a, weights_b):
        del after_ref
        step = start + pl.program_id(0)
        slot = lax.rem(step, 2)
        t = lax.rem(step, turns)

        def fetch(at, into):
            base = (at // turns) * section_blocks + lax.rem(at, turns) * count
            fetch_blocks(table_ref, blocks_ref, buffer, sem, base, into, count, block_rows)

        @pl.when(step == start)
        def _():
            fetch(step, slot)
            out_ref[...] = old_ref[...]

        @pl.when(step + 1 < stop)
        def _():
            fetch(step + 1, 1 - slot)

        pltpu.make_async_copy(buffer.at[slot], buffer.at[slot], sem.at[slot]).wait()

        grads = lax.dot_general(
            g_ref[0], buffer[slot], (((1,), (1,)), ((), ())), preferred_element_type=jnp.float32
        )
        for b in range(group):
            pooled[b * regions : (b + 1) * regions] = grads[
                :, b * channels : (b + 1) * channels
            ].astype(jnp.bfloat16)

        def one_bin(b, carry):
            p = t * group + b
            here = pl.ds(pl.multiple_of(b * regions, regions), regions)
            across[:, here] = column_weights(
                col_ref[0, pl.ds(p, 1), :], fc_ref[0, pl.ds(p, 1), :], breadth
            ).astype(jnp.bfloat16)
            row = row_ref[0, pl.ds(p, 1), :]
            frow = fr_ref[0, pl.ds(p, 1), :]
            at_line = lax.broadcasted_iota(jnp.int32, (lines, regions), 0)
            down[:, here] = row_weight(row, frow, at_line)
            return carry

        lax.fori_loop(0, group, one_bin, 0)

        def build(first, into):
            for i in range(chunk):
                into[i * breadth : (i + 1) * breadth] = across[...] * down[
                    first + i : first + i + 1, :
                ].astype(jnp.bfloat16)

        stores = (weights_a, weights_b)
        build(0, stores[0])
        for turn in range(lines // chunk):
            if turn + 1 < lines // chunk:
                build((turn + 1) * chunk, stores[(turn + 1) % 2])
            at = slice(turn * chunk * breadth, (turn + 1) * chunk * breadth)
            out_ref[at] += jnp.dot(
                stores[turn % 2][...], pooled[...], preferred_element_type=jnp.float32
            )

    samples = pl.BlockSpec((1, bins, regions), lambda i, _: ((start + i) // turns, 0, 0))
    whole = pl.BlockSpec((cells, channels), lambda i, _: (0, 0))
    return pl.pallas_call(
        body,
        grid_spec=pltpu.PrefetchScalarGridSpec(
            num_scalar_prefetch=1,
            grid=(stop - start,),
            in_specs=[
                pl.BlockSpec(memory_space=pl.ANY),
                pl.BlockSpec((1, regions, hidden), lambda i, _: ((start + i) // turns, 0, 0)),
            ]
            + [samples] * 4
            + [whole, pl.BlockSpec(memory_space=pl.ANY)],
            out_specs=whole,
            scratch_shapes=[
                pltpu.VMEM((2, count * block_rows, hidden), jnp.bfloat16),
                pltpu.SemaphoreType.DMA((2,)),
                pltpu.VMEM((group * regions, channels), jnp.bfloat16),
                pltpu.VMEM((breadth, group * regions), jnp.bfloat16),
                pltpu.VMEM((lines, group * regions), jnp.float32),
                pltpu.VMEM((chunk * breadth, group * regions), jnp.bfloat16),
                pltpu.VMEM((chunk * breadth, group * regions), jnp.bfloat16),
            ],
        ),
        out_shape=jax.ShapeDtypeStruct((cells, channels), jnp.float32),
        compiler_params=pltpu.CompilerParams(vmem_limit_bytes=VMEM_LIMIT),
        cost_estimate=pl.CostEstimate(
            flops=2 * (stop - start) * group * regions * channels * (hidden + cells),
            bytes_accessed=(stop - start) * count * block_rows * hidden * 2,
            transcendentals=0,
        ),
        name="map_grads",
    )(table, blocks, grads_first, rows, cols, fracs_row, fracs_col, before, after)


def sum_blocks(terms, half, after):
    _, block_rows, hidden = terms[0].shape
    batch = max(b for b in range(1, 17) if half % b == 0)
    count = len(terms)

    def body(*refs):
        total = None
        for ref in refs[:count]:
            value = ref[...].astype(jnp.float32)
            total = value if total is None else total + value
        refs[-1][...] = total.astype(jnp.bfloat16)

    return pl.pallas_call(
        body,
        grid=(half // batch,),
        in_specs=[
            pl.BlockSpec((batch, block_rows, hidden), lambda i: (i + half // batch, 0, 0))
        ] * count
        + [pl.BlockSpec(memory_space=pl.ANY)],
        out_specs=pl.BlockSpec((batch, block_rows, hidden), lambda i: (i, 0, 0)),
        out_shape=jax.ShapeDtypeStruct((half, block_rows, hidden), jnp.bfloat16),
        compiler_params=pltpu.CompilerParams(vmem_limit_bytes=VMEM_LIMIT),
        cost_estimate=pl.CostEstimate(
            flops=half * block_rows * hidden * count,
            bytes_accessed=half * block_rows * hidden * 2 * (count + 1),
            transcendentals=0,
        ),
        name="sum_blocks",
    )(*terms, after)


def bits_of(count):
    return list(range(count.bit_length() - 1))


PARTS = ((6, "zwxy"), (8, "yxzw"), (10, "xzyw"), (10, "yxzw"), (6, "zwxy"))
TURNS_AT = {0: 5, 5: 7, 7: 3, 8: 6}
EDGES_AT = 12


def part_orders(n_img, n_tile):
    bits = {
        "x": [("tile", b) for b in bits_of(n_tile)[:1]],
        "y": [("img", b) for b in bits_of(n_img)[1:]],
        "z": [("tile", b) for b in bits_of(n_tile)[1:2]],
        "w": [("tile", b) for b in bits_of(n_tile)[2:]],
    }
    return [[place for letter in order for place in bits[letter]] for _, order in PARTS]


def part_sizes(slots):
    total = sum(share for share, _ in PARTS)
    ends, done = [0], 0
    for share, _ in PARTS:
        done += share
        ends.append((done * slots + total // 2) // total)
    return [b - a for a, b in zip(ends, ends[1:])]


def swap(values, axis, bit):
    count = lax.axis_size(axis)
    return lax.ppermute(values, axis, [(i, i ^ (1 << bit)) for i in range(count)])


GATHER_FIRST = 12
STREAMS = ((11, "wzyx"), (10, "wzxy"), (7, "xywz"))


def gather_plan(slots, n_img, n_tile):
    if n_img * n_tile > 64:
        return slots, []
    first = GATHER_FIRST * slots // 40
    bits = {
        "x": [("tile", b) for b in bits_of(n_tile)[:1]],
        "y": [("img", b) for b in bits_of(n_img)[1:]],
        "z": [("tile", b) for b in bits_of(n_tile)[1:2]],
        "w": [("tile", b) for b in bits_of(n_tile)[2:]],
    }
    total = sum(share for share, _ in STREAMS)
    streams, done, start = [], 0, first
    for share, order in STREAMS:
        done += share
        end = first + ((slots - first) * done + total // 2) // total
        places = [place for letter in order for place in bits[letter]] + [("img", 0)]
        if end > start:
            streams.append((start, end - start, places))
        start = end
    return first, streams


def gather_blocks(own, gathered, first, streams, n_img, n_tile, after):
    slots, block_rows, hidden = own.shape
    devices = n_img * n_tile
    stages = len(streams[0][2])
    pieces = devices - 1

    def body(own_ref, part_ref, after_ref, out_ref, held, send, recv, local, taken, given):
        del after_ref
        place = {"img": lax.axis_index("img"), "tile": lax.axis_index("tile")}

        def partner(axis, step):
            here = place[axis]
            there = dict(place)
            there[axis] = here + step - 2 * step * ((here // step) % 2)
            return (there["img"], there["tile"])

        barrier = pltpu.get_barrier_semaphore()
        for axis, bit in streams[0][2]:
            pl.semaphore_signal(
                barrier,
                inc=1,
                device_id=partner(axis, 1 << bit),
                device_id_type=pl.DeviceIdType.MESH,
            )
        pl.semaphore_wait(barrier, stages)
        copies = {}

        def send_piece(s, k, p):
            start, share, places = streams[s]
            base = start * devices
            source = (
                own_ref.at[pl.ds(start, share)]
                if p == 0
                else out_ref.at[pl.ds(base + p * share, share)]
            )
            q = (1 << k) + p
            axis, bit = places[k]
            copy = pltpu.make_async_remote_copy(
                src_ref=source,
                dst_ref=out_ref.at[pl.ds(base + q * share, share)],
                send_sem=send.at[s, q - 1],
                recv_sem=recv.at[s, q - 1],
                device_id=partner(axis, 1 << bit),
                device_id_type=pl.DeviceIdType.MESH,
            )
            copy.start()
            copies[s, q] = copy

        for k in range(stages):
            for s in range(len(streams)):
                send_piece(s, k, 0)
        moves = []
        for s, (start, share, _) in enumerate(streams):
            moves.append(
                pltpu.make_async_copy(
                    own_ref.at[pl.ds(start, share)],
                    out_ref.at[pl.ds(start * devices, share)],
                    local.at[s],
                )
            )
        for move in moves:
            move.start()

        def chunk(ref, c):
            return ref.at[pl.ds(c * devices, devices)]

        depth = held.shape[0]
        take = [
            pltpu.make_async_copy(chunk(part_ref, c), held.at[c % depth], taken.at[c % depth])
            for c in range(first)
        ]
        give = [
            pltpu.make_async_copy(held.at[c % depth], chunk(out_ref, c), given.at[c % depth])
            for c in range(first)
        ]
        for c in range(min(depth, first)):
            take[c].start()
        for c in range(first):
            take[c].wait()
            give[c].start()
            if c >= 2 and c - 2 + depth < first:
                give[c - 2].wait()
                take[c - 2 + depth].start()
        for c in range(first):
            if c + depth >= first:
                give[c].wait()

        for q in range(1, devices):
            for s in range(len(streams)):
                copies[s, q].wait_recv()
                for k in range(q.bit_length(), stages):
                    send_piece(s, k, q)
        for q in range(1, devices):
            for s in range(len(streams)):
                copies[s, q].wait_send()
        for move in moves:
            move.wait()

    anywhere = pl.BlockSpec(memory_space=pl.ANY)
    return pl.pallas_call(
        body,
        in_specs=[anywhere] * 3,
        out_specs=anywhere,
        out_shape=jax.ShapeDtypeStruct((slots * devices, block_rows, hidden), jnp.bfloat16),
        scratch_shapes=[
            pltpu.VMEM((4, devices, block_rows, hidden), jnp.bfloat16),
            pltpu.SemaphoreType.DMA((len(streams), pieces)),
            pltpu.SemaphoreType.DMA((len(streams), pieces)),
            pltpu.SemaphoreType.DMA((len(streams),)),
            pltpu.SemaphoreType.DMA((4,)),
            pltpu.SemaphoreType.DMA((4,)),
        ],
        compiler_params=pltpu.CompilerParams(
            collective_id=1, has_side_effects=True, vmem_limit_bytes=VMEM_LIMIT
        ),
        name="gather_blocks",
    )(own, gathered, after)


def sum_parts(kept, sent, orders, events):
    terms = [[k, swap(s, "img", 0)] for k, s in zip(kept, sent)]
    sums = [(stage, i) for stage in range(len(orders[0])) for i in range(len(orders))]
    last = kept[0]
    for at, (stage, i) in enumerate(sums):
        if at in events:
            last = events[at](last)
        half = terms[i][-1].shape[0] // 2
        last = sum_blocks(terms[i], half, last)
        terms[i].append(swap(last, *orders[i][stage]))
    events["end"](last)
    return terms


def sum_everywhere(wide, narrow, exact, after, n_img, n_tile):
    x = [("tile", 1)]
    y = [("img", 1 << b) for b in bits_of(n_img)[1:]]
    z = [("tile", 1 << b) for b in bits_of(n_tile)[1:]]
    pair = [("img", 1)]
    orders = [pair + x + y + z, pair + y + z + x, pair + z + x + y]
    stages = len(orders[0])
    lanes = 128
    placed, rows = [], 0
    for i, array in enumerate(wide):
        for half in range(2):
            placed.append((i, half, rows, array.shape[0], lanes))
            rows += array.shape[0]
    for i, array in enumerate(narrow):
        placed.append((len(wide) + i, 0, rows, array.shape[0], array.shape[1]))
        rows += array.shape[0]
    unit = 16 * n_img * n_tile
    units = -(-rows // unit)
    streams, first = [], 0
    for i, order in enumerate(orders):
        size = (units + len(orders) - 1 - i) // len(orders) * unit
        if size:
            streams.append((order, first, size, True))
            first += size
    filled = first
    count = exact.shape[0]
    small = -(-count // (8 * n_img * n_tile)) * 8 * n_img * n_tile
    streams.append((orders[0], 0, small, False))
    operands = list(wide) + list(narrow) + [exact]
    number = len(operands)

    def body(*refs):
        inputs = refs[:number]
        (out_low, out_exact, total, going, landing, total_exact, landing_exact) = refs[
            number + 1 : number + 8
        ]
        send, recv, send_back, recv_back = refs[number + 8 :]
        place = {"img": lax.axis_index("img"), "tile": lax.axis_index("tile")}

        def partner(axis, step):
            here = place[axis]
            bit = (here // step) % 2
            there = dict(place)
            there[axis] = here + step - 2 * step * bit
            return bit, (there["img"], there["tile"])

        barrier = pltpu.get_barrier_semaphore()
        for axis, step in orders[0]:
            _, there = partner(axis, step)
            pl.semaphore_signal(
                barrier, inc=1, device_id=there, device_id_type=pl.DeviceIdType.MESH
            )
        for i, half, first, size, columns in placed:
            if columns < lanes:
                total[first : first + size] = jnp.zeros((size, lanes), jnp.float32)
            total[first : first + size, :columns] = inputs[i][
                :, half * lanes : half * lanes + columns
            ]
        if rows < filled:
            total[rows:] = jnp.zeros((filled - rows, lanes), jnp.float32)
        total_exact[...] = jnp.zeros_like(total_exact)
        total_exact[0:count] = inputs[-1][...]
        pl.semaphore_wait(barrier, stages)

        start = [first for _, first, _, _ in streams]
        copies = {}

        def rows_at(first, size):
            return pl.ds(pl.multiple_of(first, min(size, 16)), size)

        def remote(source, target, there, sent, received):
            copy = pltpu.make_async_remote_copy(
                src_ref=source,
                dst_ref=target,
                send_sem=sent,
                recv_sem=received,
                device_id=there,
                device_id_type=pl.DeviceIdType.MESH,
            )
            copy.start()
            return copy

        def send_half(s, k):
            order, first, size, low = streams[s]
            half = size >> (k + 1)
            bit, there = partner(*order[k])
            away = rows_at(start[s] + (1 - bit) * half, half)
            landed = pl.ds(first + size - 2 * half, half)
            if low:
                going[away] = total[away].astype(jnp.bfloat16)
                source, target = going.at[away], landing.at[landed]
            else:
                source, target = total_exact.at[away], landing_exact.at[landed]
            copies[s, k] = remote(source, target, there, send.at[s, k], recv.at[s, k])

        for s in range(len(streams)):
            send_half(s, 0)
        for k in range(stages):
            for s, (order, first, size, low) in enumerate(streams):
                half = size >> (k + 1)
                bit, _ = partner(*order[k])
                copies[s, k].wait()
                keep = rows_at(start[s] + bit * half, half)
                landed = pl.ds(first + size - 2 * half, half)
                if low:
                    value = total[keep] + landing[landed].astype(jnp.float32)
                    if k == stages - 1:
                        out_low[keep] = value.astype(jnp.bfloat16)
                    else:
                        total[keep] = value
                else:
                    target = out_exact if k == stages - 1 else total_exact
                    target[keep] = total_exact[keep] + landing_exact[landed]
                start[s] = start[s] + bit * half
                if k + 1 < stages:
                    send_half(s, k + 1)

        def send_back_half(s, k):
            order, _, size, low = streams[s]
            half = size >> (k + 1)
            _, there = partner(*order[k])
            at = rows_at(start[s], half)
            out = out_low if low else out_exact
            copies[s, k] = remote(
                out.at[at], out.at[at], there, send_back.at[s, k], recv_back.at[s, k]
            )

        for s in range(len(streams)):
            send_back_half(s, stages - 1)
        for k in reversed(range(stages)):
            for s, (order, _, size, _) in enumerate(streams):
                half = size >> (k + 1)
                bit, _ = partner(*order[k])
                copies[s, k].wait()
                start[s] = start[s] - bit * half
                if k > 0:
                    send_back_half(s, k - 1)

    whole = pl.BlockSpec(memory_space=pltpu.VMEM)
    low, high = pl.pallas_call(
        body,
        in_specs=[whole] * number + [pl.BlockSpec(memory_space=pl.ANY)],
        out_specs=[whole, whole],
        out_shape=[
            jax.ShapeDtypeStruct((filled, lanes), jnp.bfloat16),
            jax.ShapeDtypeStruct((small, lanes), jnp.float32),
        ],
        scratch_shapes=[
            pltpu.VMEM((filled, lanes), jnp.float32),
            pltpu.VMEM((filled, lanes), jnp.bfloat16),
            pltpu.VMEM((filled, lanes), jnp.bfloat16),
            pltpu.VMEM((small, lanes), jnp.float32),
            pltpu.VMEM((small, lanes), jnp.float32),
        ]
        + [pltpu.SemaphoreType.DMA((len(streams), stages))] * 4,
        compiler_params=pltpu.CompilerParams(
            collective_id=0, has_side_effects=True, vmem_limit_bytes=VMEM_LIMIT
        ),
        name="sum_everywhere",
    )(*operands, after)
    results, at = [], 0
    for array in wide:
        size = array.shape[0]
        results.append(
            jnp.concatenate([low[at : at + size], low[at + size : at + 2 * size]], axis=1).astype(
                jnp.float32
            )
        )
        at += 2 * size
    for array in narrow:
        results.append(low[at : at + array.shape[0], : array.shape[1]].astype(jnp.float32))
        at += array.shape[0]
    return results + [high[:count]]


def edge_rows(grad_flat, from_last, from_next, images, height, breadth, rim, after):
    channels = grad_flat.shape[1]
    padded = height + 2 * rim
    low, high = from_last.astype(jnp.bfloat16), from_next.astype(jnp.bfloat16)

    def body(own_ref, last_ref, next_ref, after_ref, out_ref):
        del after_ref
        for i in range(images):
            for r in range(height + 2):
                line = r + rim - 1
                at = (i * padded + line) * breadth
                value = own_ref[at : at + breadth]
                if r < rim + 1:
                    value = value + last_ref[i, r].astype(jnp.float32)
                if r >= height + 1 - rim:
                    value = value + next_ref[i, r - (height + 1 - rim)].astype(jnp.float32)
                out_ref[i, r] = value.astype(jnp.bfloat16)

    whole = pl.BlockSpec(memory_space=pltpu.VMEM)
    return pl.pallas_call(
        body,
        in_specs=[whole] * 3 + [pl.BlockSpec(memory_space=pl.ANY)],
        out_specs=whole,
        out_shape=jax.ShapeDtypeStruct((images, height + 2, breadth, channels), jnp.bfloat16),
        compiler_params=pltpu.CompilerParams(vmem_limit_bytes=VMEM_LIMIT),
        name="edge_rows",
    )(grad_flat, low, high, after)


def finish_blocks(terms, start, share, masters, firsts, seconds, held, scale, old):
    slots, block_rows, hidden = masters.shape
    count = len(terms)
    batch = math.gcd(math.gcd(start, share), 2)
    correct_one = 1.0 - BETA_ONE ** float(STEP)
    correct_two = 1.0 - BETA_TWO ** float(STEP)

    def body(held_ref, scale_ref, *refs):
        total = None
        for ref in refs[:count]:
            value = ref[...].astype(jnp.float32)
            total = value if total is None else total + value
        w_ref, m_ref, v_ref = refs[count : count + 3]
        outs = refs[-3:]
        place = start + pl.program_id(0) * batch
        total = total * scale_ref[0]
        grad = jnp.concatenate(
            [jnp.where(held_ref[place + i] >= 0, total[i : i + 1], 0.0) for i in range(batch)],
            axis=0,
        )
        first_new = BETA_ONE * m_ref[...] + (1.0 - BETA_ONE) * grad
        second_new = BETA_TWO * v_ref[...] + (1.0 - BETA_TWO) * grad * grad
        rooted = jnp.sqrt(second_new * (1.0 / correct_two)) + EPSILON
        outs[0][...] = w_ref[...] - RATE * (
            first_new * (1.0 / correct_one) / rooted + DECAY * w_ref[...]
        )
        outs[1][...] = first_new
        outs[2][...] = second_new

    term = pl.BlockSpec((batch, block_rows, hidden), lambda i: (i, 0, 0))
    slot = pl.BlockSpec((batch, block_rows, hidden), lambda i: (start // batch + i, 0, 0))
    smem = pl.BlockSpec(memory_space=pltpu.SMEM)
    kept = [] if old is None else list(old)
    inputs = [held, scale] + list(terms) + [masters, firsts, seconds] + kept
    return pl.pallas_call(
        body,
        grid=(share // batch,),
        in_specs=[smem, smem]
        + [term] * count
        + [slot] * 3
        + [pl.BlockSpec(memory_space=pl.ANY)] * len(kept),
        out_specs=[slot] * 3,
        out_shape=[jax.ShapeDtypeStruct(masters.shape, jnp.float32)] * 3,
        input_output_aliases={len(inputs) - 3 + j: j for j in range(len(kept))},
        compiler_params=pltpu.CompilerParams(vmem_limit_bytes=VMEM_LIMIT),
        name="finish_blocks",
    )(*inputs)


def on_device(
    features,
    conv_weight,
    conv_first,
    conv_second,
    head_weight,
    head_first,
    head_second,
    bias_vector,
    bias_first,
    bias_second,
    block_master,
    block_first,
    block_second,
    slot_block,
    roi_image,
    corner_index,
    corner_frac,
    labels,
    valid,
    box_deltas,
):
    images, height, breadth, in_channels = features.shape
    channels = conv_weight.shape[1]
    section_count, hidden, out_width = head_weight.shape
    classes = out_width - 4
    slots, block_rows, _ = block_master.shape
    all_slots = slot_block.shape[0]
    rim = HR
    first_rows = BINS * channels
    section_rows = first_rows + hidden
    section_blocks = section_rows // block_rows
    first_blocks = first_rows // block_rows
    block_total = section_count * section_blocks
    n_img, n_tile = lax.axis_size("img"), lax.axis_size("tile")
    at_img, at_tile = lax.axis_index("img"), lax.axis_index("tile")

    own_blocks = block_master.astype(jnp.bfloat16)
    go_first, streams = gather_plan(slots, n_img, n_tile)
    gathered = lax.all_gather(own_blocks[:go_first], AXES, axis=0, tiled=True)
    position = jnp.arange(all_slots, dtype=jnp.int32)
    owner_slot = (
        jnp.zeros((block_total,), jnp.int32)
        .at[jnp.where(slot_block >= 0, slot_block, block_total)]
        .set(position, mode="drop")
    )

    orders = part_orders(n_img, n_tile)
    shares = part_sizes(slots)
    groups = n_img * n_tile // 2
    row_of = (owner_slot // slots) * go_first + owner_slot % slots
    owner = owner_slot // slots
    within = owner_slot % slots
    relative = {"img": (owner // n_tile) ^ at_img, "tile": (owner % n_tile) ^ at_tile}
    for begin, share, places in streams:
        rank = jnp.zeros((block_total,), jnp.int32)
        for k, (axis, bit) in enumerate(places):
            rank = rank + (((relative[axis] >> bit) & 1) << k)
        inside = (within >= begin) & (within < begin + share)
        row_of = jnp.where(
            inside, begin * n_img * n_tile + rank * share + within - begin, row_of
        )
    kind = jnp.zeros((block_total,), jnp.int32)
    place = jnp.zeros((block_total,), jnp.int32)
    start = 0
    for i, (order, share) in enumerate(zip(orders, shares)):
        rank = jnp.zeros((block_total,), jnp.int32)
        for axis, bit in order:
            rank = rank * 2 + ((relative[axis] >> bit) & 1)
        inside = (within >= start) & (within < start + share)
        kind = jnp.where(inside, 2 * i + (relative["img"] & 1), kind)
        place = jnp.where(inside, rank * share + within - start, place)
        start += share
    kinds = 2 * len(orders)
    block_id = jnp.arange(block_total, dtype=jnp.int32)
    per_turn = POOL * channels // block_rows
    turn = (block_id // section_blocks) * (POOL + 1) + (block_id % section_blocks) // per_turn
    bucket = turn * kinds + kind
    buckets = section_count * (POOL + 1) * kinds
    within_turn = (block_id % section_blocks) % per_turn
    _, order_list, place_list = lax.sort((bucket, within_turn, place), num_keys=1)
    offsets = jnp.sum(
        (bucket[None, :] < jnp.arange(buckets + 1, dtype=jnp.int32)[:, None]).astype(jnp.int32), axis=1
    )

    valid_float = valid.astype(jnp.float32)
    conv_low = conv_weight.astype(jnp.bfloat16)
    lateral_w = conv_low[:in_channels]
    kernel_taps = conv_low[in_channels:].reshape(9, channels, channels)
    head_all = head_weight.astype(jnp.bfloat16)
    lateral_bias = bias_vector[:channels]
    conv_bias = bias_vector[channels : 2 * channels]
    lateral = (
        jnp.einsum("ihwc,cd->ihwd", features, lateral_w, preferred_element_type=jnp.float32)
        + lateral_bias
    ).astype(jnp.bfloat16)
    column_pad = ((0, 0), (0, 0), (1, 1), (0, 0))
    lateral_padded = jnp.pad(padded_2(lateral, (("tile", 1),), 1), column_pad)
    feature_map = (convolve(lateral_padded, kernel_taps, height, breadth) + conv_bias).astype(
        jnp.bfloat16
    )
    map_padded = padded_2(feature_map, (("tile", 1),), rim)
    padded_rows = height + 2 * rim
    lines = images * padded_rows
    map_t = map_padded.reshape(lines * breadth, channels).T
    sample_rows = roi_image * padded_rows + corner_index // breadth
    sample_cols = corner_index % breadth
    fracs_row = corner_frac[:, 0]
    fracs_col = corner_frac[:, 1]
    feats_t = pool_regions(map_t, sample_rows, sample_cols, fracs_row, fracs_col, breadth)
    if streams:
        gathered = gather_blocks(own_blocks, gathered, go_first, streams, n_img, n_tile, feats_t)
    first_pres = first_layer(row_of, gathered, feats_t, section_blocks)

    loss_part = jnp.zeros((), jnp.float32)
    head_grads = []
    section_bias_grads = []
    acts_t, grads_first, grads_second = [], [], []
    for section in range(section_count):
        second_slots = lax.slice_in_dim(
            row_of, section * section_blocks + first_blocks, (section + 1) * section_blocks
        )
        second_matrix = gathered[second_slots].reshape(hidden, hidden)
        head_low = head_all[section]
        offset = 2 * channels + section * (2 * hidden + out_width)
        first_bias = bias_vector[offset : offset + hidden]
        second_bias = bias_vector[offset + hidden : offset + 2 * hidden]
        head_bias = bias_vector[offset + 2 * hidden : offset + 2 * hidden + out_width]
        first_pre = first_pres[section] + first_bias
        first_act = jax.nn.silu(first_pre).astype(jnp.bfloat16)
        acts_t.append(first_act.T)
        second_pre = (
            jnp.dot(first_act, second_matrix, preferred_element_type=jnp.float32) + second_bias
        )
        second_act = jax.nn.silu(second_pre).astype(jnp.bfloat16)
        outputs = jnp.dot(second_act, head_low, preferred_element_type=jnp.float32) + head_bias
        logits = outputs[:, :classes]
        shifted = logits - jnp.max(logits, axis=1, keepdims=True)
        log_total = jnp.log(jnp.sum(jnp.exp(shifted), axis=1, keepdims=True))
        one_hot = (
            labels[section][:, None] == jnp.arange(classes, dtype=jnp.int32)[None, :]
        ).astype(jnp.float32)
        cross = log_total[:, 0] - jnp.sum(shifted * one_hot, axis=1)
        foreground = (labels[section] > 0).astype(jnp.float32)
        target = box_deltas[section].T * (
            jnp.array([10.0, 10.0, 5.0, 5.0], jnp.float32) * (section + 1)
        )
        differ = outputs[:, classes:] - target
        magnitude = jnp.abs(differ)
        smooth = jnp.where(magnitude < 1.0, 0.5 * differ * differ, magnitude - 0.5)
        loss_part = loss_part + jnp.sum(
            valid_float * (cross + foreground * jnp.sum(smooth, axis=1))
        )
        probs = jnp.exp(shifted - log_total)
        grad_logits = valid_float[:, None] * (probs - one_hot)
        grad_box = (valid_float * foreground)[:, None] * jnp.clip(differ, -1.0, 1.0)
        grad_out = jnp.concatenate([grad_logits, grad_box], axis=1).astype(jnp.bfloat16)
        head_grads.append(
            jnp.einsum("rk,rf->kf", second_act, grad_out, preferred_element_type=jnp.float32)
        )
        grad_head_bias = jnp.sum(grad_out.astype(jnp.float32), axis=0)
        grad_second = (
            jnp.einsum("rf,kf->rk", grad_out, head_low, preferred_element_type=jnp.float32)
            * silu_slope(second_pre)
        ).astype(jnp.bfloat16)
        grad_second_bias = jnp.sum(grad_second.astype(jnp.float32), axis=0)
        grad_first = (
            jnp.einsum("rf,kf->rk", grad_second, second_matrix, preferred_element_type=jnp.float32)
            * silu_slope(first_pre)
        ).astype(jnp.bfloat16)
        grad_first_bias = jnp.sum(grad_first.astype(jnp.float32), axis=0)
        section_bias_grads.extend([grad_first_bias, grad_second_bias, grad_head_bias])
        grads_first.append(grad_first)
        grads_second.append(grad_second)
    acts_t = jnp.stack(acts_t)
    grads_first = jnp.stack(grads_first)
    grads_second = jnp.stack(grads_second)

    sizes = []
    for share in shares:
        sizes += [(groups * share, block_rows, hidden)] * 2
    parts = weight_grads(
        order_list, place_list, offsets, feats_t, acts_t, grads_first, grads_second, sizes
    )

    found = {"map": jnp.zeros((lines * breadth, channels), jnp.float32)}

    def turns_of(start, stop):
        def work(after):
            found["map"] = map_grads(
                found["map"], (start, stop), row_of, gathered, grads_first, sample_rows,
                sample_cols, fracs_row, fracs_col, section_blocks, lines, breadth, after,
            )
            return found["map"]

        return work

    def edges(after):
        grad_padded_map = found["map"].reshape(images, padded_rows, breadth, channels)
        to_next = grad_padded_map[:, height + rim - 1 :].astype(jnp.bfloat16)
        to_last = grad_padded_map[:, : rim + 1].astype(jnp.bfloat16)
        ends = n_tile - 1
        from_last = lax.ppermute(to_next, "tile", [(i, i + 1) for i in range(ends)])
        from_next = lax.ppermute(to_last, "tile", [(i + 1, i) for i in range(ends)])
        found["rows"] = edge_rows(
            found["map"], from_last, from_next, images, height, breadth, rim, after
        )
        return found["rows"]

    def rest(after):
        grad_rows = found["rows"]
        grad_map = grad_rows[:, 1 : height + 1]
        grad_conv_bias = jnp.sum(grad_map.astype(jnp.float32), axis=(0, 1, 2))
        grad_map_padded = jnp.pad(grad_rows, column_pad)
        grad_taps, grad_lateral_full = convolve_back(
            grad_map_padded, lateral_padded, grad_map, kernel_taps, height, breadth
        )
        grad_lateral = grad_lateral_full.astype(jnp.bfloat16)
        grad_lateral_w = jnp.einsum(
            "ihwc,ihwd->cd", features, grad_lateral, preferred_element_type=jnp.float32
        )
        grad_lateral_bias = jnp.sum(grad_lateral.astype(jnp.float32), axis=(0, 1, 2))
        misc = jnp.concatenate(
            [grad_lateral_bias, grad_conv_bias]
            + section_bias_grads
            + [loss_part[None], jnp.sum(valid_float)[None]]
        )
        filled = -(-misc.size // 1024) * 1024
        misc = jnp.pad(misc, (0, filled - misc.size)).reshape(-1, 128)
        heads = jnp.stack(head_grads).reshape(-1, out_width)
        found["sums"] = sum_everywhere(
            [grad_lateral_w, grad_taps], [heads], misc, after, n_img, n_tile
        )
        return found["sums"][-1]

    events, start = {}, 0
    for at, count in TURNS_AT.items():
        events[at] = turns_of(start, start + count)
        start += count
    events[EDGES_AT] = edges
    events["end"] = rest
    block_terms = sum_parts(parts[0::2], parts[1::2], orders, events)

    conv_sum = jnp.concatenate(found["sums"][:2], axis=0)
    head_sum = found["sums"][2].reshape(section_count, hidden, out_width)
    misc_sum = found["sums"][3].reshape(-1)
    biases = bias_vector.shape[0]
    bias_sum, loss_total, valid_sum = misc_sum[:biases], misc_sum[biases], misc_sum[biases + 1]
    scale = 1.0 / valid_sum
    mine = lax.dynamic_slice_in_dim(slot_block, (at_img * n_tile + at_tile) * slots, slots)
    held, old, start = mine, None, 0
    for part, share in zip(block_terms, shares):
        old = finish_blocks(
            part, start, share, block_master, block_first, block_second, held, scale[None], old
        )
        start += share
    block_new, block_first_new, block_second_new = old
    step = float(STEP)
    conv_new, conv_first_new, conv_second_new = adamw(
        conv_weight, conv_first, conv_second, conv_sum * scale, step
    )
    head_new, head_first_new, head_second_new = adamw(
        head_weight, head_first, head_second, head_sum * scale, step
    )
    bias_new, bias_first_new, bias_second_new = adamw(
        bias_vector, bias_first, bias_second, bias_sum * scale, step
    )
    loss = (loss_total * scale).reshape(1)
    return (
        loss,
        conv_new,
        conv_first_new,
        conv_second_new,
        head_new,
        head_first_new,
        head_second_new,
        bias_new,
        bias_first_new,
        bias_second_new,
        block_new,
        block_first_new,
        block_second_new,
    )


def solution(mesh):
    split = P(AXES, None, None)
    return jax.shard_map(
        on_device,
        mesh=mesh,
        in_specs=(
            P("img", "tile", None, None),
            P(), P(), P(), P(), P(), P(), P(), P(), P(),
            split, split, split,
            P(),
            P(AXES),
            P(None, None, AXES),
            P(None, None, None, AXES),
            P(None, AXES),
            P(AXES),
            P(None, None, AXES),
        ),
        out_specs=(P(),) * 10 + (split,) * 3,
        check_vma=False,
    )
```

```python
import math

import jax
import jax.numpy as jnp
from jax import lax
from jax.experimental import pallas as pl
from jax.experimental.pallas import tpu as pltpu
from jax.sharding import PartitionSpec as P

HR = 2
STEP = 5
BINS = 49
POOL = 7

BETA_ONE = 0.9
BETA_TWO = 0.999
RATE = 0.025
DECAY = 0.01
EPSILON = 1e-08

VMEM_LIMIT = 56 * 1024 * 1024
AXES = ("img", "tile")


def padded_2(cells, sides, width):
    for axis, dim in sides:
        count = lax.axis_size(axis)
        ends = count - 1
        head = lax.slice_in_dim(cells, 0, width, axis=dim)
        tail = lax.slice_in_dim(cells, cells.shape[dim] - width, cells.shape[dim], axis=dim)
        cells = jnp.concatenate(
            [
                lax.ppermute(tail, axis, [(i, (i + 1) % count) for i in range(ends)]),
                cells,
                lax.ppermute(head, axis, [((i + 1) % count, i) for i in range(ends)]),
            ],
            axis=dim,
        )
    return cells


def adamw(master, first, second, grad, step):
    first_new = BETA_ONE * first + (1.0 - BETA_ONE) * grad
    second_new = BETA_TWO * second + (1.0 - BETA_TWO) * grad * grad
    first_hat = first_new / (1.0 - BETA_ONE**step)
    second_hat = second_new / (1.0 - BETA_TWO**step)
    master_new = master - RATE * (first_hat / (jnp.sqrt(second_hat) + EPSILON) + DECAY * master)
    return (master_new, first_new, second_new)


def silu_slope(value):
    sigmoid = jax.nn.sigmoid(value)
    return sigmoid * (1.0 + value * (1.0 - sigmoid))


def convolve(padded, kernel_taps, height, breadth):
    summed = None
    for kernel_pos in range(9):
        row_shift = kernel_pos // 3
        col_shift = kernel_pos % 3
        window = padded[:, row_shift : row_shift + height, col_shift : col_shift + breadth]
        contrib = jnp.einsum(
            "ihwc,cd->ihwd", window, kernel_taps[kernel_pos], preferred_element_type=jnp.float32
        )
        summed = contrib if summed is None else summed + contrib
    return summed


def convolve_back(grad_padded, lateral_padded, grad_low, kernel_taps, height, breadth):
    grad_input = None
    tap_grads = []
    for kernel_pos in range(9):
        row_shift = kernel_pos // 3
        col_shift = kernel_pos % 3
        window = lateral_padded[:, row_shift : row_shift + height, col_shift : col_shift + breadth]
        tap_grads.append(
            jnp.einsum("ihwc,ihwd->cd", window, grad_low, preferred_element_type=jnp.float32)
        )
        source = grad_padded[
            :, 2 - row_shift : 2 - row_shift + height, 2 - col_shift : 2 - col_shift + breadth
        ]
        contrib = jnp.einsum(
            "ihwd,cd->ihwc", source, kernel_taps[kernel_pos], preferred_element_type=jnp.float32
        )
        grad_input = contrib if grad_input is None else grad_input + contrib
    return (jnp.concatenate(tap_grads, axis=0), grad_input)


def column_weights(column, frac, breadth):
    regions = column.shape[1]
    away = lax.broadcasted_iota(jnp.int32, (breadth, regions), 0) - column
    return jnp.where(away == 0, 1.0 - frac, jnp.where(away == 1, frac, 0.0))


def row_weight(row, frac, at):
    away = at - row
    return jnp.where(away == 0, 1.0 - frac, jnp.where(away == 1, frac, 0.0))


def pool_regions(map_t, rows, cols, fracs_row, fracs_col, breadth):
    section_count, bins, regions = rows.shape
    channels, cells = map_t.shape
    lines = cells // breadth
    group = POOL
    chunk = 8

    def body(map_ref, row_ref, col_ref, fr_ref, fc_ref, out_ref):
        turn = pl.program_id(1)

        def one_bin(b, carry):
            p = turn * group + b
            row = row_ref[0, pl.ds(p, 1), :]
            col = col_ref[0, pl.ds(p, 1), :]
            frow = fr_ref[0, pl.ds(p, 1), :]
            fcol = fc_ref[0, pl.ds(p, 1), :]
            across = column_weights(col, fcol, breadth)
            total = None
            for first in range(0, lines, chunk):
                weights = jnp.concatenate(
                    [
                        (across * row_weight(row, frow, line)).astype(jnp.bfloat16)
                        for line in range(first, first + chunk)
                    ],
                    axis=0,
                )
                part = jnp.dot(
                    map_ref[:, first * breadth : (first + chunk) * breadth],
                    weights,
                    preferred_element_type=jnp.float32,
                )
                total = part if total is None else total + part
            out_ref[0, b] = total.astype(jnp.bfloat16)
            return carry

        lax.fori_loop(0, group, one_bin, 0)

    samples = pl.BlockSpec((1, bins, regions), lambda u, t: (u, 0, 0))
    return pl.pallas_call(
        body,
        grid=(section_count, bins // group),
        in_specs=[pl.BlockSpec((channels, cells), lambda u, t: (0, 0))] + [samples] * 4,
        out_specs=pl.BlockSpec((1, group, channels, regions), lambda u, t: (u, t, 0, 0)),
        out_shape=jax.ShapeDtypeStruct((section_count, bins, channels, regions), jnp.bfloat16),
        compiler_params=pltpu.CompilerParams(vmem_limit_bytes=VMEM_LIMIT),
        cost_estimate=pl.CostEstimate(
            flops=2 * section_count * bins * regions * cells * channels,
            bytes_accessed=section_count * bins * regions * channels * 2,
            transcendentals=0,
        ),
        name="pool_regions",
    )(map_t, rows, cols, fracs_row, fracs_col)


def fetch_blocks(table, blocks_ref, buffer, sem, base, slot, count, block_rows):
    def one(b, carry):
        pltpu.make_async_copy(
            blocks_ref.at[table[base + b]],
            buffer.at[slot, pl.ds(pl.multiple_of(b * block_rows, block_rows), block_rows)],
            sem.at[slot],
        ).start()
        return carry

    lax.fori_loop(0, count, one, 0, unroll=8)


def first_layer(table, blocks, feats_t, section_blocks):
    section_count, bins, channels, regions = feats_t.shape
    _, block_rows, hidden = blocks.shape
    group = POOL
    turns = bins // group
    per_bin = channels // block_rows
    count = group * per_bin

    def body(table_ref, blocks_ref, x_ref, out_ref, buffer, sem):
        u, t = pl.program_id(0), pl.program_id(1)
        step = u * turns + t
        slot = lax.rem(step, 2)

        def fetch(at, into):
            base = (at // turns) * section_blocks + lax.rem(at, turns) * count
            fetch_blocks(table_ref, blocks_ref, buffer, sem, base, into, count, block_rows)

        @pl.when(step == 0)
        def _():
            fetch(step, slot)

        @pl.when(step + 1 < section_count * turns)
        def _():
            fetch(step + 1, 1 - slot)

        pltpu.make_async_copy(buffer.at[slot], buffer.at[slot], sem.at[slot]).wait()

        @pl.when(t == 0)
        def _():
            out_ref[...] = jnp.zeros_like(out_ref)

        out_ref[0] += lax.dot_general(
            x_ref[0].reshape(group * channels, regions),
            buffer[slot],
            (((0,), (0,)), ((), ())),
            preferred_element_type=jnp.float32,
        )

    return pl.pallas_call(
        body,
        grid_spec=pltpu.PrefetchScalarGridSpec(
            num_scalar_prefetch=1,
            grid=(section_count, turns),
            in_specs=[
                pl.BlockSpec(memory_space=pl.ANY),
                pl.BlockSpec((1, group, channels, regions), lambda u, t, _: (u, t, 0, 0)),
            ],
            out_specs=pl.BlockSpec((1, regions, hidden), lambda u, t, _: (u, 0, 0)),
            scratch_shapes=[
                pltpu.VMEM((2, count * block_rows, hidden), jnp.bfloat16),
                pltpu.SemaphoreType.DMA((2,)),
            ],
        ),
        out_shape=jax.ShapeDtypeStruct((section_count, regions, hidden), jnp.float32),
        compiler_params=pltpu.CompilerParams(vmem_limit_bytes=VMEM_LIMIT),
        cost_estimate=pl.CostEstimate(
            flops=2 * section_count * bins * regions * channels * hidden,
            bytes_accessed=section_count * bins * channels * (regions + hidden) * 2,
            transcendentals=0,
        ),
        name="first_layer",
    )(table, blocks, feats_t)


def weight_grads(order, place, offsets, feats_t, acts_t, grads_first, grads_second, sizes):
    section_count, bins, channels, regions = feats_t.shape
    hidden = grads_first.shape[2]
    block_rows = sizes[0][1]
    group = POOL
    turns = bins // group + 1
    rows = group * channels
    wide = acts_t.shape[1]
    steps = section_count * turns
    kinds = len(sizes)

    def body(order_ref, place_ref, offset_ref, x_ref, a_ref, gf_ref, gs_ref, *rest):
        outs, (buffer, sem) = rest[:kinds], rest[kinds:]
        u, t = pl.program_id(0), pl.program_id(1)
        step = u * turns + t
        slot = lax.rem(step, 2)

        def drain(at, into):
            last = lax.rem(at, turns) == turns - 1

            @pl.when(last)
            def _():
                half = buffer.at[into, pl.ds(0, wide)]
                pltpu.make_async_copy(half, half, sem.at[into]).wait()

            @pl.when(jnp.logical_not(last))
            def _():
                pltpu.make_async_copy(buffer.at[into], buffer.at[into], sem.at[into]).wait()

        @pl.when(step >= 2)
        def _():
            drain(step - 2, slot)

        @pl.when(t < turns - 1)
        def _():
            buffer[slot] = jnp.dot(
                x_ref[0].reshape(rows, regions), gf_ref[0], preferred_element_type=jnp.float32
            ).astype(jnp.bfloat16)

        @pl.when(t == turns - 1)
        def _():
            buffer[slot, 0:wide] = jnp.dot(
                a_ref[0], gs_ref[0], preferred_element_type=jnp.float32
            ).astype(jnp.bfloat16)

        for kind in range(kinds):

            def one(i, carry, kind=kind):
                at = pl.ds(pl.multiple_of(order_ref[i] * block_rows, block_rows), block_rows)
                pltpu.make_async_copy(
                    buffer.at[slot, at], outs[kind].at[place_ref[i]], sem.at[slot]
                ).start()
                return carry

            lax.fori_loop(
                offset_ref[step * kinds + kind], offset_ref[step * kinds + kind + 1], one, 0
            )

        @pl.when(step == steps - 1)
        def _():
            drain(step - 1, 1 - slot)
            drain(step, slot)

    return pl.pallas_call(
        body,
        grid_spec=pltpu.PrefetchScalarGridSpec(
            num_scalar_prefetch=3,
            grid=(section_count, turns),
            in_specs=[
                pl.BlockSpec(
                    (1, group, channels, regions),
                    lambda u, t, *_: (u, jnp.minimum(t, turns - 2), 0, 0),
                ),
                pl.BlockSpec((1, wide, regions), lambda u, t, *_: (u, 0, 0)),
                pl.BlockSpec((1, regions, hidden), lambda u, t, *_: (u, 0, 0)),
                pl.BlockSpec((1, regions, hidden), lambda u, t, *_: (u, 0, 0)),
            ],
            out_specs=[pl.BlockSpec(memory_space=pl.ANY)] * kinds,
            scratch_shapes=[
                pltpu.VMEM((2, rows, hidden), jnp.bfloat16),
                pltpu.SemaphoreType.DMA((2,)),
            ],
        ),
        out_shape=[jax.ShapeDtypeStruct(size, jnp.bfloat16) for size in sizes],
        compiler_params=pltpu.CompilerParams(vmem_limit_bytes=VMEM_LIMIT),
        cost_estimate=pl.CostEstimate(
            flops=2 * section_count * regions * (bins * channels + wide) * hidden,
            bytes_accessed=section_count * (bins * channels + wide) * (regions + hidden) * 2,
            transcendentals=0,
        ),
        name="weight_grads",
    )(order, place, offsets, feats_t, acts_t, grads_first, grads_second)


def map_grads(before, span, table, blocks, grads_first, rows, cols, fracs_row, fracs_col, section_blocks, lines, breadth, after):
    section_count, bins, regions = rows.shape
    _, block_rows, hidden = blocks.shape
    cells, channels = before.shape
    group = POOL
    chunk = 8
    turns = bins // group
    count = group * channels // block_rows
    start, stop = span

    def body(table_ref, blocks_ref, g_ref, row_ref, col_ref, fr_ref, fc_ref, old_ref, after_ref, out_ref, buffer, sem, pooled, across, down, weights_a, weights_b):
        del after_ref
        step = start + pl.program_id(0)
        slot = lax.rem(step, 2)
        t = lax.rem(step, turns)

        def fetch(at, into):
            base = (at // turns) * section_blocks + lax.rem(at, turns) * count
            fetch_blocks(table_ref, blocks_ref, buffer, sem, base, into, count, block_rows)

        @pl.when(step == start)
        def _():
            fetch(step, slot)
            out_ref[...] = old_ref[...]

        @pl.when(step + 1 < stop)
        def _():
            fetch(step + 1, 1 - slot)

        pltpu.make_async_copy(buffer.at[slot], buffer.at[slot], sem.at[slot]).wait()

        grads = lax.dot_general(
            g_ref[0], buffer[slot], (((1,), (1,)), ((), ())), preferred_element_type=jnp.float32
        )
        for b in range(group):
            pooled[b * regions : (b + 1) * regions] = grads[
                :, b * channels : (b + 1) * channels
            ].astype(jnp.bfloat16)

        def one_bin(b, carry):
            p = t * group + b
            here = pl.ds(pl.multiple_of(b * regions, regions), regions)
            across[:, here] = column_weights(
                col_ref[0, pl.ds(p, 1), :], fc_ref[0, pl.ds(p, 1), :], breadth
            ).astype(jnp.bfloat16)
            row = row_ref[0, pl.ds(p, 1), :]
            frow = fr_ref[0, pl.ds(p, 1), :]
            at_line = lax.broadcasted_iota(jnp.int32, (lines, regions), 0)
            down[:, here] = row_weight(row, frow, at_line)
            return carry

        lax.fori_loop(0, group, one_bin, 0)

        def build(first, into):
            for i in range(chunk):
                into[i * breadth : (i + 1) * breadth] = across[...] * down[
                    first + i : first + i + 1, :
                ].astype(jnp.bfloat16)

        stores = (weights_a, weights_b)
        build(0, stores[0])
        for turn in range(lines // chunk):
            if turn + 1 < lines // chunk:
                build((turn + 1) * chunk, stores[(turn + 1) % 2])
            at = slice(turn * chunk * breadth, (turn + 1) * chunk * breadth)
            out_ref[at] += jnp.dot(
                stores[turn % 2][...], pooled[...], preferred_element_type=jnp.float32
            )

    samples = pl.BlockSpec((1, bins, regions), lambda i, _: ((start + i) // turns, 0, 0))
    whole = pl.BlockSpec((cells, channels), lambda i, _: (0, 0))
    return pl.pallas_call(
        body,
        grid_spec=pltpu.PrefetchScalarGridSpec(
            num_scalar_prefetch=1,
            grid=(stop - start,),
            in_specs=[
                pl.BlockSpec(memory_space=pl.ANY),
                pl.BlockSpec((1, regions, hidden), lambda i, _: ((start + i) // turns, 0, 0)),
            ]
            + [samples] * 4
            + [whole, pl.BlockSpec(memory_space=pl.ANY)],
            out_specs=whole,
            scratch_shapes=[
                pltpu.VMEM((2, count * block_rows, hidden), jnp.bfloat16),
                pltpu.SemaphoreType.DMA((2,)),
                pltpu.VMEM((group * regions, channels), jnp.bfloat16),
                pltpu.VMEM((breadth, group * regions), jnp.bfloat16),
                pltpu.VMEM((lines, group * regions), jnp.float32),
                pltpu.VMEM((chunk * breadth, group * regions), jnp.bfloat16),
                pltpu.VMEM((chunk * breadth, group * regions), jnp.bfloat16),
            ],
        ),
        out_shape=jax.ShapeDtypeStruct((cells, channels), jnp.float32),
        compiler_params=pltpu.CompilerParams(vmem_limit_bytes=VMEM_LIMIT),
        cost_estimate=pl.CostEstimate(
            flops=2 * (stop - start) * group * regions * channels * (hidden + cells),
            bytes_accessed=(stop - start) * count * block_rows * hidden * 2,
            transcendentals=0,
        ),
        name="map_grads",
    )(table, blocks, grads_first, rows, cols, fracs_row, fracs_col, before, after)


def sum_blocks(terms, half, after):
    _, block_rows, hidden = terms[0].shape
    batch = max(b for b in range(1, 17) if half % b == 0)
    count = len(terms)

    def body(*refs):
        total = None
        for ref in refs[:count]:
            value = ref[...].astype(jnp.float32)
            total = value if total is None else total + value
        refs[-1][...] = total.astype(jnp.bfloat16)

    return pl.pallas_call(
        body,
        grid=(half // batch,),
        in_specs=[
            pl.BlockSpec((batch, block_rows, hidden), lambda i: (i + half // batch, 0, 0))
        ] * count
        + [pl.BlockSpec(memory_space=pl.ANY)],
        out_specs=pl.BlockSpec((batch, block_rows, hidden), lambda i: (i, 0, 0)),
        out_shape=jax.ShapeDtypeStruct((half, block_rows, hidden), jnp.bfloat16),
        compiler_params=pltpu.CompilerParams(vmem_limit_bytes=VMEM_LIMIT),
        cost_estimate=pl.CostEstimate(
            flops=half * block_rows * hidden * count,
            bytes_accessed=half * block_rows * hidden * 2 * (count + 1),
            transcendentals=0,
        ),
        name="sum_blocks",
    )(*terms, after)


def bits_of(count):
    return list(range(count.bit_length() - 1))


PARTS = ((6, "zwyx"), (6, "yxzw"), (10, "xzyw"), (12, "yxzw"), (6, "zwxy"))
TURNS_AT = {0: 5, 5: 7, 7: 3, 8: 6}
EDGES_AT = 12


def part_orders(n_img, n_tile):
    bits = {
        "x": [("tile", b) for b in bits_of(n_tile)[:1]],
        "y": [("img", b) for b in bits_of(n_img)[1:]],
        "z": [("tile", b) for b in bits_of(n_tile)[1:2]],
        "w": [("tile", b) for b in bits_of(n_tile)[2:]],
    }
    return [[place for letter in order for place in bits[letter]] for _, order in PARTS]


def part_sizes(slots):
    total = sum(share for share, _ in PARTS)
    ends, done = [0], 0
    for share, _ in PARTS:
        done += share
        ends.append((done * slots + total // 2) // total)
    return [b - a for a, b in zip(ends, ends[1:])]


def swap(values, axis, bit):
    count = lax.axis_size(axis)
    return lax.ppermute(values, axis, [(i, i ^ (1 << bit)) for i in range(count)])


GATHER_FIRST = 12
STREAMS = ((11, "wzyx"), (10, "wzxy"), (7, "xywz"))


def gather_plan(slots, n_img, n_tile):
    if n_img * n_tile > 64:
        return slots, []
    first = GATHER_FIRST * slots // 40
    bits = {
        "x": [("tile", b) for b in bits_of(n_tile)[:1]],
        "y": [("img", b) for b in bits_of(n_img)[1:]],
        "z": [("tile", b) for b in bits_of(n_tile)[1:2]],
        "w": [("tile", b) for b in bits_of(n_tile)[2:]],
    }
    total = sum(share for share, _ in STREAMS)
    streams, done, start = [], 0, first
    for share, order in STREAMS:
        done += share
        end = first + ((slots - first) * done + total // 2) // total
        places = [place for letter in order for place in bits[letter]] + [("img", 0)]
        if end > start:
            streams.append((start, end - start, places))
        start = end
    return first, streams


def gather_blocks(own, gathered, first, streams, n_img, n_tile, after):
    slots, block_rows, hidden = own.shape
    devices = n_img * n_tile
    stages = len(streams[0][2])
    pieces = devices - 1

    def body(own_ref, part_ref, after_ref, out_ref, held, send, recv, local, taken, given):
        del after_ref
        place = {"img": lax.axis_index("img"), "tile": lax.axis_index("tile")}

        def partner(axis, step):
            here = place[axis]
            there = dict(place)
            there[axis] = here + step - 2 * step * ((here // step) % 2)
            return (there["img"], there["tile"])

        barrier = pltpu.get_barrier_semaphore()
        for axis, bit in streams[0][2]:
            pl.semaphore_signal(
                barrier,
                inc=1,
                device_id=partner(axis, 1 << bit),
                device_id_type=pl.DeviceIdType.MESH,
            )
        pl.semaphore_wait(barrier, stages)
        copies = {}

        def send_piece(s, k, p):
            start, share, places = streams[s]
            base = start * devices
            source = (
                own_ref.at[pl.ds(start, share)]
                if p == 0
                else out_ref.at[pl.ds(base + p * share, share)]
            )
            q = (1 << k) + p
            axis, bit = places[k]
            copy = pltpu.make_async_remote_copy(
                src_ref=source,
                dst_ref=out_ref.at[pl.ds(base + q * share, share)],
                send_sem=send.at[s, q - 1],
                recv_sem=recv.at[s, q - 1],
                device_id=partner(axis, 1 << bit),
                device_id_type=pl.DeviceIdType.MESH,
            )
            copy.start()
            copies[s, q] = copy

        for k in range(stages):
            for s in range(len(streams)):
                send_piece(s, k, 0)
        moves = []
        for s, (start, share, _) in enumerate(streams):
            moves.append(
                pltpu.make_async_copy(
                    own_ref.at[pl.ds(start, share)],
                    out_ref.at[pl.ds(start * devices, share)],
                    local.at[s],
                )
            )
        for move in moves:
            move.start()

        def chunk(ref, c):
            return ref.at[pl.ds(c * devices, devices)]

        depth = held.shape[0]
        take = [
            pltpu.make_async_copy(chunk(part_ref, c), held.at[c % depth], taken.at[c % depth])
            for c in range(first)
        ]
        give = [
            pltpu.make_async_copy(held.at[c % depth], chunk(out_ref, c), given.at[c % depth])
            for c in range(first)
        ]
        for c in range(min(depth, first)):
            take[c].start()
        for c in range(first):
            take[c].wait()
            give[c].start()
            if c >= 2 and c - 2 + depth < first:
                give[c - 2].wait()
                take[c - 2 + depth].start()
        for c in range(first):
            if c + depth >= first:
                give[c].wait()

        for q in range(1, devices):
            for s in range(len(streams)):
                copies[s, q].wait_recv()
                for k in range(q.bit_length(), stages):
                    send_piece(s, k, q)
        for q in range(1, devices):
            for s in range(len(streams)):
                copies[s, q].wait_send()
        for move in moves:
            move.wait()

    anywhere = pl.BlockSpec(memory_space=pl.ANY)
    return pl.pallas_call(
        body,
        in_specs=[anywhere] * 3,
        out_specs=anywhere,
        out_shape=jax.ShapeDtypeStruct((slots * devices, block_rows, hidden), jnp.bfloat16),
        scratch_shapes=[
            pltpu.VMEM((4, devices, block_rows, hidden), jnp.bfloat16),
            pltpu.SemaphoreType.DMA((len(streams), pieces)),
            pltpu.SemaphoreType.DMA((len(streams), pieces)),
            pltpu.SemaphoreType.DMA((len(streams),)),
            pltpu.SemaphoreType.DMA((4,)),
            pltpu.SemaphoreType.DMA((4,)),
        ],
        compiler_params=pltpu.CompilerParams(
            collective_id=1, has_side_effects=True, vmem_limit_bytes=VMEM_LIMIT
        ),
        name="gather_blocks",
    )(own, gathered, after)


def sum_parts(kept, sent, orders, events):
    terms = [[k, swap(s, "img", 0)] for k, s in zip(kept, sent)]
    sums = [(stage, i) for stage in range(len(orders[0])) for i in range(len(orders))]
    last = kept[0]
    for at, (stage, i) in enumerate(sums):
        if at in events:
            last = events[at](last)
        half = terms[i][-1].shape[0] // 2
        last = sum_blocks(terms[i], half, last)
        terms[i].append(swap(last, *orders[i][stage]))
    events["end"](last)
    return terms


def sum_everywhere(wide, narrow, exact, after, n_img, n_tile):
    x = [("tile", 1)]
    y = [("img", 1 << b) for b in bits_of(n_img)[1:]]
    z = [("tile", 1 << b) for b in bits_of(n_tile)[1:]]
    pair = [("img", 1)]
    orders = [pair + x + y + z, pair + y + z + x, pair + z + x + y]
    stages = len(orders[0])
    lanes = 128
    placed, rows = [], 0
    for i, array in enumerate(wide):
        for half in range(2):
            placed.append((i, half, rows, array.shape[0], lanes))
            rows += array.shape[0]
    for i, array in enumerate(narrow):
        placed.append((len(wide) + i, 0, rows, array.shape[0], array.shape[1]))
        rows += array.shape[0]
    unit = 16 * n_img * n_tile
    units = -(-rows // unit)
    streams, first = [], 0
    for i, order in enumerate(orders):
        size = (units + len(orders) - 1 - i) // len(orders) * unit
        if size:
            streams.append((order, first, size, True))
            first += size
    filled = first
    count = exact.shape[0]
    small = -(-count // (8 * n_img * n_tile)) * 8 * n_img * n_tile
    streams.append((orders[0], 0, small, False))
    operands = list(wide) + list(narrow) + [exact]
    number = len(operands)

    def body(*refs):
        inputs = refs[:number]
        (out_low, out_exact, total, going, landing, total_exact, landing_exact) = refs[
            number + 1 : number + 8
        ]
        send, recv, send_back, recv_back = refs[number + 8 :]
        place = {"img": lax.axis_index("img"), "tile": lax.axis_index("tile")}

        def partner(axis, step):
            here = place[axis]
            bit = (here // step) % 2
            there = dict(place)
            there[axis] = here + step - 2 * step * bit
            return bit, (there["img"], there["tile"])

        barrier = pltpu.get_barrier_semaphore()
        for axis, step in orders[0]:
            _, there = partner(axis, step)
            pl.semaphore_signal(
                barrier, inc=1, device_id=there, device_id_type=pl.DeviceIdType.MESH
            )
        for i, half, first, size, columns in placed:
            if columns < lanes:
                total[first : first + size] = jnp.zeros((size, lanes), jnp.float32)
            total[first : first + size, :columns] = inputs[i][
                :, half * lanes : half * lanes + columns
            ]
        if rows < filled:
            total[rows:] = jnp.zeros((filled - rows, lanes), jnp.float32)
        total_exact[...] = jnp.zeros_like(total_exact)
        total_exact[0:count] = inputs[-1][...]
        pl.semaphore_wait(barrier, stages)

        start = [first for _, first, _, _ in streams]
        copies = {}

        def rows_at(first, size):
            return pl.ds(pl.multiple_of(first, min(size, 16)), size)

        def remote(source, target, there, sent, received):
            copy = pltpu.make_async_remote_copy(
                src_ref=source,
                dst_ref=target,
                send_sem=sent,
                recv_sem=received,
                device_id=there,
                device_id_type=pl.DeviceIdType.MESH,
            )
            copy.start()
            return copy

        def send_half(s, k):
            order, first, size, low = streams[s]
            half = size >> (k + 1)
            bit, there = partner(*order[k])
            away = rows_at(start[s] + (1 - bit) * half, half)
            landed = pl.ds(first + size - 2 * half, half)
            if low:
                going[away] = total[away].astype(jnp.bfloat16)
                source, target = going.at[away], landing.at[landed]
            else:
                source, target = total_exact.at[away], landing_exact.at[landed]
            copies[s, k] = remote(source, target, there, send.at[s, k], recv.at[s, k])

        for s in range(len(streams)):
            send_half(s, 0)
        for k in range(stages):
            for s, (order, first, size, low) in enumerate(streams):
                half = size >> (k + 1)
                bit, _ = partner(*order[k])
                copies[s, k].wait()
                keep = rows_at(start[s] + bit * half, half)
                landed = pl.ds(first + size - 2 * half, half)
                if low:
                    value = total[keep] + landing[landed].astype(jnp.float32)
                    if k == stages - 1:
                        out_low[keep] = value.astype(jnp.bfloat16)
                    else:
                        total[keep] = value
                else:
                    target = out_exact if k == stages - 1 else total_exact
                    target[keep] = total_exact[keep] + landing_exact[landed]
                start[s] = start[s] + bit * half
                if k + 1 < stages:
                    send_half(s, k + 1)

        def send_back_half(s, k):
            order, _, size, low = streams[s]
            half = size >> (k + 1)
            _, there = partner(*order[k])
            at = rows_at(start[s], half)
            out = out_low if low else out_exact
            copies[s, k] = remote(
                out.at[at], out.at[at], there, send_back.at[s, k], recv_back.at[s, k]
            )

        for s in range(len(streams)):
            send_back_half(s, stages - 1)
        for k in reversed(range(stages)):
            for s, (order, _, size, _) in enumerate(streams):
                half = size >> (k + 1)
                bit, _ = partner(*order[k])
                copies[s, k].wait()
                start[s] = start[s] - bit * half
                if k > 0:
                    send_back_half(s, k - 1)

    whole = pl.BlockSpec(memory_space=pltpu.VMEM)
    low, high = pl.pallas_call(
        body,
        in_specs=[whole] * number + [pl.BlockSpec(memory_space=pl.ANY)],
        out_specs=[whole, whole],
        out_shape=[
            jax.ShapeDtypeStruct((filled, lanes), jnp.bfloat16),
            jax.ShapeDtypeStruct((small, lanes), jnp.float32),
        ],
        scratch_shapes=[
            pltpu.VMEM((filled, lanes), jnp.float32),
            pltpu.VMEM((filled, lanes), jnp.bfloat16),
            pltpu.VMEM((filled, lanes), jnp.bfloat16),
            pltpu.VMEM((small, lanes), jnp.float32),
            pltpu.VMEM((small, lanes), jnp.float32),
        ]
        + [pltpu.SemaphoreType.DMA((len(streams), stages))] * 4,
        compiler_params=pltpu.CompilerParams(
            collective_id=0, has_side_effects=True, vmem_limit_bytes=VMEM_LIMIT
        ),
        name="sum_everywhere",
    )(*operands, after)
    results, at = [], 0
    for array in wide:
        size = array.shape[0]
        results.append(
            jnp.concatenate([low[at : at + size], low[at + size : at + 2 * size]], axis=1).astype(
                jnp.float32
            )
        )
        at += 2 * size
    for array in narrow:
        results.append(low[at : at + array.shape[0], : array.shape[1]].astype(jnp.float32))
        at += array.shape[0]
    return results + [high[:count]]


def edge_rows(grad_flat, from_last, from_next, images, height, breadth, rim, after):
    channels = grad_flat.shape[1]
    padded = height + 2 * rim
    low, high = from_last.astype(jnp.bfloat16), from_next.astype(jnp.bfloat16)

    def body(own_ref, last_ref, next_ref, after_ref, out_ref):
        del after_ref
        for i in range(images):
            for r in range(height + 2):
                line = r + rim - 1
                at = (i * padded + line) * breadth
                value = own_ref[at : at + breadth]
                if r < rim + 1:
                    value = value + last_ref[i, r].astype(jnp.float32)
                if r >= height + 1 - rim:
                    value = value + next_ref[i, r - (height + 1 - rim)].astype(jnp.float32)
                out_ref[i, r] = value.astype(jnp.bfloat16)

    whole = pl.BlockSpec(memory_space=pltpu.VMEM)
    return pl.pallas_call(
        body,
        in_specs=[whole] * 3 + [pl.BlockSpec(memory_space=pl.ANY)],
        out_specs=whole,
        out_shape=jax.ShapeDtypeStruct((images, height + 2, breadth, channels), jnp.bfloat16),
        compiler_params=pltpu.CompilerParams(vmem_limit_bytes=VMEM_LIMIT),
        name="edge_rows",
    )(grad_flat, low, high, after)


def finish_blocks(terms, start, share, masters, firsts, seconds, held, scale, old):
    slots, block_rows, hidden = masters.shape
    count = len(terms)
    batch = math.gcd(math.gcd(start, share), 2)
    correct_one = 1.0 - BETA_ONE ** float(STEP)
    correct_two = 1.0 - BETA_TWO ** float(STEP)

    def body(held_ref, scale_ref, *refs):
        total = None
        for ref in refs[:count]:
            value = ref[...].astype(jnp.float32)
            total = value if total is None else total + value
        w_ref, m_ref, v_ref = refs[count : count + 3]
        outs = refs[-3:]
        place = start + pl.program_id(0) * batch
        total = total * scale_ref[0]
        grad = jnp.concatenate(
            [jnp.where(held_ref[place + i] >= 0, total[i : i + 1], 0.0) for i in range(batch)],
            axis=0,
        )
        first_new = BETA_ONE * m_ref[...] + (1.0 - BETA_ONE) * grad
        second_new = BETA_TWO * v_ref[...] + (1.0 - BETA_TWO) * grad * grad
        rooted = jnp.sqrt(second_new * (1.0 / correct_two)) + EPSILON
        outs[0][...] = w_ref[...] - RATE * (
            first_new * (1.0 / correct_one) / rooted + DECAY * w_ref[...]
        )
        outs[1][...] = first_new
        outs[2][...] = second_new

    term = pl.BlockSpec((batch, block_rows, hidden), lambda i: (i, 0, 0))
    slot = pl.BlockSpec((batch, block_rows, hidden), lambda i: (start // batch + i, 0, 0))
    smem = pl.BlockSpec(memory_space=pltpu.SMEM)
    kept = [] if old is None else list(old)
    inputs = [held, scale] + list(terms) + [masters, firsts, seconds] + kept
    return pl.pallas_call(
        body,
        grid=(share // batch,),
        in_specs=[smem, smem]
        + [term] * count
        + [slot] * 3
        + [pl.BlockSpec(memory_space=pl.ANY)] * len(kept),
        out_specs=[slot] * 3,
        out_shape=[jax.ShapeDtypeStruct(masters.shape, jnp.float32)] * 3,
        input_output_aliases={len(inputs) - 3 + j: j for j in range(len(kept))},
        compiler_params=pltpu.CompilerParams(vmem_limit_bytes=VMEM_LIMIT),
        name="finish_blocks",
    )(*inputs)


def on_device(
    features,
    conv_weight,
    conv_first,
    conv_second,
    head_weight,
    head_first,
    head_second,
    bias_vector,
    bias_first,
    bias_second,
    block_master,
    block_first,
    block_second,
    slot_block,
    roi_image,
    corner_index,
    corner_frac,
    labels,
    valid,
    box_deltas,
):
    images, height, breadth, in_channels = features.shape
    channels = conv_weight.shape[1]
    section_count, hidden, out_width = head_weight.shape
    classes = out_width - 4
    slots, block_rows, _ = block_master.shape
    all_slots = slot_block.shape[0]
    rim = HR
    first_rows = BINS * channels
    section_rows = first_rows + hidden
    section_blocks = section_rows // block_rows
    first_blocks = first_rows // block_rows
    block_total = section_count * section_blocks
    n_img, n_tile = lax.axis_size("img"), lax.axis_size("tile")
    at_img, at_tile = lax.axis_index("img"), lax.axis_index("tile")

    own_blocks = block_master.astype(jnp.bfloat16)
    go_first, streams = gather_plan(slots, n_img, n_tile)
    gathered = lax.all_gather(own_blocks[:go_first], AXES, axis=0, tiled=True)
    position = jnp.arange(all_slots, dtype=jnp.int32)
    owner_slot = (
        jnp.zeros((block_total,), jnp.int32)
        .at[jnp.where(slot_block >= 0, slot_block, block_total)]
        .set(position, mode="drop")
    )

    orders = part_orders(n_img, n_tile)
    shares = part_sizes(slots)
    groups = n_img * n_tile // 2
    row_of = (owner_slot // slots) * go_first + owner_slot % slots
    owner = owner_slot // slots
    within = owner_slot % slots
    relative = {"img": (owner // n_tile) ^ at_img, "tile": (owner % n_tile) ^ at_tile}
    for begin, share, places in streams:
        rank = jnp.zeros((block_total,), jnp.int32)
        for k, (axis, bit) in enumerate(places):
            rank = rank + (((relative[axis] >> bit) & 1) << k)
        inside = (within >= begin) & (within < begin + share)
        row_of = jnp.where(
            inside, begin * n_img * n_tile + rank * share + within - begin, row_of
        )
    kind = jnp.zeros((block_total,), jnp.int32)
    place = jnp.zeros((block_total,), jnp.int32)
    start = 0
    for i, (order, share) in enumerate(zip(orders, shares)):
        rank = jnp.zeros((block_total,), jnp.int32)
        for axis, bit in order:
            rank = rank * 2 + ((relative[axis] >> bit) & 1)
        inside = (within >= start) & (within < start + share)
        kind = jnp.where(inside, 2 * i + (relative["img"] & 1), kind)
        place = jnp.where(inside, rank * share + within - start, place)
        start += share
    kinds = 2 * len(orders)
    block_id = jnp.arange(block_total, dtype=jnp.int32)
    per_turn = POOL * channels // block_rows
    turn = (block_id // section_blocks) * (POOL + 1) + (block_id % section_blocks) // per_turn
    bucket = turn * kinds + kind
    buckets = section_count * (POOL + 1) * kinds
    within_turn = (block_id % section_blocks) % per_turn
    _, order_list, place_list = lax.sort((bucket, within_turn, place), num_keys=1)
    offsets = jnp.sum(
        (bucket[None, :] < jnp.arange(buckets + 1, dtype=jnp.int32)[:, None]).astype(jnp.int32), axis=1
    )

    valid_float = valid.astype(jnp.float32)
    conv_low = conv_weight.astype(jnp.bfloat16)
    lateral_w = conv_low[:in_channels]
    kernel_taps = conv_low[in_channels:].reshape(9, channels, channels)
    head_all = head_weight.astype(jnp.bfloat16)
    lateral_bias = bias_vector[:channels]
    conv_bias = bias_vector[channels : 2 * channels]
    lateral = (
        jnp.einsum("ihwc,cd->ihwd", features, lateral_w, preferred_element_type=jnp.float32)
        + lateral_bias
    ).astype(jnp.bfloat16)
    column_pad = ((0, 0), (0, 0), (1, 1), (0, 0))
    lateral_padded = jnp.pad(padded_2(lateral, (("tile", 1),), 1), column_pad)
    feature_map = (convolve(lateral_padded, kernel_taps, height, breadth) + conv_bias).astype(
        jnp.bfloat16
    )
    map_padded = padded_2(feature_map, (("tile", 1),), rim)
    padded_rows = height + 2 * rim
    lines = images * padded_rows
    map_t = map_padded.reshape(lines * breadth, channels).T
    sample_rows = roi_image * padded_rows + corner_index // breadth
    sample_cols = corner_index % breadth
    fracs_row = corner_frac[:, 0]
    fracs_col = corner_frac[:, 1]
    feats_t = pool_regions(map_t, sample_rows, sample_cols, fracs_row, fracs_col, breadth)
    if streams:
        gathered = gather_blocks(own_blocks, gathered, go_first, streams, n_img, n_tile, feats_t)
    first_pres = first_layer(row_of, gathered, feats_t, section_blocks)

    loss_part = jnp.zeros((), jnp.float32)
    head_grads = []
    section_bias_grads = []
    acts_t, grads_first, grads_second = [], [], []
    for section in range(section_count):
        second_slots = lax.slice_in_dim(
            row_of, section * section_blocks + first_blocks, (section + 1) * section_blocks
        )
        second_matrix = gathered[second_slots].reshape(hidden, hidden)
        head_low = head_all[section]
        offset = 2 * channels + section * (2 * hidden + out_width)
        first_bias = bias_vector[offset : offset + hidden]
        second_bias = bias_vector[offset + hidden : offset + 2 * hidden]
        head_bias = bias_vector[offset + 2 * hidden : offset + 2 * hidden + out_width]
        first_pre = first_pres[section] + first_bias
        first_act = jax.nn.silu(first_pre).astype(jnp.bfloat16)
        acts_t.append(first_act.T)
        second_pre = (
            jnp.dot(first_act, second_matrix, preferred_element_type=jnp.float32) + second_bias
        )
        second_act = jax.nn.silu(second_pre).astype(jnp.bfloat16)
        outputs = jnp.dot(second_act, head_low, preferred_element_type=jnp.float32) + head_bias
        logits = outputs[:, :classes]
        shifted = logits - jnp.max(logits, axis=1, keepdims=True)
        log_total = jnp.log(jnp.sum(jnp.exp(shifted), axis=1, keepdims=True))
        one_hot = (
            labels[section][:, None] == jnp.arange(classes, dtype=jnp.int32)[None, :]
        ).astype(jnp.float32)
        cross = log_total[:, 0] - jnp.sum(shifted * one_hot, axis=1)
        foreground = (labels[section] > 0).astype(jnp.float32)
        target = box_deltas[section].T * (
            jnp.array([10.0, 10.0, 5.0, 5.0], jnp.float32) * (section + 1)
        )
        differ = outputs[:, classes:] - target
        magnitude = jnp.abs(differ)
        smooth = jnp.where(magnitude < 1.0, 0.5 * differ * differ, magnitude - 0.5)
        loss_part = loss_part + jnp.sum(
            valid_float * (cross + foreground * jnp.sum(smooth, axis=1))
        )
        probs = jnp.exp(shifted - log_total)
        grad_logits = valid_float[:, None] * (probs - one_hot)
        grad_box = (valid_float * foreground)[:, None] * jnp.clip(differ, -1.0, 1.0)
        grad_out = jnp.concatenate([grad_logits, grad_box], axis=1).astype(jnp.bfloat16)
        head_grads.append(
            jnp.einsum("rk,rf->kf", second_act, grad_out, preferred_element_type=jnp.float32)
        )
        grad_head_bias = jnp.sum(grad_out.astype(jnp.float32), axis=0)
        grad_second = (
            jnp.einsum("rf,kf->rk", grad_out, head_low, preferred_element_type=jnp.float32)
            * silu_slope(second_pre)
        ).astype(jnp.bfloat16)
        grad_second_bias = jnp.sum(grad_second.astype(jnp.float32), axis=0)
        grad_first = (
            jnp.einsum("rf,kf->rk", grad_second, second_matrix, preferred_element_type=jnp.float32)
            * silu_slope(first_pre)
        ).astype(jnp.bfloat16)
        grad_first_bias = jnp.sum(grad_first.astype(jnp.float32), axis=0)
        section_bias_grads.extend([grad_first_bias, grad_second_bias, grad_head_bias])
        grads_first.append(grad_first)
        grads_second.append(grad_second)
    acts_t = jnp.stack(acts_t)
    grads_first = jnp.stack(grads_first)
    grads_second = jnp.stack(grads_second)

    sizes = []
    for share in shares:
        sizes += [(groups * share, block_rows, hidden)] * 2
    parts = weight_grads(
        order_list, place_list, offsets, feats_t, acts_t, grads_first, grads_second, sizes
    )

    found = {"map": jnp.zeros((lines * breadth, channels), jnp.float32)}

    def turns_of(start, stop):
        def work(after):
            found["map"] = map_grads(
                found["map"], (start, stop), row_of, gathered, grads_first, sample_rows,
                sample_cols, fracs_row, fracs_col, section_blocks, lines, breadth, after,
            )
            return found["map"]

        return work

    def edges(after):
        grad_padded_map = found["map"].reshape(images, padded_rows, breadth, channels)
        to_next = grad_padded_map[:, height + rim - 1 :].astype(jnp.bfloat16)
        to_last = grad_padded_map[:, : rim + 1].astype(jnp.bfloat16)
        ends = n_tile - 1
        from_last = lax.ppermute(to_next, "tile", [(i, i + 1) for i in range(ends)])
        from_next = lax.ppermute(to_last, "tile", [(i + 1, i) for i in range(ends)])
        found["rows"] = edge_rows(
            found["map"], from_last, from_next, images, height, breadth, rim, after
        )
        return found["rows"]

    def rest(after):
        grad_rows = found["rows"]
        grad_map = grad_rows[:, 1 : height + 1]
        grad_conv_bias = jnp.sum(grad_map.astype(jnp.float32), axis=(0, 1, 2))
        grad_map_padded = jnp.pad(grad_rows, column_pad)
        grad_taps, grad_lateral_full = convolve_back(
            grad_map_padded, lateral_padded, grad_map, kernel_taps, height, breadth
        )
        grad_lateral = grad_lateral_full.astype(jnp.bfloat16)
        grad_lateral_w = jnp.einsum(
            "ihwc,ihwd->cd", features, grad_lateral, preferred_element_type=jnp.float32
        )
        grad_lateral_bias = jnp.sum(grad_lateral.astype(jnp.float32), axis=(0, 1, 2))
        misc = jnp.concatenate(
            [grad_lateral_bias, grad_conv_bias]
            + section_bias_grads
            + [loss_part[None], jnp.sum(valid_float)[None]]
        )
        filled = -(-misc.size // 1024) * 1024
        misc = jnp.pad(misc, (0, filled - misc.size)).reshape(-1, 128)
        heads = jnp.stack(head_grads).reshape(-1, out_width)
        found["sums"] = sum_everywhere(
            [grad_lateral_w, grad_taps], [heads], misc, after, n_img, n_tile
        )
        return found["sums"][-1]

    events, start = {}, 0
    for at, count in TURNS_AT.items():
        events[at] = turns_of(start, start + count)
        start += count
    events[EDGES_AT] = edges
    events["end"] = rest
    block_terms = sum_parts(parts[0::2], parts[1::2], orders, events)

    conv_sum = jnp.concatenate(found["sums"][:2], axis=0)
    head_sum = found["sums"][2].reshape(section_count, hidden, out_width)
    misc_sum = found["sums"][3].reshape(-1)
    biases = bias_vector.shape[0]
    bias_sum, loss_total, valid_sum = misc_sum[:biases], misc_sum[biases], misc_sum[biases + 1]
    scale = 1.0 / valid_sum
    mine = lax.dynamic_slice_in_dim(slot_block, (at_img * n_tile + at_tile) * slots, slots)
    held, old, start = mine, None, 0
    for part, share in zip(block_terms, shares):
        old = finish_blocks(
            part, start, share, block_master, block_first, block_second, held, scale[None], old
        )
        start += share
    block_new, block_first_new, block_second_new = old
    step = float(STEP)
    conv_new, conv_first_new, conv_second_new = adamw(
        conv_weight, conv_first, conv_second, conv_sum * scale, step
    )
    head_new, head_first_new, head_second_new = adamw(
        head_weight, head_first, head_second, head_sum * scale, step
    )
    bias_new, bias_first_new, bias_second_new = adamw(
        bias_vector, bias_first, bias_second, bias_sum * scale, step
    )
    loss = (loss_total * scale).reshape(1)
    return (
        loss,
        conv_new,
        conv_first_new,
        conv_second_new,
        head_new,
        head_first_new,
        head_second_new,
        bias_new,
        bias_first_new,
        bias_second_new,
        block_new,
        block_first_new,
        block_second_new,
    )


def solution(mesh):
    split = P(AXES, None, None)
    return jax.shard_map(
        on_device,
        mesh=mesh,
        in_specs=(
            P("img", "tile", None, None),
            P(), P(), P(), P(), P(), P(), P(), P(), P(),
            split, split, split,
            P(),
            P(AXES),
            P(None, None, AXES),
            P(None, None, None, AXES),
            P(None, AXES),
            P(AXES),
            P(None, None, AXES),
        ),
        out_specs=(P(),) * 10 + (split,) * 3,
        check_vma=False,
    )
```
